256 devices in a mesh: ctx: 8 (over y, core), req: 8 (over z), mp: 4 (over x).
Axes of the slice: x: 4, y: 4, z: 8, core: 2. Of those that a mesh axis runs over, the one named last changes fastest.
Arguments:
- token_ids: int32 [64, 16], replicated, may hold values from 0 to 25599
- embed_table: bfloat16 [25600, 7168], P('mp', ('ctx', 'req')), may hold values from -0.29882812 to 0.29882812
- queries: bfloat16 [64, 16, 3584], P(('ctx', 'req'), None, 'mp'), may hold values from -80 to 80
- draft_kv: bfloat16 [2, 64, 16, 3584], P(None, ('ctx', 'req'), None, 'mp'), may hold values from -4 to 4
- prefix_kv: bfloat16 [2, 16384, 3584], P(None, 'ctx', 'mp'), may hold values from -4 to 4
- suffix_kv: bfloat16 [2, 64, 512, 3584], P(None, ('ctx', 'req'), None, 'mp'), may hold values from -4 to 4
- suffix_len: int32 [64], P(('ctx', 'req')), may hold values from 1 to 512, as said below
- slopes: float32 [32], P('mp'), may hold values from 3.0517578e-06 to 0.08
- out_weight: bfloat16 [3584, 7168], P('mp', ('ctx', 'req')), may hold values from -0.09375 to 0.09375
- ln_gain: float32 [7168], P('mp'), may hold values from 0.5 to 1.5
- up_weight: bfloat16 [7168, 14336], P('mp', ('ctx', 'req')), may hold values from -0.0625 to 0.0625
- down_weight: bfloat16 [14336, 7168], P(('ctx', 'req'), 'mp'), may hold values from -0.046875 to 0.046875
Outputs:
- residual: float32 [64, 16, 7168], P(('ctx', 'req'), None, 'mp')
- layer_out: float32 [64, 16, 7168], P(('ctx', 'req'), None, 'mp')
The draws below stay inside these ranges and needn't reach their ends.
Inputs may be any that keep to these rules, and one draw needn't show every extreme that they name: `suffix_len`: in every draw some request has exactly 512 filled slots.
All inputs are finite; a program needn't handle non-finite values.
Results may differ from the reference program's by a relative error of at most 0.015.
Values may be sent and summed in bfloat16 or wider, within the bound.
No kernel may reach another device: no remote copies, remote signals or barrier semaphores. Data moves between devices by JAX's collectives and lax.ppermute only.
A program may use at most 128 MiB of HBM per device.

```python
import math
import jax
import jax.numpy as jnp
import numpy as np
from jax import lax

D = 7168
HEADS = 32
HD = 112
FF = 14336
VOCAB = 25600
DRAFT = 16
SUFFIX = 512
PREFIX = 16384
REQUESTS = 64
ROWS = 1024


def prefix_table(key):
    table = jnp.clip(jax.random.normal(jax.random.fold_in(key, 11), (2, PREFIX, HEADS * HD), jnp.float32), -4.0, 4.0)
    return table.astype(jnp.bfloat16)


def draw_prefix_kv(key, part):
    return prefix_table(key)


def draw_queries(key, part):
    values = jnp.clip(jax.random.normal(jax.random.fold_in(key, 23), (REQUESTS, DRAFT, HEADS * HD), jnp.float32), -4.0, 4.0)
    return values.astype(jnp.bfloat16)


def draw_slopes(key, part):
    chooser = jax.random.uniform(jax.random.fold_in(key, 5), (HEADS,), jnp.float32)
    fast_share = 0.5
    fast_rate = jnp.exp(jax.random.uniform(jax.random.fold_in(key, 7), (HEADS,), jnp.float32, math.log(0.02), math.log(0.08)))
    slow_rate = jnp.exp(jax.random.uniform(jax.random.fold_in(key, 9), (HEADS,), jnp.float32, math.log(0.05 / PREFIX), math.log(1.0 / PREFIX)))
    return jnp.where(chooser < fast_share, fast_rate, slow_rate).astype(jnp.float32)


def draw_suffix_len(key, part):
    earlier = jax.random.randint(jax.random.fold_in(key, 3), (REQUESTS,), 1, SUFFIX + 1)
    further = jax.random.randint(jax.random.fold_in(key, 4), (REQUESTS,), 1, SUFFIX + 1)
    lengths = jnp.minimum(earlier, further)
    longest = jax.random.randint(jax.random.fold_in(key, 6), (), 0, REQUESTS)
    return lengths.at[longest].set(SUFFIX).astype(jnp.int32)


def with_ends(entries, stream_key, smallest, top_value):
    longest = entries.shape.index(max(entries.shape))
    spots = []
    for shift in (0, 1):
        where = [jax.random.randint(jax.random.fold_in(stream_key, axis), (), 0, length) for axis, length in enumerate(entries.shape)]
        where[longest] = (where[longest] + shift) % entries.shape[longest]
        spots.append(tuple(where))
    return entries.at[spots[0]].set(smallest).at[spots[1]].set(top_value)


def levels(own_key, extent, split, least, high):
    factor_of, own = 1.0, jax.random.fold_in(own_key, 6)
    for position, parts in split:
        heights = jnp.exp(jax.random.uniform(jax.random.fold_in(own, position), (parts,), jnp.float32, least / len(split), high / len(split)))
        factor_of = factor_of * jnp.repeat(heights, extent[position] // parts).reshape([-1 if axis == position else 1 for axis in range(len(extent))])
    return factor_of


def rank_table(count, skew):
    portions = [(1 << 20) // math.isqrt(standing ** skew) + 1 for standing in range(1, count + 1)]
    scale = 1 + sum(portions) // (1 << 30)
    return np.cumsum(np.array([max(1, weight // scale) for weight in portions]))


def ranked_ids(own_key, shape, number_of, skew):
    listing = rank_table(number_of, skew)
    lot = jax.random.randint(jax.random.fold_in(own_key, 1), shape, 0, int(listing[number_of - 1]))
    standing = jnp.searchsorted(jnp.asarray(listing, jnp.int32), lot, side="right")
    return jax.random.permutation(jax.random.fold_in(own_key, 2), number_of)[standing].astype(jnp.int32)


def bell_draw(stream_key, extent, spread, reach, pieces=(), kind=jnp.bfloat16):
    array = spread * jax.random.normal(stream_key, extent, jnp.float32)
    if pieces:
        array = array * levels(stream_key, extent, pieces, -0.22, 0.18)
    return jnp.clip(array, -reach, reach).astype(kind)


def setup_inputs(seed: int = 0) -> dict:
    arg_keys = jax.random.split(jax.random.key(seed), 13)
    token_ids = with_ends(ranked_ids(arg_keys[0], (REQUESTS, DRAFT), VOCAB, 2), jax.random.fold_in(arg_keys[0], 3), 0, VOCAB - 1).astype(jnp.int32)
    embed_table = bell_draw(arg_keys[1], (VOCAB, D), 0.05, 0.29882812, ((0, 4), (1, 64)))
    queries = draw_queries(jax.random.fold_in(arg_keys[12], 71), 0)
    draft_kv = bell_draw(arg_keys[3], (2, REQUESTS, DRAFT, HEADS * HD), 1.0, 4.0, ((1, 64), (3, 4)))
    prefix_kv = draw_prefix_kv(jax.random.fold_in(arg_keys[12], 71), 0)
    suffix_kv = bell_draw(arg_keys[5], (2, REQUESTS, SUFFIX, HEADS * HD), 1.0, 4.0, ((1, 64), (3, 4)))
    suffix_len = draw_suffix_len(jax.random.fold_in(arg_keys[12], 71), 0)
    slopes = draw_slopes(jax.random.fold_in(arg_keys[12], 71), 0)
    out_weight = bell_draw(arg_keys[8], (HEADS * HD, D), (HEADS * HD) ** -0.5, 0.09375, ((0, 4), (1, 64)))
    ln_gain = jnp.clip(1.0 + 0.1 * jax.random.normal(arg_keys[9], (D,), jnp.float32), 0.5, 1.5)
    up_weight = bell_draw(arg_keys[10], (D, FF), D ** -0.5, 0.0625, ((0, 4), (1, 64)))
    down_weight = bell_draw(arg_keys[11], (FF, D), FF ** -0.5, 0.046875, ((0, 64), (1, 4)))
    return {"token_ids": token_ids, "embed_table": embed_table, "queries": queries, "draft_kv": draft_kv, "prefix_kv": prefix_kv, "suffix_kv": suffix_kv, "suffix_len": suffix_len, "slopes": slopes, "out_weight": out_weight, "ln_gain": ln_gain, "up_weight": up_weight, "down_weight": down_weight}


def head_scores(query_heads, key_heads, query_pos, key_pos, slopes):
    content = jnp.einsum('thd,khd->htk', query_heads, key_heads) / math.sqrt(HD)
    distance = (query_pos[:, None] - key_pos[None, :]).astype(jnp.float32)
    return content - slopes[:, None, None] * distance[None, :, :]

def weighted_part(scores, row_top, value_heads):
    weights = jnp.exp(scores - row_top)
    rounded = lax.optimization_barrier(weights.astype(jnp.bfloat16)).astype(jnp.float32)
    return (lax.optimization_barrier(jnp.sum(weights, axis=2)), jnp.einsum('htk,khd->thd', rounded, value_heads))

def reference(token_ids, embed_table, queries, draft_kv, prefix_kv, suffix_kv, suffix_len, slopes, out_weight, ln_gain, up_weight, down_weight):
    embedded = jnp.take(embed_table, token_ids, axis=0)
    prompt_keys = prefix_kv[0].astype(jnp.float32).reshape(PREFIX, HEADS, HD)
    prompt_values = prefix_kv[1].astype(jnp.float32).reshape(PREFIX, HEADS, HD)
    prompt_index = jnp.arange(PREFIX, dtype=jnp.int32)
    draft_index = jnp.arange(DRAFT, dtype=jnp.int32)
    slot_index = jnp.arange(SUFFIX, dtype=jnp.int32)

    def one_request(inputs):
        query_rows, draft_pair, suffix_pair, length = inputs
        query_heads = query_rows.astype(jnp.float32).reshape(DRAFT, HEADS, HD)
        query_pos = PREFIX + length + draft_index
        prompt_scores = head_scores(query_heads, prompt_keys, query_pos, prompt_index, slopes)
        suffix_keys = suffix_pair[0].astype(jnp.float32).reshape(SUFFIX, HEADS, HD)
        suffix_values = suffix_pair[1].astype(jnp.float32).reshape(SUFFIX, HEADS, HD)
        suffix_scores = head_scores(query_heads, suffix_keys, query_pos, PREFIX + slot_index, slopes)
        suffix_scores = jnp.where((slot_index < length)[None, None, :], suffix_scores, -jnp.inf)
        draft_keys = draft_pair[0].astype(jnp.float32).reshape(DRAFT, HEADS, HD)
        draft_values = draft_pair[1].astype(jnp.float32).reshape(DRAFT, HEADS, HD)
        draft_scores = head_scores(query_heads, draft_keys, query_pos, PREFIX + length + draft_index, slopes)
        draft_scores = jnp.where((draft_index[None, :] <= draft_index[:, None])[None], draft_scores, -jnp.inf)
        row_top = jnp.maximum(jnp.maximum(lax.optimization_barrier(jnp.max(prompt_scores, axis=2)), lax.optimization_barrier(jnp.max(suffix_scores, axis=2))), lax.optimization_barrier(jnp.max(draft_scores, axis=2)))[:, :, None]
        prompt_total, prompt_sum = weighted_part(prompt_scores, row_top, prompt_values)
        suffix_total, suffix_sum = weighted_part(suffix_scores, row_top, suffix_values)
        draft_total, draft_sum = weighted_part(draft_scores, row_top, draft_values)
        totals = (prompt_total + suffix_total + draft_total).T
        attended = (prompt_sum + suffix_sum + draft_sum) / totals[:, :, None]
        return attended.reshape(DRAFT, HEADS * HD).astype(jnp.bfloat16)
    attended = lax.map(one_request, (queries, jnp.moveaxis(draft_kv, 1, 0), jnp.moveaxis(suffix_kv, 1, 0), suffix_len))
    attended_rows = attended.reshape(ROWS, HEADS * HD)
    projected = jnp.dot(attended_rows, out_weight, preferred_element_type=jnp.float32)
    residual_wide = embedded.reshape(ROWS, D).astype(jnp.float32) + projected
    mean_value = lax.optimization_barrier(jnp.mean(residual_wide, axis=1, keepdims=True))
    mean_square = lax.optimization_barrier(jnp.mean(residual_wide * residual_wide, axis=1, keepdims=True))
    normed = ((residual_wide - mean_value) * lax.rsqrt(mean_square - mean_value * mean_value + 1e-05) * ln_gain[None, :]).astype(jnp.bfloat16)
    lifted = jnp.dot(normed, up_weight, preferred_element_type=jnp.float32)
    activated = jax.nn.gelu(lifted, approximate=False).astype(jnp.bfloat16)
    lowered = jnp.dot(activated, down_weight, preferred_element_type=jnp.float32)
    layer_out = residual_wide + lowered
    return (residual_wide.reshape(REQUESTS, DRAFT, D), layer_out.reshape(REQUESTS, DRAFT, D))
```

```python
import functools
import math

import jax
import jax.numpy as jnp
from jax import lax
from jax.experimental import pallas as pl
from jax.experimental.pallas import tpu as pltpu
from jax.sharding import PartitionSpec as P

LANES = 128
F32 = jnp.float32
BF16 = jnp.bfloat16


def head_lanes(head, tile, head_size):
    first = max(head * head_size - tile * LANES, 0)
    last = min((head + 1) * head_size - tile * LANES, LANES)
    return first, last


def head_tiles(head, head_size):
    return range(head * head_size // LANES, ((head + 1) * head_size - 1) // LANES + 1)


def lane_mask(shape, first, last):
    lane = lax.broadcasted_iota(jnp.int32, shape, len(shape) - 1)
    return (lane >= first) & (lane < last)


def split_three(value):
    high = value.astype(BF16).astype(F32)
    rest = value - high
    middle = rest.astype(BF16).astype(F32)
    low = rest - middle
    return high, middle, low


def prompt_kernel(
    offset_ref, slopes_ref, query_ref, prefix_ref, out_ref, kv_buf, sems, *, heads, head_size
):
    rows, width = query_ref.shape
    keys = kv_buf.shape[2]
    tiles = width // LANES
    copies = {}
    for tile in range(tiles):
        for which in range(2):
            copies[which, tile] = pltpu.make_async_copy(
                prefix_ref.at[which, :, pl.ds(tile * LANES, LANES)],
                kv_buf.at[which, tile],
                sems.at[which, tile],
            )
            copies[which, tile].start()
    scale = 1.0 / math.sqrt(head_size)
    position = (
        lax.broadcasted_iota(jnp.int32, (1, keys), 1) - offset_ref[0]
    ).astype(F32)
    arrived = set()

    def wait(which, tile):
        if (which, tile) not in arrived:
            arrived.add((which, tile))
            copies[which, tile].wait()

    parts = [jnp.zeros((rows, LANES), F32) for _ in range(tiles)]
    stats = jnp.zeros((rows, LANES), F32)
    stat_lane = lax.broadcasted_iota(jnp.int32, (rows, LANES), 1)
    for head in range(heads):
        span = head_tiles(head, head_size)
        for tile in span:
            wait(0, tile)
        query_window = jnp.concatenate(
            [
                jnp.where(
                    lane_mask((rows, LANES), *head_lanes(head, tile, head_size)),
                    query_ref[:, tile * LANES : (tile + 1) * LANES],
                    jnp.zeros((rows, LANES), BF16),
                )
                for tile in span
            ],
            axis=1,
        )
        key_window = jnp.concatenate([kv_buf[0, tile] for tile in span], axis=1)
        scores = lax.dot_general(
            query_window, key_window, (((1,), (1,)), ((), ())), preferred_element_type=F32
        )
        scores = scores * scale + slopes_ref[head] * position
        top = jnp.max(scores, axis=1, keepdims=True)
        weights = jnp.exp(scores - top)
        total = jnp.sum(weights, axis=1, keepdims=True)
        for tile in span:
            wait(1, tile)
        value_window = jnp.concatenate([kv_buf[1, tile] for tile in span], axis=1)
        sums = jnp.dot(weights.astype(BF16), value_window, preferred_element_type=F32)
        sums = sums * (1.0 / total)
        for place, tile in enumerate(span):
            parts[tile] = jnp.where(
                lane_mask((rows, LANES), *head_lanes(head, tile, head_size)),
                sums[:, place * LANES : (place + 1) * LANES],
                parts[tile],
            )
        stats = jnp.where(stat_lane % heads == head, top + jnp.log(total), stats)
    for tile in range(tiles):
        out_ref[:, tile * LANES : (tile + 1) * LANES] = parts[tile].astype(BF16)
    high, middle, low = split_three(stats)
    group = stat_lane // heads
    packed = jnp.where(
        group == 0, high, jnp.where(group == 1, middle, jnp.where(group == 2, low, 0.0))
    )
    out_ref[:, tiles * LANES :] = packed.astype(BF16)


def prompt_part(query_rows, prefix_kv, slopes, offset):
    rows, width = query_rows.shape
    heads = slopes.shape[0]
    keys = prefix_kv.shape[1]
    tiles = width // LANES
    return pl.pallas_call(
        functools.partial(prompt_kernel, heads=heads, head_size=width // heads),
        out_shape=jax.ShapeDtypeStruct((rows, width + LANES), BF16),
        in_specs=[
            pl.BlockSpec(memory_space=pltpu.SMEM),
            pl.BlockSpec(memory_space=pltpu.SMEM),
            pl.BlockSpec(memory_space=pltpu.VMEM),
            pl.BlockSpec(memory_space=pl.ANY),
        ],
        out_specs=pl.BlockSpec(memory_space=pltpu.VMEM),
        scratch_shapes=[
            pltpu.VMEM((2, tiles, keys, LANES), BF16),
            pltpu.SemaphoreType.DMA((2, tiles)),
        ],
        compiler_params=pltpu.CompilerParams(vmem_limit_bytes=40 * 1024 * 1024),
    )(offset, slopes, query_rows, prefix_kv)


def own_kernel(
    length_ref, slopes_ref, query_ref, suffix_ref, draft_ref, out_ref, stats_ref, *, heads, head_size
):
    draft, width = query_ref.shape
    slots = suffix_ref.shape[1]
    rows = heads * draft
    query = query_ref[...]
    masks = [
        lane_mask((draft, width), head * head_size, (head + 1) * head_size)
        for head in range(heads)
    ]
    spread = jnp.concatenate(
        [jnp.where(mask, query, jnp.zeros_like(query)) for mask in masks], axis=0
    )
    row = lax.broadcasted_iota(jnp.int32, (rows, 1), 0)
    slope = jnp.zeros((rows, 1), F32)
    for head in range(heads):
        slope = jnp.where(row // draft == head, slopes_ref[head], slope)
    scale = 1.0 / math.sqrt(head_size)
    length = length_ref[0]
    contract = (((1,), (1,)), ((), ()))
    slot = lax.broadcasted_iota(jnp.int32, (rows, slots), 1)
    suffix_scores = lax.dot_general(spread, suffix_ref[0], contract, preferred_element_type=F32)
    suffix_scores = suffix_scores * scale + slope * slot.astype(F32)
    suffix_scores = jnp.where(slot < length, suffix_scores, -jnp.inf)
    place = lax.broadcasted_iota(jnp.int32, (rows, draft), 1)
    draft_scores = lax.dot_general(spread, draft_ref[0], contract, preferred_element_type=F32)
    draft_scores = draft_scores * scale + slope * (place + length).astype(F32)
    token = lax.broadcasted_iota(jnp.int32, (rows, draft), 0) % draft
    draft_scores = jnp.where(place <= token, draft_scores, -jnp.inf)
    top = jnp.maximum(
        jnp.max(suffix_scores, axis=1, keepdims=True), jnp.max(draft_scores, axis=1, keepdims=True)
    )
    suffix_weights = jnp.exp(suffix_scores - top)
    draft_weights = jnp.exp(draft_scores - top)
    total = jnp.sum(suffix_weights, axis=1, keepdims=True) + jnp.sum(
        draft_weights, axis=1, keepdims=True
    )
    sums = jnp.dot(suffix_weights.astype(BF16), suffix_ref[1], preferred_element_type=F32)
    sums += jnp.dot(draft_weights.astype(BF16), draft_ref[1], preferred_element_type=F32)
    sums = sums * (1.0 / total)
    level = top + jnp.log(total)
    result = jnp.zeros((draft, width), F32)
    stats = jnp.zeros((draft, LANES), F32)
    lane = lax.broadcasted_iota(jnp.int32, (draft, LANES), 1)
    for head in range(heads):
        rows_of = slice(head * draft, (head + 1) * draft)
        result = jnp.where(masks[head], sums[rows_of], result)
        stats = jnp.where(lane == head, level[rows_of], stats)
    out_ref[...] = result
    stats_ref[...] = stats


def own_part(query_rows, suffix_kv, draft_kv, slopes, length):
    draft, width = query_rows.shape
    heads = slopes.shape[0]
    vmem = pl.BlockSpec(memory_space=pltpu.VMEM)
    smem = pl.BlockSpec(memory_space=pltpu.SMEM)
    return pl.pallas_call(
        functools.partial(own_kernel, heads=heads, head_size=width // heads),
        out_shape=(
            jax.ShapeDtypeStruct((draft, width), F32),
            jax.ShapeDtypeStruct((draft, LANES), F32),
        ),
        in_specs=[smem, smem, vmem, vmem, vmem],
        out_specs=(vmem, vmem),
        compiler_params=pltpu.CompilerParams(vmem_limit_bytes=24 * 1024 * 1024),
    )(length, slopes, query_rows, suffix_kv, draft_kv)


def merge_kernel(parts_ref, own_ref, level_ref, out_ref, *, heads, head_size):
    count, draft, _ = parts_ref.shape
    width = own_ref.shape[1]
    tiles = width // LANES
    levels = [level_ref[...]]
    for part in range(count):
        packed = parts_ref[part, :, width:].astype(F32)
        levels.append(
            packed
            + pltpu.roll(packed, LANES - heads, 1)
            + pltpu.roll(packed, LANES - 2 * heads, 1)
        )
    top = functools.reduce(jnp.maximum, levels)
    shares = [jnp.exp(level - top) for level in levels]
    total = functools.reduce(jnp.add, shares)
    shares = [share / total for share in shares]
    for tile in range(tiles):
        lanes = slice(tile * LANES, (tile + 1) * LANES)
        joined = jnp.zeros((draft, LANES), F32)
        for part, share in enumerate(shares):
            factor = jnp.zeros((draft, LANES), F32)
            for head in range(heads):
                first, last = head_lanes(head, tile, head_size)
                if first < last:
                    factor = jnp.where(
                        lane_mask((draft, LANES), first, last), share[:, head : head + 1], factor
                    )
            value = own_ref[:, lanes] if part == 0 else parts_ref[part - 1, :, lanes].astype(F32)
            joined += factor * value
        out_ref[:, lanes] = joined.astype(BF16)


def merge_parts(parts, own, level, heads):
    draft, width = own.shape
    vmem = pl.BlockSpec(memory_space=pltpu.VMEM)
    return pl.pallas_call(
        functools.partial(merge_kernel, heads=heads, head_size=width // heads),
        out_shape=jax.ShapeDtypeStruct((draft, width), BF16),
        in_specs=[vmem, vmem, vmem],
        out_specs=vmem,
    )(parts, own, level)


def residual_kernel(parts_ref, out_ref, sums_ref, *, sources):
    req, mp, pair, draft, columns = parts_ref.shape
    blocks = []
    for half in range(pair):
        for source in range(req):
            block = parts_ref[source, 0, half].astype(F32)
            for piece in range(1, mp):
                block += parts_ref[source, piece, half].astype(F32)
            blocks.append(block)
    residual = jnp.concatenate(blocks, axis=1)
    out_ref[...] = residual
    lane = lax.broadcasted_iota(jnp.int32, (draft, LANES), 1)
    first = jnp.sum(residual, axis=1, keepdims=True)
    second = jnp.sum(residual * residual, axis=1, keepdims=True)
    sums_ref[...] = jnp.where(lane == 0, first, jnp.where(lane == 1, second, 0.0))


def residual_rows(parts):
    req, mp, pair, draft, columns = parts.shape
    vmem = pl.BlockSpec(memory_space=pltpu.VMEM)
    return pl.pallas_call(
        functools.partial(residual_kernel, sources=mp),
        out_shape=(
            jax.ShapeDtypeStruct((draft, req * pair * columns), F32),
            jax.ShapeDtypeStruct((draft, LANES), F32),
        ),
        in_specs=[vmem],
        out_specs=(vmem, vmem),
    )(parts)


def norm_kernel(residual_ref, sums_ref, gain_ref, out_ref, *, model_width):
    sums = sums_ref[0]
    for part in range(1, sums_ref.shape[0]):
        sums += sums_ref[part]
    mean = sums[:, 0:1] / model_width
    mean_square = sums[:, 1:2] / model_width
    factor = lax.rsqrt(mean_square - mean * mean + 1e-05)
    out_ref[...] = ((residual_ref[...] - mean) * factor * gain_ref[...]).astype(BF16)


def norm_rows(residual, sums, gain, model_width):
    vmem = pl.BlockSpec(memory_space=pltpu.VMEM)
    return pl.pallas_call(
        functools.partial(norm_kernel, model_width=model_width),
        out_shape=jax.ShapeDtypeStruct(residual.shape, BF16),
        in_specs=[vmem, vmem, vmem],
        out_specs=vmem,
    )(residual, sums, gain[None, :])


def spread_to_all(value, axis):
    count = lax.axis_size(axis)
    return exchange(jnp.broadcast_to(value[None], (count,) + value.shape), axis)


def exchange(value, axis):
    return lax.all_to_all(value, axis, split_axis=0, concat_axis=0, tiled=True)


def per_device(
    token_ids,
    embed_table,
    queries,
    draft_kv,
    prefix_kv,
    suffix_kv,
    suffix_len,
    slopes,
    out_weight,
    ln_gain,
    up_weight,
    down_weight,
):
    heads = slopes.shape[0]
    _, draft, width = queries.shape
    prompt_local = prefix_kv.shape[1]
    ctx_count = lax.axis_size("ctx")
    req_count = lax.axis_size("req")
    mp_count = lax.axis_size("mp")
    ctx_index = lax.axis_index("ctx")
    model_index = lax.axis_index("mp")
    quarter = ln_gain.shape[0]
    rows = req_count * draft
    columns = out_weight.shape[1]
    hidden = up_weight.shape[1]

    out_all = lax.all_gather(out_weight, "ctx")
    up_all = lax.all_gather(up_weight, "ctx")
    down_all = lax.all_gather(down_weight, "ctx")

    gathered = spread_to_all(queries[0], "ctx").reshape(ctx_count * draft, width)
    own, own_level = own_part(
        queries[0], suffix_kv[:, 0], draft_kv[:, 0], slopes, suffix_len
    )
    vocab_local = embed_table.shape[0]
    shifted = token_ids.reshape(-1) - model_index * vocab_local
    one_hot = (
        shifted[:, None] == jnp.arange(vocab_local, dtype=jnp.int32)[None, :]
    ).astype(BF16)
    looked_up = jnp.dot(one_hot, embed_table, preferred_element_type=F32).astype(BF16)
    embedded = exchange(looked_up.reshape(ctx_count, rows, columns), "ctx")

    offset = (prompt_local * (ctx_count - ctx_index)).astype(jnp.int32).reshape(1)
    parts = prompt_part(gathered, prefix_kv, slopes, offset)
    parts = exchange(parts.reshape(ctx_count, draft, -1), "ctx")
    attended = merge_parts(parts, own, own_level, heads)

    attended_rows = spread_to_all(attended, "req").reshape(rows, width)
    projected = jnp.einsum(
        "mk,ckn->cmn", attended_rows, out_all, preferred_element_type=F32
    ) + embedded.astype(F32)
    pair = ctx_count // mp_count
    message = (
        projected.astype(BF16)
        .reshape(mp_count, pair, req_count, draft, columns)
        .transpose(2, 0, 1, 3, 4)
        .reshape(req_count * mp_count, pair, draft, columns)
    )
    message = exchange(message, ("req", "mp"))
    residual, sums = residual_rows(message.reshape(req_count, mp_count, pair, draft, columns))
    normed = norm_rows(residual, spread_to_all(sums, "mp"), ln_gain, quarter * mp_count)

    normed_rows = spread_to_all(normed, "req").reshape(rows, quarter)
    lifted = jnp.einsum("mk,ckn->cmn", normed_rows, up_all, preferred_element_type=F32)
    share = rows // mp_count
    lifted = exchange(
        lifted.astype(BF16)
        .reshape(ctx_count, mp_count, share, hidden)
        .transpose(1, 0, 2, 3),
        "mp",
    )
    activated = jax.nn.gelu(jnp.sum(lifted.astype(F32), axis=0), approximate=False).astype(BF16)
    activated = (
        spread_to_all(activated, "mp").transpose(1, 0, 2, 3).reshape(ctx_count, rows, hidden)
    )
    lowered = jnp.einsum("cmh,chn->mn", activated, down_all, preferred_element_type=F32)
    lowered = exchange(lowered.astype(BF16).reshape(req_count, draft, quarter), "req")
    layer_out = residual + jnp.sum(lowered.astype(F32), axis=0)
    return residual[None], layer_out[None]


def solution(mesh):
    in_specs = (
        P(),
        P("mp", ("ctx", "req")),
        P(("ctx", "req"), None, "mp"),
        P(None, ("ctx", "req"), None, "mp"),
        P(None, "ctx", "mp"),
        P(None, ("ctx", "req"), None, "mp"),
        P(("ctx", "req")),
        P("mp"),
        P("mp", ("ctx", "req")),
        P("mp"),
        P("mp", ("ctx", "req")),
        P(("ctx", "req"), "mp"),
    )
    out_specs = (P(("ctx", "req"), None, "mp"), P(("ctx", "req"), None, "mp"))
    return jax.shard_map(
        per_device, mesh=mesh, in_specs=in_specs, out_specs=out_specs, check_vma=False
    )
```

```python
import functools
import math

import jax
import jax.numpy as jnp
from jax import lax
from jax.experimental import pallas as pl
from jax.experimental.pallas import tpu as pltpu
from jax.sharding import PartitionSpec as P

LANES = 128
F32 = jnp.float32
BF16 = jnp.bfloat16
WHOLE_VMEM = 60 * 1024 * 1024


def head_lanes(head, tile, head_size):
    first = max(head * head_size - tile * LANES, 0)
    last = min((head + 1) * head_size - tile * LANES, LANES)
    return first, last


def head_tiles(head, head_size):
    return range(head * head_size // LANES, ((head + 1) * head_size - 1) // LANES + 1)


def lane_mask(shape, first, last):
    lane = lax.broadcasted_iota(jnp.int32, shape, len(shape) - 1)
    return (lane >= first) & (lane < last)


def split_three(value):
    high = value.astype(BF16).astype(F32)
    rest = value - high
    middle = rest.astype(BF16).astype(F32)
    low = rest - middle
    return high, middle, low


def prompt_kernel(
    offset_ref, slopes_ref, query_ref, prefix_ref, out_ref, kv_buf, sems, *, heads, head_size
):
    rows, width = query_ref.shape
    keys = kv_buf.shape[2]
    tiles = width // LANES
    copies = {}
    for tile in range(tiles):
        for which in range(2):
            copies[which, tile] = pltpu.make_async_copy(
                prefix_ref.at[which, :, pl.ds(tile * LANES, LANES)],
                kv_buf.at[which, tile],
                sems.at[which, tile],
            )
            copies[which, tile].start()
    scale = 1.0 / math.sqrt(head_size)
    position = (
        lax.broadcasted_iota(jnp.int32, (1, keys), 1) - offset_ref[0]
    ).astype(F32)
    arrived = set()

    def wait(which, tile):
        if (which, tile) not in arrived:
            arrived.add((which, tile))
            copies[which, tile].wait()

    parts = [jnp.zeros((rows, LANES), F32) for _ in range(tiles)]
    stats = jnp.zeros((rows, LANES), F32)
    stat_lane = lax.broadcasted_iota(jnp.int32, (rows, LANES), 1)
    for head in range(heads):
        span = head_tiles(head, head_size)
        for tile in span:
            wait(0, tile)
        query_window = jnp.concatenate(
            [
                jnp.where(
                    lane_mask((rows, LANES), *head_lanes(head, tile, head_size)),
                    query_ref[:, tile * LANES : (tile + 1) * LANES],
                    jnp.zeros((rows, LANES), BF16),
                )
                for tile in span
            ],
            axis=1,
        )
        key_window = jnp.concatenate([kv_buf[0, tile] for tile in span], axis=1)
        scores = lax.dot_general(
            query_window, key_window, (((1,), (1,)), ((), ())), preferred_element_type=F32
        )
        scores = scores * scale + slopes_ref[head] * position
        top = jnp.max(scores, axis=1, keepdims=True)
        weights = jnp.exp(scores - top)
        total = jnp.sum(weights, axis=1, keepdims=True)
        for tile in span:
            wait(1, tile)
        value_window = jnp.concatenate([kv_buf[1, tile] for tile in span], axis=1)
        sums = jnp.dot(weights.astype(BF16), value_window, preferred_element_type=F32)
        sums = sums * (1.0 / total)
        for place, tile in enumerate(span):
            parts[tile] = jnp.where(
                lane_mask((rows, LANES), *head_lanes(head, tile, head_size)),
                sums[:, place * LANES : (place + 1) * LANES],
                parts[tile],
            )
        stats = jnp.where(stat_lane % heads == head, top + jnp.log(total), stats)
    for tile in range(tiles):
        out_ref[:, tile * LANES : (tile + 1) * LANES] = parts[tile].astype(BF16)
    high, middle, low = split_three(stats)
    group = stat_lane // heads
    packed = jnp.where(
        group == 0, high, jnp.where(group == 1, middle, jnp.where(group == 2, low, 0.0))
    )
    out_ref[:, tiles * LANES :] = packed.astype(BF16)


def prompt_part(query_rows, prefix_kv, slopes, offset):
    rows, width = query_rows.shape
    heads = slopes.shape[0]
    keys = prefix_kv.shape[1]
    tiles = width // LANES
    return pl.pallas_call(
        functools.partial(prompt_kernel, heads=heads, head_size=width // heads),
        out_shape=jax.ShapeDtypeStruct((rows, width + LANES), BF16),
        in_specs=[
            pl.BlockSpec(memory_space=pltpu.SMEM),
            pl.BlockSpec(memory_space=pltpu.SMEM),
            pl.BlockSpec(memory_space=pltpu.VMEM),
            pl.BlockSpec(memory_space=pltpu.HBM),
        ],
        out_specs=pl.BlockSpec(memory_space=pltpu.VMEM),
        scratch_shapes=[
            pltpu.VMEM((2, tiles, keys, LANES), BF16),
            pltpu.SemaphoreType.DMA((2, tiles)),
        ],
        compiler_params=pltpu.CompilerParams(vmem_limit_bytes=WHOLE_VMEM),
    )(offset, slopes, query_rows, prefix_kv)


def own_kernel(
    length_ref, slopes_ref, query_ref, suffix_ref, draft_ref, out_ref, stats_ref, *, heads, head_size
):
    draft, width = query_ref.shape
    slots = suffix_ref.shape[1]
    rows = heads * draft
    query = query_ref[...]
    masks = [
        lane_mask((draft, width), head * head_size, (head + 1) * head_size)
        for head in range(heads)
    ]
    spread = jnp.concatenate(
        [jnp.where(mask, query, jnp.zeros_like(query)) for mask in masks], axis=0
    )
    row = lax.broadcasted_iota(jnp.int32, (rows, 1), 0)
    slope = jnp.zeros((rows, 1), F32)
    for head in range(heads):
        slope = jnp.where(row // draft == head, slopes_ref[head], slope)
    scale = 1.0 / math.sqrt(head_size)
    length = length_ref[0]
    contract = (((1,), (1,)), ((), ()))
    slot = lax.broadcasted_iota(jnp.int32, (rows, slots), 1)
    suffix_scores = lax.dot_general(spread, suffix_ref[0], contract, preferred_element_type=F32)
    suffix_scores = suffix_scores * scale + slope * slot.astype(F32)
    suffix_scores = jnp.where(slot < length, suffix_scores, -jnp.inf)
    place = lax.broadcasted_iota(jnp.int32, (rows, draft), 1)
    draft_scores = lax.dot_general(spread, draft_ref[0], contract, preferred_element_type=F32)
    draft_scores = draft_scores * scale + slope * (place + length).astype(F32)
    token = lax.broadcasted_iota(jnp.int32, (rows, draft), 0) % draft
    draft_scores = jnp.where(place <= token, draft_scores, -jnp.inf)
    top = jnp.maximum(
        jnp.max(suffix_scores, axis=1, keepdims=True), jnp.max(draft_scores, axis=1, keepdims=True)
    )
    suffix_weights = jnp.exp(suffix_scores - top)
    draft_weights = jnp.exp(draft_scores - top)
    total = jnp.sum(suffix_weights, axis=1, keepdims=True) + jnp.sum(
        draft_weights, axis=1, keepdims=True
    )
    sums = jnp.dot(suffix_weights.astype(BF16), suffix_ref[1], preferred_element_type=F32)
    sums += jnp.dot(draft_weights.astype(BF16), draft_ref[1], preferred_element_type=F32)
    sums = sums * (1.0 / total)
    level = top + jnp.log(total)
    result = jnp.zeros((draft, width), F32)
    stats = jnp.zeros((draft, LANES), F32)
    lane = lax.broadcasted_iota(jnp.int32, (draft, LANES), 1)
    for head in range(heads):
        rows_of = slice(head * draft, (head + 1) * draft)
        result = jnp.where(masks[head], sums[rows_of], result)
        stats = jnp.where(lane == head, level[rows_of], stats)
    out_ref[...] = result
    stats_ref[...] = stats


def own_part(query_rows, suffix_kv, draft_kv, slopes, length):
    draft, width = query_rows.shape
    heads = slopes.shape[0]
    vmem = pl.BlockSpec(memory_space=pltpu.VMEM)
    smem = pl.BlockSpec(memory_space=pltpu.SMEM)
    return pl.pallas_call(
        functools.partial(own_kernel, heads=heads, head_size=width // heads),
        out_shape=(
            jax.ShapeDtypeStruct((draft, width), F32),
            jax.ShapeDtypeStruct((draft, LANES), F32),
        ),
        in_specs=[smem, smem, vmem, vmem, vmem],
        out_specs=(vmem, vmem),
        compiler_params=pltpu.CompilerParams(vmem_limit_bytes=24 * 1024 * 1024),
    )(length, slopes, query_rows, suffix_kv, draft_kv)


def merge_kernel(parts_ref, own_ref, level_ref, out_ref, *, heads, head_size):
    count, draft, _ = parts_ref.shape
    width = own_ref.shape[1]
    tiles = width // LANES
    levels = [level_ref[...]]
    for part in range(count):
        packed = parts_ref[part, :, width:].astype(F32)
        levels.append(
            packed
            + pltpu.roll(packed, LANES - heads, 1)
            + pltpu.roll(packed, LANES - 2 * heads, 1)
        )
    top = functools.reduce(jnp.maximum, levels)
    shares = [jnp.exp(level - top) for level in levels]
    total = functools.reduce(jnp.add, shares)
    shares = [share / total for share in shares]
    for tile in range(tiles):
        lanes = slice(tile * LANES, (tile + 1) * LANES)
        joined = jnp.zeros((draft, LANES), F32)
        for part, share in enumerate(shares):
            factor = jnp.zeros((draft, LANES), F32)
            for head in range(heads):
                first, last = head_lanes(head, tile, head_size)
                if first < last:
                    factor = jnp.where(
                        lane_mask((draft, LANES), first, last), share[:, head : head + 1], factor
                    )
            value = own_ref[:, lanes] if part == 0 else parts_ref[part - 1, :, lanes].astype(F32)
            joined += factor * value
        joined = joined.astype(BF16)
        for target in range(out_ref.shape[0]):
            out_ref[target, :, lanes] = joined


def merge_parts(parts, own, level, heads, targets):
    draft, width = own.shape
    vmem = pl.BlockSpec(memory_space=pltpu.VMEM)
    return pl.pallas_call(
        functools.partial(merge_kernel, heads=heads, head_size=width // heads),
        out_shape=jax.ShapeDtypeStruct((targets, draft, width), BF16),
        in_specs=[vmem, vmem, vmem],
        out_specs=vmem,
    )(parts, own, level)


def residual_kernel(parts_ref, out_ref, sums_ref):
    mp, pair, draft, columns = parts_ref.shape
    blocks = []
    for half in range(pair):
        block = parts_ref[0, half].astype(F32)
        for piece in range(1, mp):
            block += parts_ref[piece, half].astype(F32)
        blocks.append(block)
        out_ref[:, half * columns : (half + 1) * columns] = block
    lane = lax.broadcasted_iota(jnp.int32, (draft, LANES), 1)
    first = sum(jnp.sum(block, axis=1, keepdims=True) for block in blocks)
    second = sum(jnp.sum(block * block, axis=1, keepdims=True) for block in blocks)
    sums_ref[...] = jnp.where(lane == 0, first, jnp.where(lane == 1, second, 0.0))


def residual_rows(parts):
    mp, pair, draft, columns = parts.shape
    vmem = pl.BlockSpec(memory_space=pltpu.VMEM)
    return pl.pallas_call(
        residual_kernel,
        out_shape=(
            jax.ShapeDtypeStruct((draft, pair * columns), F32),
            jax.ShapeDtypeStruct((draft, LANES), F32),
        ),
        in_specs=[vmem],
        out_specs=(vmem, vmem),
    )(parts)


def norm_kernel(residual_ref, gain_ref, *rest, model_width):
    *sums_refs, out_ref = rest
    sums = functools.reduce(jnp.add, [ref[...] for ref in sums_refs])
    mean = sums[:, 0:1] / model_width
    mean_square = sums[:, 1:2] / model_width
    factor = lax.rsqrt(mean_square - mean * mean + 1e-05)
    normed = ((residual_ref[...] - mean) * factor * gain_ref[...]).astype(BF16)
    for target in range(out_ref.shape[0]):
        out_ref[target] = normed


def norm_rows(residual, sums, gain, model_width, targets):
    vmem = pl.BlockSpec(memory_space=pltpu.VMEM)
    return pl.pallas_call(
        functools.partial(norm_kernel, model_width=model_width),
        out_shape=jax.ShapeDtypeStruct((targets,) + residual.shape, BF16),
        in_specs=[vmem] * (2 + len(sums)),
        out_specs=vmem,
    )(residual, gain[None, :], *sums)


def arriving(refs, buf, sems):
    blocks = refs[0].shape[0]
    copies = [
        pltpu.make_async_copy(ref.at[block], buf.at[place * blocks + block], sems.at[place * blocks + block])
        for place, ref in enumerate(refs)
        for block in range(blocks)
    ]
    for copy in copies:
        copy.start()

    def block_at(index):
        copies[index].wait()
        return buf[index]

    return block_at


def lift_kernel(rows_ref, own_ref, other_ref, out_ref, buf, sems):
    block_at = arriving((own_ref, other_ref), buf, sems)
    rows = rows_ref[...]
    shares, blocks, share, _ = out_ref.shape
    for block in range(blocks):
        lifted = lax.dot_general(
            rows, block_at(block), (((1,), (1,)), ((), ())), preferred_element_type=F32
        ).astype(BF16)
        for piece in range(shares):
            out_ref[piece, block] = lifted[piece * share : (piece + 1) * share]


def lift_rows(rows, own, other, shares):
    vmem = pl.BlockSpec(memory_space=pltpu.VMEM)
    hbm = pl.BlockSpec(memory_space=pltpu.HBM)
    blocks, hidden, width = own.shape
    return pl.pallas_call(
        lift_kernel,
        out_shape=jax.ShapeDtypeStruct((shares, 2 * blocks, rows.shape[0] // shares, hidden), BF16),
        in_specs=[vmem, hbm, hbm],
        out_specs=vmem,
        scratch_shapes=[
            pltpu.VMEM((2 * blocks, hidden, width), BF16),
            pltpu.SemaphoreType.DMA((2 * blocks,)),
        ],
        compiler_params=pltpu.CompilerParams(vmem_limit_bytes=WHOLE_VMEM),
    )(rows, own, other)


def gelu_kernel(parts_ref, out_ref):
    total = parts_ref[0].astype(F32)
    for piece in range(1, parts_ref.shape[0]):
        total += parts_ref[piece].astype(F32)
    activated = (0.5 * total * (1.0 + lax.erf(total * math.sqrt(0.5)))).astype(BF16)
    for target in range(out_ref.shape[0]):
        out_ref[target] = activated


def activate(parts):
    vmem = pl.BlockSpec(memory_space=pltpu.VMEM)
    return pl.pallas_call(
        gelu_kernel,
        out_shape=jax.ShapeDtypeStruct(parts.shape, BF16),
        in_specs=[vmem],
        out_specs=vmem,
    )(parts)


def lower_kernel(hidden_ref, own_ref, other_ref, out_ref, buf, sems):
    block_at = arriving((own_ref, other_ref), buf, sems)
    shares, blocks, share, _ = hidden_ref.shape
    targets, draft, width = out_ref.shape
    total = None
    for block in range(blocks):
        rows = jnp.concatenate([hidden_ref[piece, block] for piece in range(shares)], axis=0)
        product = jnp.dot(rows, block_at(block), preferred_element_type=F32)
        total = product if total is None else total + product
    out_ref[...] = total.astype(BF16).reshape(targets, draft, width)


def lower_rows(hidden, own, other, targets):
    vmem = pl.BlockSpec(memory_space=pltpu.VMEM)
    hbm = pl.BlockSpec(memory_space=pltpu.HBM)
    rows = hidden.shape[0] * hidden.shape[2]
    blocks, features, width = own.shape
    return pl.pallas_call(
        lower_kernel,
        out_shape=jax.ShapeDtypeStruct((targets, rows // targets, width), BF16),
        in_specs=[vmem, hbm, hbm],
        out_specs=vmem,
        scratch_shapes=[
            pltpu.VMEM((2 * blocks, features, width), BF16),
            pltpu.SemaphoreType.DMA((2 * blocks,)),
        ],
        compiler_params=pltpu.CompilerParams(vmem_limit_bytes=WHOLE_VMEM),
    )(hidden, own, other)


def finish_kernel(parts_ref, residual_ref, out_ref):
    total = parts_ref[0].astype(F32)
    for piece in range(1, parts_ref.shape[0]):
        total += parts_ref[piece].astype(F32)
    out_ref[...] = residual_ref[...] + total


def finish(parts, residual):
    vmem = pl.BlockSpec(memory_space=pltpu.VMEM)
    return pl.pallas_call(
        finish_kernel,
        out_shape=jax.ShapeDtypeStruct(residual.shape, F32),
        in_specs=[vmem, vmem],
        out_specs=vmem,
    )(parts, residual)


def after(value, earlier):
    return lax.optimization_barrier((value, earlier))[0]


def shifted_by(value, axis, step):
    count = lax.axis_size(axis)
    return lax.ppermute(value, axis, [(i, (i + step) % count) for i in range(count)])


def exchange(value, axis):
    return lax.all_to_all(value, axis, split_axis=0, concat_axis=0, tiled=True)


def per_device(
    token_ids,
    embed_table,
    queries,
    draft_kv,
    prefix_kv,
    suffix_kv,
    suffix_len,
    slopes,
    out_weight,
    ln_gain,
    up_weight,
    down_weight,
):
    ctx = ("y", "core")
    heads = slopes.shape[0]
    _, draft, width = queries.shape
    prompt_local = prefix_kv.shape[1]
    ctx_count = lax.axis_size(ctx)
    req_count = lax.axis_size("req")
    mp_count = lax.axis_size("mp")
    ctx_index = lax.axis_index(ctx)
    model_index = lax.axis_index("mp")
    quarter = ln_gain.shape[0]
    columns = out_weight.shape[1]

    copies = jnp.broadcast_to(queries, (ctx_count, draft, width))
    gathered = exchange(copies, ctx)
    out_all = lax.all_gather(out_weight.T, "req", tiled=True)
    up_own = lax.all_gather(after(up_weight, copies).T, "y")
    down_own = lax.all_gather(after(down_weight, copies), "y")

    vocab_local = embed_table.shape[0]
    shifted = (
        token_ids.reshape(ctx_count, req_count, draft).transpose(1, 0, 2).reshape(-1)
        - model_index * vocab_local
    )
    one_hot = (
        shifted[:, None] == jnp.arange(vocab_local, dtype=jnp.int32)[None, :]
    ).astype(BF16)
    looked_up = jnp.dot(one_hot, embed_table, preferred_element_type=F32).astype(BF16)
    own, own_level = own_part(queries[0], suffix_kv[:, 0], draft_kv[:, 0], slopes, suffix_len)
    gathered, looked_up, own = lax.optimization_barrier((gathered, looked_up, own))
    embedded = exchange(looked_up.reshape(req_count, ctx_count * draft, columns), "req")

    offset = (prompt_local * (ctx_count - ctx_index)).astype(jnp.int32).reshape(1)
    parts = prompt_part(gathered.reshape(ctx_count * draft, width), prefix_kv, slopes, offset)
    parts, embedded = lax.optimization_barrier((parts, embedded))
    embedded = embedded.transpose(1, 0, 2).reshape(ctx_count * draft, req_count * columns)
    parts = exchange(parts.reshape(ctx_count, draft, -1), ctx)
    attended = exchange(merge_parts(parts, own, own_level, heads, ctx_count), ctx)

    projected = lax.dot_general(
        attended.reshape(ctx_count * draft, width),
        out_all,
        (((1,), (1,)), ((), ())),
        preferred_element_type=F32,
    ) + embedded.astype(F32)
    projected = exchange(projected.astype(BF16).reshape(ctx_count, draft, -1), ctx)
    up_other = shifted_by(after(up_own, projected), "core", 1)
    pieces = exchange(projected.reshape(mp_count, ctx_count // mp_count, draft, -1), "mp")
    residual, sums = residual_rows(pieces)
    sums = [sums] + [shifted_by(sums, "mp", step) for step in range(1, mp_count)]
    normed = norm_rows(residual, sums, ln_gain, quarter * mp_count, req_count)
    down_other = shifted_by(after(down_own, normed), "core", 1)
    normed = exchange(normed, "req")

    lifted = exchange(
        lift_rows(normed.reshape(req_count * draft, quarter), up_own, up_other, mp_count), "mp"
    )
    activated = exchange(activate(lifted), "mp")
    lowered = exchange(lower_rows(activated, down_own, down_other, req_count), "req")
    layer_out = finish(lowered, residual)
    return residual[None], layer_out[None]


def solution(mesh):
    chips = jax.sharding.Mesh(
        mesh.devices.reshape((mesh.shape["ctx"] // 2, 2) + mesh.devices.shape[1:]),
        ("y", "core", "req", "mp"),
    )
    rows = ("y", "core", "req")
    in_specs = (
        P(),
        P("mp", rows),
        P(rows, None, "mp"),
        P(None, rows, None, "mp"),
        P(None, ("y", "core"), "mp"),
        P(None, rows, None, "mp"),
        P(rows),
        P("mp"),
        P("mp", rows),
        P("mp"),
        P("mp", rows),
        P(rows, "mp"),
    )
    out_specs = (P(rows, None, "mp"), P(rows, None, "mp"))
    return jax.shard_map(
        per_device, mesh=chips, in_specs=in_specs, out_specs=out_specs, check_vma=False
    )
```

```python
import functools
import math

import jax
import jax.numpy as jnp
from jax import lax
from jax.experimental import pallas as pl
from jax.experimental.pallas import tpu as pltpu
from jax.sharding import PartitionSpec as P

LANES = 128
F32 = jnp.float32
BF16 = jnp.bfloat16
WHOLE_VMEM = 58 * 1024 * 1024


def head_lanes(head, tile, head_size):
    first = max(head * head_size - tile * LANES, 0)
    last = min((head + 1) * head_size - tile * LANES, LANES)
    return first, last


def head_tiles(head, head_size):
    return range(head * head_size // LANES, ((head + 1) * head_size - 1) // LANES + 1)


def lane_mask(shape, first, last):
    lane = lax.broadcasted_iota(jnp.int32, shape, len(shape) - 1)
    return (lane >= first) & (lane < last)


def split_three(value):
    high = value.astype(BF16).astype(F32)
    rest = value - high
    middle = rest.astype(BF16).astype(F32)
    low = rest - middle
    return high, middle, low


def prompt_kernel(
    offset_ref, slopes_ref, query_ref, looked_ref, prefix_ref, out_ref, kv_buf, sems, *, heads, head_size
):
    rows, width = query_ref.shape
    keys = kv_buf.shape[2]
    tiles = width // LANES
    copies = {}
    for tile in range(tiles):
        for which in range(2):
            copies[which, tile] = pltpu.make_async_copy(
                prefix_ref.at[which, :, pl.ds(tile * LANES, LANES)],
                kv_buf.at[which, tile],
                sems.at[which, tile],
            )
            copies[which, tile].start()
    scale = 1.0 / math.sqrt(head_size)
    position = (
        lax.broadcasted_iota(jnp.int32, (1, keys), 1) - offset_ref[0]
    ).astype(F32)
    arrived = set()

    def wait(which, tile):
        if (which, tile) not in arrived:
            arrived.add((which, tile))
            copies[which, tile].wait()

    parts = [jnp.zeros((rows, LANES), F32) for _ in range(tiles)]
    stats = jnp.zeros((rows, LANES), F32)
    stat_lane = lax.broadcasted_iota(jnp.int32, (rows, LANES), 1)
    for head in range(heads):
        span = head_tiles(head, head_size)
        for tile in span:
            wait(0, tile)
        query_window = jnp.concatenate(
            [
                jnp.where(
                    lane_mask((rows, LANES), *head_lanes(head, tile, head_size)),
                    query_ref[:, tile * LANES : (tile + 1) * LANES],
                    jnp.zeros((rows, LANES), BF16),
                )
                for tile in span
            ],
            axis=1,
        )
        key_window = jnp.concatenate([kv_buf[0, tile] for tile in span], axis=1)
        scores = lax.dot_general(
            query_window, key_window, (((1,), (1,)), ((), ())), preferred_element_type=F32
        )
        scores = scores * scale + slopes_ref[head] * position
        top = jnp.max(scores, axis=1, keepdims=True)
        weights = jnp.exp(scores - top)
        total = jnp.sum(weights, axis=1, keepdims=True)
        for tile in span:
            wait(1, tile)
        value_window = jnp.concatenate([kv_buf[1, tile] for tile in span], axis=1)
        sums = jnp.dot(weights.astype(BF16), value_window, preferred_element_type=F32)
        sums = sums * (1.0 / total)
        for place, tile in enumerate(span):
            parts[tile] = jnp.where(
                lane_mask((rows, LANES), *head_lanes(head, tile, head_size)),
                sums[:, place * LANES : (place + 1) * LANES],
                parts[tile],
            )
        stats = jnp.where(stat_lane % heads == head, top + jnp.log(total), stats)
    high, middle, low = split_three(stats)
    group = stat_lane // heads
    packed = jnp.where(
        group == 0, high, jnp.where(group == 1, middle, jnp.where(group == 2, low, 0.0))
    )
    targets = out_ref.shape[0]
    draft = rows // targets
    for tile, value in enumerate([*parts, packed]):
        value = value.astype(BF16)
        for target in range(targets):
            out_ref[target, tile * draft : (tile + 1) * draft] = value[
                target * draft : (target + 1) * draft
            ]
    for target in range(targets):
        out_ref[target, (tiles + 1) * draft :] = looked_ref[
            :, target * LANES : (target + 1) * LANES
        ]


def prompt_part(query_rows, prefix_kv, slopes, offset, looked_up, targets):
    rows, width = query_rows.shape
    heads = slopes.shape[0]
    keys = prefix_kv.shape[1]
    tiles = width // LANES
    return pl.pallas_call(
        functools.partial(prompt_kernel, heads=heads, head_size=width // heads),
        out_shape=jax.ShapeDtypeStruct(
            (targets, (tiles + 1) * (rows // targets) + looked_up.shape[0], LANES), BF16
        ),
        in_specs=[
            pl.BlockSpec(memory_space=pltpu.SMEM),
            pl.BlockSpec(memory_space=pltpu.SMEM),
            pl.BlockSpec(memory_space=pltpu.VMEM),
            pl.BlockSpec(memory_space=pltpu.VMEM),
            pl.BlockSpec(memory_space=pltpu.HBM),
        ],
        out_specs=pl.BlockSpec(memory_space=pltpu.VMEM),
        scratch_shapes=[
            pltpu.VMEM((2, tiles, keys, LANES), BF16),
            pltpu.SemaphoreType.DMA((2, tiles)),
        ],
        compiler_params=pltpu.CompilerParams(vmem_limit_bytes=WHOLE_VMEM),
    )(offset, slopes, query_rows, looked_up, prefix_kv)


def own_kernel(
    length_ref, slopes_ref, query_ref, suffix_ref, draft_ref, out_ref, stats_ref, *, heads, head_size
):
    draft, width = query_ref.shape
    slots = suffix_ref.shape[1]
    rows = heads * draft
    query = query_ref[...]
    masks = [
        lane_mask((draft, width), head * head_size, (head + 1) * head_size)
        for head in range(heads)
    ]
    spread = jnp.concatenate(
        [jnp.where(mask, query, jnp.zeros_like(query)) for mask in masks], axis=0
    )
    row = lax.broadcasted_iota(jnp.int32, (rows, 1), 0)
    slope = jnp.zeros((rows, 1), F32)
    for head in range(heads):
        slope = jnp.where(row // draft == head, slopes_ref[head], slope)
    scale = 1.0 / math.sqrt(head_size)
    length = length_ref[0]
    contract = (((1,), (1,)), ((), ()))
    slot = lax.broadcasted_iota(jnp.int32, (rows, slots), 1)
    suffix_scores = lax.dot_general(spread, suffix_ref[0], contract, preferred_element_type=F32)
    suffix_scores = suffix_scores * scale + slope * slot.astype(F32)
    suffix_scores = jnp.where(slot < length, suffix_scores, -jnp.inf)
    place = lax.broadcasted_iota(jnp.int32, (rows, draft), 1)
    draft_scores = lax.dot_general(spread, draft_ref[0], contract, preferred_element_type=F32)
    draft_scores = draft_scores * scale + slope * (place + length).astype(F32)
    token = lax.broadcasted_iota(jnp.int32, (rows, draft), 0) % draft
    draft_scores = jnp.where(place <= token, draft_scores, -jnp.inf)
    top = jnp.maximum(
        jnp.max(suffix_scores, axis=1, keepdims=True), jnp.max(draft_scores, axis=1, keepdims=True)
    )
    suffix_weights = jnp.exp(suffix_scores - top)
    draft_weights = jnp.exp(draft_scores - top)
    total = jnp.sum(suffix_weights, axis=1, keepdims=True) + jnp.sum(
        draft_weights, axis=1, keepdims=True
    )
    sums = jnp.dot(suffix_weights.astype(BF16), suffix_ref[1], preferred_element_type=F32)
    sums += jnp.dot(draft_weights.astype(BF16), draft_ref[1], preferred_element_type=F32)
    sums = sums * (1.0 / total)
    level = top + jnp.log(total)
    result = jnp.zeros((draft, width), F32)
    stats = jnp.zeros((draft, LANES), F32)
    lane = lax.broadcasted_iota(jnp.int32, (draft, LANES), 1)
    for head in range(heads):
        rows_of = slice(head * draft, (head + 1) * draft)
        result = jnp.where(masks[head], sums[rows_of], result)
        stats = jnp.where(lane == head, level[rows_of], stats)
    out_ref[...] = result
    stats_ref[...] = stats


def own_part(query_rows, suffix_kv, draft_kv, slopes, length):
    draft, width = query_rows.shape
    heads = slopes.shape[0]
    vmem = pl.BlockSpec(memory_space=pltpu.VMEM)
    smem = pl.BlockSpec(memory_space=pltpu.SMEM)
    return pl.pallas_call(
        functools.partial(own_kernel, heads=heads, head_size=width // heads),
        out_shape=(
            jax.ShapeDtypeStruct((draft, width), F32),
            jax.ShapeDtypeStruct((draft, LANES), F32),
        ),
        in_specs=[smem, smem, vmem, vmem, vmem],
        out_specs=(vmem, vmem),
        compiler_params=pltpu.CompilerParams(vmem_limit_bytes=24 * 1024 * 1024),
    )(length, slopes, query_rows, suffix_kv, draft_kv)


def merge_kernel(parts_ref, own_ref, level_ref, out_ref, *, heads, head_size):
    count = parts_ref.shape[0]
    draft, width = own_ref.shape
    tiles = width // LANES
    levels = [level_ref[...]]
    for part in range(count):
        packed = parts_ref[part, tiles * draft : (tiles + 1) * draft].astype(F32)
        levels.append(
            packed
            + pltpu.roll(packed, LANES - heads, 1)
            + pltpu.roll(packed, LANES - 2 * heads, 1)
        )
    top = functools.reduce(jnp.maximum, levels)
    shares = [jnp.exp(level - top) for level in levels]
    total = functools.reduce(jnp.add, shares)
    shares = [share / total for share in shares]
    for tile in range(tiles):
        lanes = slice(tile * LANES, (tile + 1) * LANES)
        joined = jnp.zeros((draft, LANES), F32)
        for part, share in enumerate(shares):
            factor = jnp.zeros((draft, LANES), F32)
            for head in range(heads):
                first, last = head_lanes(head, tile, head_size)
                if first < last:
                    factor = jnp.where(
                        lane_mask((draft, LANES), first, last), share[:, head : head + 1], factor
                    )
            if part == 0:
                value = own_ref[:, lanes]
            else:
                value = parts_ref[part - 1, tile * draft : (tile + 1) * draft].astype(F32)
            joined += factor * value
        joined = joined.astype(BF16)
        for target in range(out_ref.shape[0]):
            out_ref[target, :, lanes] = joined


def merge_parts(parts, own, level, heads, targets):
    draft, width = own.shape
    vmem = pl.BlockSpec(memory_space=pltpu.VMEM)
    return pl.pallas_call(
        functools.partial(merge_kernel, heads=heads, head_size=width // heads),
        out_shape=jax.ShapeDtypeStruct((targets, draft, width), BF16),
        in_specs=[vmem, vmem, vmem],
        out_specs=vmem,
    )(parts, own, level)


def project_kernel(rows_ref, weight_ref, parts_ref, out_ref):
    blocks, columns, _ = weight_ref.shape
    targets, held, _ = out_ref.shape
    req, draft, width = rows_ref.shape
    mp = targets // req
    pair = held // draft
    rows = rows_ref[...].reshape(req * draft, width)
    for block in range(blocks):
        product = lax.dot_general(
            rows, weight_ref[block], (((1,), (1,)), ((), ())), preferred_element_type=F32
        )
        looked_up = parts_ref[block, parts_ref.shape[1] - columns :].astype(F32)
        product = (product + jnp.transpose(looked_up)).astype(BF16)
        piece, half = divmod(block, pair)
        for target in range(req):
            out_ref[target * mp + piece, half * draft : (half + 1) * draft] = product[
                target * draft : (target + 1) * draft
            ]


def project_rows(rows, weight, parts, mp):
    req, draft, _ = rows.shape
    blocks, columns, _ = weight.shape
    vmem = pl.BlockSpec(memory_space=pltpu.VMEM)
    return pl.pallas_call(
        project_kernel,
        out_shape=jax.ShapeDtypeStruct((req * mp, blocks // mp * draft, columns), BF16),
        in_specs=[vmem, vmem, vmem],
        out_specs=vmem,
    )(rows, weight, parts)


def residual_kernel(parts_ref, out_ref, sums_ref, *, mp):
    sources, held, columns = parts_ref.shape
    draft = out_ref.shape[0]
    blocks = []
    for half in range(held // draft):
        lines = slice(half * draft, (half + 1) * draft)
        for source in range(sources // mp):
            block = parts_ref[source * mp, lines].astype(F32)
            for piece in range(1, mp):
                block += parts_ref[source * mp + piece, lines].astype(F32)
            blocks.append(block)
    residual = jnp.concatenate(blocks, axis=1)
    out_ref[...] = residual
    lane = lax.broadcasted_iota(jnp.int32, (draft, LANES), 1)
    first = jnp.sum(residual, axis=1, keepdims=True)
    second = jnp.sum(residual * residual, axis=1, keepdims=True)
    sums_ref[...] = jnp.where(lane == 0, first, jnp.where(lane == 1, second, 0.0))


def residual_rows(parts, mp, draft):
    sources, held, columns = parts.shape
    vmem = pl.BlockSpec(memory_space=pltpu.VMEM)
    return pl.pallas_call(
        functools.partial(residual_kernel, mp=mp),
        out_shape=(
            jax.ShapeDtypeStruct((draft, sources // mp * held // draft * columns), F32),
            jax.ShapeDtypeStruct((draft, LANES), F32),
        ),
        in_specs=[vmem],
        out_specs=(vmem, vmem),
    )(parts)


def norm_kernel(residual_ref, gain_ref, *rest, model_width):
    *sums_refs, out_ref = rest
    sums = functools.reduce(jnp.add, [ref[...] for ref in sums_refs])
    mean = sums[:, 0:1] / model_width
    mean_square = sums[:, 1:2] / model_width
    factor = lax.rsqrt(mean_square - mean * mean + 1e-05)
    normed = ((residual_ref[...] - mean) * factor * gain_ref[...]).astype(BF16)
    for target in range(out_ref.shape[0]):
        out_ref[target] = normed


def norm_rows(residual, sums, gain, model_width, targets):
    vmem = pl.BlockSpec(memory_space=pltpu.VMEM)
    return pl.pallas_call(
        functools.partial(norm_kernel, model_width=model_width),
        out_shape=jax.ShapeDtypeStruct((targets,) + residual.shape, BF16),
        in_specs=[vmem] * (2 + len(sums)),
        out_specs=vmem,
    )(residual, gain[None, :], *sums)


def arriving(ref, buf, sems):
    copies = [
        pltpu.make_async_copy(ref.at[block], buf.at[block], sems.at[block])
        for block in range(ref.shape[0])
    ]
    for copy in copies:
        copy.start()

    def block_at(index):
        copies[index].wait()
        return buf[index]

    return block_at


def lift_kernel(rows_ref, weight_ref, out_ref, buf, sems):
    block_at = arriving(weight_ref, buf, sems)
    rows = rows_ref[...]
    pair = out_ref.shape[1]
    for block in range(weight_ref.shape[0]):
        out_ref[block // pair, block % pair] = lax.dot_general(
            block_at(block), rows, (((1,), (1,)), ((), ())), preferred_element_type=F32
        ).astype(BF16)


def lift_rows(rows, weight, mp):
    blocks, hidden, width = weight.shape
    return pl.pallas_call(
        lift_kernel,
        out_shape=jax.ShapeDtypeStruct((mp, blocks // mp, hidden, rows.shape[0]), BF16),
        in_specs=[pl.BlockSpec(memory_space=pltpu.VMEM), pl.BlockSpec(memory_space=pltpu.HBM)],
        out_specs=pl.BlockSpec(memory_space=pltpu.VMEM),
        scratch_shapes=[
            pltpu.VMEM((blocks, hidden, width), BF16),
            pltpu.SemaphoreType.DMA((blocks,)),
        ],
        compiler_params=pltpu.CompilerParams(vmem_limit_bytes=WHOLE_VMEM),
    )(rows, weight)


def gelu_kernel(parts_ref, out_ref):
    total = parts_ref[0].astype(F32)
    for piece in range(1, parts_ref.shape[0]):
        total += parts_ref[piece].astype(F32)
    activated = (0.5 * total * (1.0 + lax.erf(total * math.sqrt(0.5)))).astype(BF16)
    for target in range(out_ref.shape[0]):
        out_ref[target] = activated


def activate(parts):
    vmem = pl.BlockSpec(memory_space=pltpu.VMEM)
    return pl.pallas_call(
        gelu_kernel,
        out_shape=jax.ShapeDtypeStruct(parts.shape, BF16),
        in_specs=[vmem],
        out_specs=vmem,
    )(parts)


def lower_kernel(hidden_ref, weight_ref, out_ref, buf, sems):
    block_at = arriving(weight_ref, buf, sems)
    _, pair, _, rows = hidden_ref.shape
    targets, draft, width = out_ref.shape
    total = None
    for block in range(weight_ref.shape[0]):
        product = lax.dot_general(
            hidden_ref[block // pair, block % pair],
            block_at(block),
            (((0,), (0,)), ((), ())),
            preferred_element_type=F32,
        )
        total = product if total is None else total + product
    out_ref[...] = total.astype(BF16).reshape(targets, draft, width)


def lower_rows(hidden, weight, targets):
    blocks, features, width = weight.shape
    return pl.pallas_call(
        lower_kernel,
        out_shape=jax.ShapeDtypeStruct((targets, hidden.shape[3] // targets, width), BF16),
        in_specs=[pl.BlockSpec(memory_space=pltpu.VMEM), pl.BlockSpec(memory_space=pltpu.HBM)],
        out_specs=pl.BlockSpec(memory_space=pltpu.VMEM),
        scratch_shapes=[
            pltpu.VMEM((blocks, features, width), BF16),
            pltpu.SemaphoreType.DMA((blocks,)),
        ],
        compiler_params=pltpu.CompilerParams(vmem_limit_bytes=WHOLE_VMEM),
    )(hidden, weight)


def finish_kernel(parts_ref, residual_ref, out_ref):
    total = parts_ref[0].astype(F32)
    for piece in range(1, parts_ref.shape[0]):
        total += parts_ref[piece].astype(F32)
    out_ref[...] = residual_ref[...] + total


def finish(parts, residual):
    vmem = pl.BlockSpec(memory_space=pltpu.VMEM)
    return pl.pallas_call(
        finish_kernel,
        out_shape=jax.ShapeDtypeStruct(residual.shape, F32),
        in_specs=[vmem, vmem],
        out_specs=vmem,
    )(parts, residual)


def after(value, earlier):
    return lax.optimization_barrier((value, earlier))[0]


def shifted_by(value, axis, step):
    count = lax.axis_size(axis)
    return lax.ppermute(value, axis, [(i, (i + step) % count) for i in range(count)])


def exchange(value, axis):
    return lax.all_to_all(value, axis, split_axis=0, concat_axis=0, tiled=True)


def per_device(
    token_ids,
    embed_table,
    queries,
    draft_kv,
    prefix_kv,
    suffix_kv,
    suffix_len,
    slopes,
    out_weight,
    ln_gain,
    up_weight,
    down_weight,
):
    heads = slopes.shape[0]
    _, draft, width = queries.shape
    prompt_local = prefix_kv.shape[1]
    ctx_count = lax.axis_size("ctx")
    req_count = lax.axis_size("req")
    mp_count = lax.axis_size("mp")
    ctx_index = lax.axis_index("ctx")
    model_index = lax.axis_index("mp")
    quarter = ln_gain.shape[0]

    copies = jnp.broadcast_to(queries, (ctx_count, draft, width))
    gathered = exchange(copies, "ctx")
    out_all = lax.all_gather(out_weight.T, "ctx")
    up_all = lax.all_gather(after(up_weight, copies).T, "ctx")
    down_all = lax.all_gather(after(down_weight, copies), "ctx")

    vocab_local = embed_table.shape[0]
    shifted = token_ids.reshape(-1) - model_index * vocab_local
    one_hot = (
        shifted[:, None] == jnp.arange(vocab_local, dtype=jnp.int32)[None, :]
    ).astype(BF16)
    looked_up = jnp.dot(one_hot, embed_table, preferred_element_type=F32).astype(BF16)
    own, own_level = own_part(queries[0], suffix_kv[:, 0], draft_kv[:, 0], slopes, suffix_len)
    gathered, looked_up, own = lax.optimization_barrier((gathered, looked_up, own))

    offset = (prompt_local * (ctx_count - ctx_index)).astype(jnp.int32).reshape(1)
    parts = prompt_part(
        gathered.reshape(ctx_count * draft, width),
        prefix_kv,
        slopes,
        offset,
        looked_up.T,
        ctx_count,
    )
    parts = exchange(parts, "ctx")
    attended = exchange(merge_parts(parts, own, own_level, heads, req_count), "req")

    pieces = exchange(project_rows(attended, out_all, parts, mp_count), ("req", "mp"))
    residual, sums = residual_rows(pieces, mp_count, draft)
    sums = [sums] + [shifted_by(sums, "mp", step) for step in range(1, mp_count)]
    normed = exchange(norm_rows(residual, sums, ln_gain, quarter * mp_count, req_count), "req")

    lifted = exchange(
        lift_rows(normed.reshape(req_count * draft, quarter), up_all, mp_count), "mp"
    )
    activated = exchange(activate(lifted), "mp")
    lowered = exchange(lower_rows(activated, down_all, req_count), "req")
    layer_out = finish(lowered, residual)
    return residual[None], layer_out[None]


def solution(mesh):
    rows = ("ctx", "req")
    in_specs = (
        P(),
        P("mp", rows),
        P(rows, None, "mp"),
        P(None, rows, None, "mp"),
        P(None, "ctx", "mp"),
        P(None, rows, None, "mp"),
        P(rows),
        P("mp"),
        P("mp", rows),
        P("mp"),
        P("mp", rows),
        P(rows, "mp"),
    )
    out_specs = (P(rows, None, "mp"), P(rows, None, "mp"))
    return jax.shard_map(
        per_device, mesh=mesh, in_specs=in_specs, out_specs=out_specs, check_vma=False
    )
```

```python
import functools
import math

import jax
import jax.numpy as jnp
from jax import lax
from jax.experimental import pallas as pl
from jax.experimental.pallas import tpu as pltpu
from jax.sharding import PartitionSpec as P

LANES = 128
F32 = jnp.float32
BF16 = jnp.bfloat16
MIB = 1024 * 1024


def head_lanes(head, tile, head_size):
    first = max(head * head_size - tile * LANES, 0)
    last = min((head + 1) * head_size - tile * LANES, LANES)
    return first, last


def head_tiles(head, head_size):
    return range(head * head_size // LANES, ((head + 1) * head_size - 1) // LANES + 1)


def lane_mask(shape, first, last):
    lane = lax.broadcasted_iota(jnp.int32, shape, len(shape) - 1)
    return (lane >= first) & (lane < last)


def split_three(value):
    high = value.astype(BF16).astype(F32)
    rest = value - high
    middle = rest.astype(BF16).astype(F32)
    low = rest - middle
    return high, middle, low


def prompt_kernel(
    offset_ref, slopes_ref, query_ref, looked_ref, prefix_ref, out_ref, *, heads, head_size
):
    rows, width = query_ref.shape
    keys = prefix_ref.shape[1]
    tiles = width // LANES
    scale = 1.0 / math.sqrt(head_size)
    position = (
        lax.broadcasted_iota(jnp.int32, (1, keys), 1) - offset_ref[0]
    ).astype(F32)
    parts = [jnp.zeros((rows, LANES), F32) for _ in range(tiles)]
    stats = jnp.zeros((rows, LANES), F32)
    stat_lane = lax.broadcasted_iota(jnp.int32, (rows, LANES), 1)
    for head in range(heads):
        span = head_tiles(head, head_size)
        window = slice(span[0] * LANES, (span[-1] + 1) * LANES)
        query_window = jnp.concatenate(
            [
                jnp.where(
                    lane_mask((rows, LANES), *head_lanes(head, tile, head_size)),
                    query_ref[:, tile * LANES : (tile + 1) * LANES],
                    jnp.zeros((rows, LANES), BF16),
                )
                for tile in span
            ],
            axis=1,
        )
        scores = lax.dot_general(
            query_window,
            prefix_ref[0, :, window],
            (((1,), (1,)), ((), ())),
            preferred_element_type=F32,
        )
        scores = scores * scale + slopes_ref[head] * position
        top = jnp.max(scores, axis=1, keepdims=True)
        weights = jnp.exp(scores - top)
        total = jnp.sum(weights, axis=1, keepdims=True)
        sums = jnp.dot(
            weights.astype(BF16), prefix_ref[1, :, window], preferred_element_type=F32
        )
        sums = sums * (1.0 / total)
        for place, tile in enumerate(span):
            parts[tile] = jnp.where(
                lane_mask((rows, LANES), *head_lanes(head, tile, head_size)),
                sums[:, place * LANES : (place + 1) * LANES],
                parts[tile],
            )
        stats = jnp.where(stat_lane % heads == head, top + jnp.log(total), stats)
    high, middle, low = split_three(stats)
    group = stat_lane // heads
    packed = jnp.where(
        group == 0, high, jnp.where(group == 1, middle, jnp.where(group == 2, low, 0.0))
    )
    targets = out_ref.shape[0]
    draft = rows // targets
    for tile, value in enumerate([*parts, packed]):
        value = value.astype(BF16)
        for target in range(targets):
            out_ref[target, tile * draft : (tile + 1) * draft] = value[
                target * draft : (target + 1) * draft
            ]
    for target in range(targets):
        out_ref[target, (tiles + 1) * draft :] = looked_ref[
            :, target * LANES : (target + 1) * LANES
        ]


def prompt_part(query_rows, prefix_kv, slopes, offset, looked_up, targets):
    rows, width = query_rows.shape
    heads = slopes.shape[0]
    tiles = width // LANES
    return pl.pallas_call(
        functools.partial(prompt_kernel, heads=heads, head_size=width // heads),
        out_shape=jax.ShapeDtypeStruct(
            (targets, (tiles + 1) * (rows // targets) + looked_up.shape[0], LANES), BF16
        ),
        in_specs=[
            pl.BlockSpec(memory_space=pltpu.SMEM),
            pl.BlockSpec(memory_space=pltpu.SMEM),
            pl.BlockSpec(memory_space=pltpu.VMEM),
            pl.BlockSpec(memory_space=pltpu.VMEM),
            pl.BlockSpec(memory_space=pltpu.VMEM),
        ],
        out_specs=pl.BlockSpec(memory_space=pltpu.VMEM),
        compiler_params=pltpu.CompilerParams(vmem_limit_bytes=20 * MIB),
    )(offset, slopes, query_rows, looked_up, prefix_kv)


def own_kernel(
    length_ref, slopes_ref, query_ref, suffix_ref, draft_ref, out_ref, stats_ref, *, heads, head_size
):
    draft, width = query_ref.shape
    slots = suffix_ref.shape[1]
    rows = heads * draft
    query = query_ref[...]
    masks = [
        lane_mask((draft, width), head * head_size, (head + 1) * head_size)
        for head in range(heads)
    ]
    spread = jnp.concatenate(
        [jnp.where(mask, query, jnp.zeros_like(query)) for mask in masks], axis=0
    )
    row = lax.broadcasted_iota(jnp.int32, (rows, 1), 0)
    slope = jnp.zeros((rows, 1), F32)
    for head in range(heads):
        slope = jnp.where(row // draft == head, slopes_ref[head], slope)
    scale = 1.0 / math.sqrt(head_size)
    length = length_ref[0]
    contract = (((1,), (1,)), ((), ()))
    slot = lax.broadcasted_iota(jnp.int32, (rows, slots), 1)
    suffix_scores = lax.dot_general(spread, suffix_ref[0], contract, preferred_element_type=F32)
    suffix_scores = suffix_scores * scale + slope * slot.astype(F32)
    suffix_scores = jnp.where(slot < length, suffix_scores, -jnp.inf)
    place = lax.broadcasted_iota(jnp.int32, (rows, draft), 1)
    draft_scores = lax.dot_general(spread, draft_ref[0], contract, preferred_element_type=F32)
    draft_scores = draft_scores * scale + slope * (place + length).astype(F32)
    token = lax.broadcasted_iota(jnp.int32, (rows, draft), 0) % draft
    draft_scores = jnp.where(place <= token, draft_scores, -jnp.inf)
    top = jnp.maximum(
        jnp.max(suffix_scores, axis=1, keepdims=True), jnp.max(draft_scores, axis=1, keepdims=True)
    )
    suffix_weights = jnp.exp(suffix_scores - top)
    draft_weights = jnp.exp(draft_scores - top)
    total = jnp.sum(suffix_weights, axis=1, keepdims=True) + jnp.sum(
        draft_weights, axis=1, keepdims=True
    )
    sums = jnp.dot(suffix_weights.astype(BF16), suffix_ref[1], preferred_element_type=F32)
    sums += jnp.dot(draft_weights.astype(BF16), draft_ref[1], preferred_element_type=F32)
    sums = sums * (1.0 / total)
    level = top + jnp.log(total)
    result = jnp.zeros((draft, width), F32)
    stats = jnp.zeros((draft, LANES), F32)
    lane = lax.broadcasted_iota(jnp.int32, (draft, LANES), 1)
    for head in range(heads):
        rows_of = slice(head * draft, (head + 1) * draft)
        result = jnp.where(masks[head], sums[rows_of], result)
        stats = jnp.where(lane == head, level[rows_of], stats)
    out_ref[...] = result
    stats_ref[...] = stats


def own_part(query_rows, suffix_kv, draft_kv, slopes, length):
    draft, width = query_rows.shape
    heads = slopes.shape[0]
    vmem = pl.BlockSpec(memory_space=pltpu.VMEM)
    smem = pl.BlockSpec(memory_space=pltpu.SMEM)
    return pl.pallas_call(
        functools.partial(own_kernel, heads=heads, head_size=width // heads),
        out_shape=(
            jax.ShapeDtypeStruct((draft, width), F32),
            jax.ShapeDtypeStruct((draft, LANES), F32),
        ),
        in_specs=[smem, smem, vmem, vmem, vmem],
        out_specs=(vmem, vmem),
        compiler_params=pltpu.CompilerParams(vmem_limit_bytes=12 * MIB),
    )(length, slopes, query_rows, suffix_kv, draft_kv)


def merge_kernel(parts_ref, own_ref, level_ref, out_ref, *, heads, head_size):
    count = parts_ref.shape[0]
    draft, width = own_ref.shape
    tiles = width // LANES
    levels = [level_ref[...]]
    for part in range(count):
        packed = parts_ref[part, tiles * draft : (tiles + 1) * draft].astype(F32)
        levels.append(
            packed
            + pltpu.roll(packed, LANES - heads, 1)
            + pltpu.roll(packed, LANES - 2 * heads, 1)
        )
    top = functools.reduce(jnp.maximum, levels)
    shares = [jnp.exp(level - top) for level in levels]
    total = functools.reduce(jnp.add, shares)
    shares = [share / total for share in shares]
    for tile in range(tiles):
        lanes = slice(tile * LANES, (tile + 1) * LANES)
        joined = jnp.zeros((draft, LANES), F32)
        for part, share in enumerate(shares):
            factor = jnp.zeros((draft, LANES), F32)
            for head in range(heads):
                first, last = head_lanes(head, tile, head_size)
                if first < last:
                    factor = jnp.where(
                        lane_mask((draft, LANES), first, last), share[:, head : head + 1], factor
                    )
            if part == 0:
                value = own_ref[:, lanes]
            else:
                value = parts_ref[part - 1, tile * draft : (tile + 1) * draft].astype(F32)
            joined += factor * value
        joined = joined.astype(BF16)
        for target in range(out_ref.shape[0]):
            out_ref[target, :, lanes] = joined


def merge_parts(parts, own, level, heads, targets):
    draft, width = own.shape
    vmem = pl.BlockSpec(memory_space=pltpu.VMEM)
    return pl.pallas_call(
        functools.partial(merge_kernel, heads=heads, head_size=width // heads),
        out_shape=jax.ShapeDtypeStruct((targets, draft, width), BF16),
        in_specs=[vmem, vmem, vmem],
        out_specs=vmem,
    )(parts, own, level)


def packed_sums(value, lanes):
    lane = lax.broadcasted_iota(jnp.int32, (value.shape[0], lanes), 1)
    packed = jnp.zeros((value.shape[0], lanes), F32)
    for place, term in enumerate(split_three(value)):
        packed = jnp.where(lane == place, term, packed)
    return packed.astype(BF16)


def project_kernel(rows_ref, weight_ref, parts_ref, out_ref):
    blocks, columns, _ = weight_ref.shape
    targets, held, lanes = out_ref.shape
    req, draft, width = rows_ref.shape
    mp = targets // req
    pair = held // draft
    rows = rows_ref[...].reshape(req * draft, width)
    products = []
    for block in range(blocks):
        product = lax.dot_general(
            rows, weight_ref[block], (((1,), (1,)), ((), ())), preferred_element_type=F32
        )
        looked_up = parts_ref[block, parts_ref.shape[1] - columns :].astype(F32)
        products.append(product + jnp.transpose(looked_up))
    sums = packed_sums(
        jnp.sum(functools.reduce(jnp.add, products), axis=1, keepdims=True), lanes - columns
    )
    for block, product in enumerate(products):
        product = jnp.concatenate([product.astype(BF16), sums], axis=1)
        piece, half = divmod(block, pair)
        for target in range(req):
            out_ref[target * mp + piece, half * draft : (half + 1) * draft] = product[
                target * draft : (target + 1) * draft
            ]


def project_rows(rows, weight, parts, mp):
    req, draft, _ = rows.shape
    blocks, columns, _ = weight.shape
    lanes = -(-(columns + 3) // LANES) * LANES
    vmem = pl.BlockSpec(memory_space=pltpu.VMEM)
    return pl.pallas_call(
        project_kernel,
        out_shape=jax.ShapeDtypeStruct((req * mp, blocks // mp * draft, lanes), BF16),
        in_specs=[vmem, vmem, vmem],
        out_specs=vmem,
    )(rows, weight, parts)


def residual_kernel(parts_ref, gain_ref, out_ref, centred_ref, *, mp, columns):
    sources, held, _ = parts_ref.shape
    draft, width = out_ref.shape
    blocks = []
    for half in range(held // draft):
        lines = slice(half * draft, (half + 1) * draft)
        for source in range(sources // mp):
            block = parts_ref[source * mp, lines].astype(F32)
            for piece in range(1, mp):
                block += parts_ref[source * mp + piece, lines].astype(F32)
            blocks.append(block)
    residual = jnp.concatenate([block[:, :columns] for block in blocks], axis=1)
    out_ref[...] = residual
    sums = functools.reduce(jnp.add, blocks[: sources // mp])
    mean = sum(sums[:, columns + term : columns + term + 1] for term in range(3)) / (mp * width)
    centred = residual - mean
    squares = packed_sums(jnp.sum(centred * centred, axis=1, keepdims=True), LANES)
    scaled = (centred * gain_ref[...]).astype(BF16)
    for target in range(centred_ref.shape[0]):
        centred_ref[target, :, :width] = scaled
        centred_ref[target, :, width:] = squares


def residual_rows(parts, gain, mp, draft, columns, targets):
    vmem = pl.BlockSpec(memory_space=pltpu.VMEM)
    width = gain.shape[0]
    return pl.pallas_call(
        functools.partial(residual_kernel, mp=mp, columns=columns),
        out_shape=(
            jax.ShapeDtypeStruct((draft, width), F32),
            jax.ShapeDtypeStruct((targets, draft, width + LANES), BF16),
        ),
        in_specs=[vmem, vmem],
        out_specs=(vmem, vmem),
    )(parts, gain[None, :])


def lift_kernel(rows_ref, weight_ref, out_ref):
    blocks, hidden, width = weight_ref.shape
    mp, height, _ = out_ref.shape
    pair = blocks // mp
    rows = rows_ref[:, :width]
    for block in range(blocks):
        piece, place = divmod(block, pair)
        out_ref[piece, place * hidden : (place + 1) * hidden] = lax.dot_general(
            weight_ref[block], rows, (((1,), (1,)), ((), ())), preferred_element_type=F32
        ).astype(BF16)
    squares = jnp.transpose(rows_ref[:, width:].astype(F32)).astype(BF16)
    for piece in range(mp):
        out_ref[piece, pair * hidden :] = squares[: height - pair * hidden]


def lift_rows(rows, weight, mp):
    blocks, hidden, _ = weight.shape
    vmem = pl.BlockSpec(memory_space=pltpu.VMEM)
    return pl.pallas_call(
        lift_kernel,
        out_shape=jax.ShapeDtypeStruct((mp, blocks // mp * hidden + 16, rows.shape[0]), BF16),
        in_specs=[vmem, vmem],
        out_specs=vmem,
        compiler_params=pltpu.CompilerParams(vmem_limit_bytes=20 * MIB),
    )(rows, weight)


def gelu_kernel(parts_ref, out_ref, *, model_width):
    hidden = out_ref.shape[1]
    total = parts_ref[0].astype(F32)
    for piece in range(1, parts_ref.shape[0]):
        total += parts_ref[piece].astype(F32)
    squares = sum(total[hidden + term : hidden + term + 1] for term in range(3))
    lifted = total[:hidden] * lax.rsqrt(squares / model_width + 1e-05)
    activated = (0.5 * lifted * (1.0 + lax.erf(lifted * math.sqrt(0.5)))).astype(BF16)
    for target in range(out_ref.shape[0]):
        out_ref[target] = activated


def activate(parts, hidden, model_width):
    vmem = pl.BlockSpec(memory_space=pltpu.VMEM)
    return pl.pallas_call(
        functools.partial(gelu_kernel, model_width=model_width),
        out_shape=jax.ShapeDtypeStruct((parts.shape[0], hidden, parts.shape[2]), BF16),
        in_specs=[vmem],
        out_specs=vmem,
    )(parts)


def lower_kernel(hidden_ref, weight_ref, out_ref):
    blocks, features, _ = weight_ref.shape
    pair = blocks // hidden_ref.shape[0]
    total = None
    for block in range(blocks):
        piece, place = divmod(block, pair)
        product = lax.dot_general(
            hidden_ref[piece, place * features : (place + 1) * features],
            weight_ref[block],
            (((0,), (0,)), ((), ())),
            preferred_element_type=F32,
        )
        total = product if total is None else total + product
    out_ref[...] = total.astype(BF16).reshape(out_ref.shape)


def lower_rows(hidden, weight, targets):
    vmem = pl.BlockSpec(memory_space=pltpu.VMEM)
    return pl.pallas_call(
        lower_kernel,
        out_shape=jax.ShapeDtypeStruct((targets, hidden.shape[2] // targets, weight.shape[2]), BF16),
        in_specs=[vmem, vmem],
        out_specs=vmem,
        compiler_params=pltpu.CompilerParams(vmem_limit_bytes=20 * MIB),
    )(hidden, weight)


def finish_kernel(parts_ref, residual_ref, out_ref):
    total = parts_ref[0].astype(F32)
    for piece in range(1, parts_ref.shape[0]):
        total += parts_ref[piece].astype(F32)
    out_ref[...] = residual_ref[...] + total


def finish(parts, residual):
    vmem = pl.BlockSpec(memory_space=pltpu.VMEM)
    return pl.pallas_call(
        finish_kernel,
        out_shape=jax.ShapeDtypeStruct(residual.shape, F32),
        in_specs=[vmem, vmem],
        out_specs=vmem,
    )(parts, residual)


def after(value, earlier):
    return lax.optimization_barrier((value, earlier))[0]


def exchange(value, axis):
    return lax.all_to_all(value, axis, split_axis=0, concat_axis=0, tiled=True)


def per_device(
    token_ids,
    embed_table,
    queries,
    draft_kv,
    prefix_kv,
    suffix_kv,
    suffix_len,
    slopes,
    out_weight,
    ln_gain,
    up_weight,
    down_weight,
):
    heads = slopes.shape[0]
    _, draft, width = queries.shape
    prompt_local = prefix_kv.shape[1]
    ctx_count = lax.axis_size("ctx")
    req_count = lax.axis_size("req")
    mp_count = lax.axis_size("mp")
    ctx_index = lax.axis_index("ctx")
    model_index = lax.axis_index("mp")
    quarter = ln_gain.shape[0]

    copies = jnp.broadcast_to(queries, (ctx_count, draft, width))
    gathered = exchange(copies, "ctx")
    out_all = lax.all_gather(out_weight.T, "ctx")
    up_all = lax.all_gather(after(up_weight, copies).T, "ctx")
    down_all = lax.all_gather(after(down_weight, copies), "ctx")

    vocab_local = embed_table.shape[0]
    shifted = token_ids.reshape(-1) - model_index * vocab_local
    one_hot = (
        shifted[:, None] == jnp.arange(vocab_local, dtype=jnp.int32)[None, :]
    ).astype(BF16)
    looked_up = jnp.dot(one_hot, embed_table, preferred_element_type=F32).astype(BF16)
    gathered, looked_up = lax.optimization_barrier((gathered, looked_up))

    offset = (prompt_local * (ctx_count - ctx_index)).astype(jnp.int32).reshape(1)
    parts = prompt_part(
        gathered.reshape(ctx_count * draft, width),
        prefix_kv,
        slopes,
        offset,
        looked_up.T,
        ctx_count,
    )
    own, own_level = own_part(
        after(queries[0], parts), suffix_kv[:, 0], draft_kv[:, 0], slopes, suffix_len
    )
    parts = exchange(parts, "ctx")
    attended = exchange(merge_parts(parts, own, own_level, heads, req_count), "req")

    pieces = exchange(project_rows(attended, out_all, parts, mp_count), ("req", "mp"))
    residual, centred = residual_rows(
        pieces, ln_gain, mp_count, draft, out_weight.shape[1], req_count
    )
    centred, up_all = lax.optimization_barrier((centred, up_all))
    centred = exchange(centred, "req").reshape(req_count * draft, -1)

    lifted = exchange(lift_rows(centred, up_all, mp_count), "mp")
    activated, down_all = lax.optimization_barrier(
        (
            activate(lifted, ctx_count // mp_count * up_weight.shape[1], quarter * mp_count),
            down_all,
        )
    )
    activated = exchange(activated, "mp")
    lowered = exchange(lower_rows(activated, down_all, req_count), "req")
    layer_out = finish(lowered, residual)
    return residual[None], layer_out[None]


def solution(mesh):
    rows = ("ctx", "req")
    in_specs = (
        P(),
        P("mp", rows),
        P(rows, None, "mp"),
        P(None, rows, None, "mp"),
        P(None, "ctx", "mp"),
        P(None, rows, None, "mp"),
        P(rows),
        P("mp"),
        P("mp", rows),
        P("mp"),
        P("mp", rows),
        P(rows, "mp"),
    )
    out_specs = (P(rows, None, "mp"), P(rows, None, "mp"))
    return jax.shard_map(
        per_device, mesh=mesh, in_specs=in_specs, out_specs=out_specs, check_vma=False
    )
```

```python
import functools
import math

import jax
import jax.numpy as jnp
from jax import lax
from jax.experimental import pallas as pl
from jax.experimental.pallas import tpu as pltpu
from jax.sharding import PartitionSpec as P

LANES = 128
F32 = jnp.float32
BF16 = jnp.bfloat16
MIB = 1024 * 1024


def head_lanes(head, tile, head_size):
    first = max(head * head_size - tile * LANES, 0)
    last = min((head + 1) * head_size - tile * LANES, LANES)
    return first, last


def head_tiles(head, head_size):
    return range(head * head_size // LANES, ((head + 1) * head_size - 1) // LANES + 1)


def lane_mask(shape, first, last):
    lane = lax.broadcasted_iota(jnp.int32, shape, len(shape) - 1)
    return (lane >= first) & (lane < last)


def split_three(value):
    high = value.astype(BF16).astype(F32)
    rest = value - high
    middle = rest.astype(BF16).astype(F32)
    low = rest - middle
    return high, middle, low


def prompt_kernel(
    offset_ref, slopes_ref, query_ref, looked_ref, prefix_ref, out_ref, *, heads, head_size
):
    rows, width = query_ref.shape
    keys = prefix_ref.shape[1]
    tiles = width // LANES
    scale = 1.0 / math.sqrt(head_size)
    position = (
        lax.broadcasted_iota(jnp.int32, (1, keys), 1) - offset_ref[0]
    ).astype(F32)
    parts = [jnp.zeros((rows, LANES), F32) for _ in range(tiles)]
    stats = jnp.zeros((rows, LANES), F32)
    stat_lane = lax.broadcasted_iota(jnp.int32, (rows, LANES), 1)
    for head in range(heads):
        span = head_tiles(head, head_size)
        window = slice(span[0] * LANES, (span[-1] + 1) * LANES)
        query_window = jnp.concatenate(
            [
                jnp.where(
                    lane_mask((rows, LANES), *head_lanes(head, tile, head_size)),
                    query_ref[:, tile * LANES : (tile + 1) * LANES],
                    jnp.zeros((rows, LANES), BF16),
                )
                for tile in span
            ],
            axis=1,
        )
        scores = lax.dot_general(
            query_window,
            prefix_ref[0, :, window],
            (((1,), (1,)), ((), ())),
            preferred_element_type=F32,
        )
        scores = scores * scale + slopes_ref[head] * position
        top = jnp.max(scores, axis=1, keepdims=True)
        weights = jnp.exp(scores - top)
        total = jnp.sum(weights, axis=1, keepdims=True)
        sums = jnp.dot(
            weights.astype(BF16), prefix_ref[1, :, window], preferred_element_type=F32
        )
        sums = sums * (1.0 / total)
        for place, tile in enumerate(span):
            parts[tile] = jnp.where(
                lane_mask((rows, LANES), *head_lanes(head, tile, head_size)),
                sums[:, place * LANES : (place + 1) * LANES],
                parts[tile],
            )
        stats = jnp.where(stat_lane % heads == head, top + jnp.log(total), stats)
    high, middle, low = split_three(stats)
    group = stat_lane // heads
    packed = jnp.where(
        group == 0, high, jnp.where(group == 1, middle, jnp.where(group == 2, low, 0.0))
    )
    targets = out_ref.shape[0]
    draft = rows // targets
    for tile, value in enumerate([*parts, packed]):
        value = value.astype(BF16)
        for target in range(targets):
            out_ref[target, tile * draft : (tile + 1) * draft] = value[
                target * draft : (target + 1) * draft
            ]
    for target in range(targets):
        out_ref[target, (tiles + 1) * draft :] = looked_ref[
            :, target * LANES : (target + 1) * LANES
        ]


def prompt_part(query_rows, prefix_kv, slopes, offset, looked_up, targets):
    rows, width = query_rows.shape
    heads = slopes.shape[0]
    tiles = width // LANES
    return pl.pallas_call(
        functools.partial(prompt_kernel, heads=heads, head_size=width // heads),
        out_shape=jax.ShapeDtypeStruct(
            (targets, (tiles + 1) * (rows // targets) + looked_up.shape[0], LANES), BF16
        ),
        in_specs=[
            pl.BlockSpec(memory_space=pltpu.SMEM),
            pl.BlockSpec(memory_space=pltpu.SMEM),
            pl.BlockSpec(memory_space=pltpu.VMEM),
            pl.BlockSpec(memory_space=pltpu.VMEM),
            pl.BlockSpec(memory_space=pltpu.VMEM),
        ],
        out_specs=pl.BlockSpec(memory_space=pltpu.VMEM),
        compiler_params=pltpu.CompilerParams(vmem_limit_bytes=20 * MIB),
    )(offset, slopes, query_rows, looked_up, prefix_kv)


def lookup_kernel(ids_ref, table_ref, out_ref):
    count = ids_ref.shape[1]
    features, vocab = table_ref.shape
    step = math.gcd(vocab, 2 * LANES)
    ids = ids_ref[...]
    place = lax.broadcasted_iota(jnp.int32, (step, count), 0)
    total = jnp.zeros((features, count), F32)
    for first in range(0, vocab, step):
        chosen = jnp.where(place == ids - first, 1.0, 0.0).astype(BF16)
        total += jnp.dot(table_ref[:, first : first + step], chosen, preferred_element_type=F32)
    out_ref[...] = total.astype(BF16)


def look_up(ids, table):
    vmem = pl.BlockSpec(memory_space=pltpu.VMEM)
    return pl.pallas_call(
        lookup_kernel,
        out_shape=jax.ShapeDtypeStruct((table.shape[0], ids.shape[1]), BF16),
        in_specs=[vmem, vmem],
        out_specs=vmem,
        compiler_params=pltpu.CompilerParams(vmem_limit_bytes=12 * MIB),
    )(ids, table)


def own_kernel(
    length_ref, slopes_ref, query_ref, suffix_ref, draft_ref, out_ref, stats_ref, *, heads, head_size
):
    draft, width = query_ref.shape
    slots = suffix_ref.shape[1]
    rows = heads * draft
    query = query_ref[...]
    masks = [
        lane_mask((draft, width), head * head_size, (head + 1) * head_size)
        for head in range(heads)
    ]
    spread = jnp.concatenate(
        [jnp.where(mask, query, jnp.zeros_like(query)) for mask in masks], axis=0
    )
    row = lax.broadcasted_iota(jnp.int32, (rows, 1), 0)
    slope = jnp.zeros((rows, 1), F32)
    for head in range(heads):
        slope = jnp.where(row // draft == head, slopes_ref[head], slope)
    scale = 1.0 / math.sqrt(head_size)
    length = length_ref[0]
    contract = (((1,), (1,)), ((), ()))
    slot = lax.broadcasted_iota(jnp.int32, (rows, slots), 1)
    suffix_scores = lax.dot_general(spread, suffix_ref[0], contract, preferred_element_type=F32)
    suffix_scores = suffix_scores * scale + slope * slot.astype(F32)
    suffix_scores = jnp.where(slot < length, suffix_scores, -jnp.inf)
    place = lax.broadcasted_iota(jnp.int32, (rows, draft), 1)
    draft_scores = lax.dot_general(spread, draft_ref[0], contract, preferred_element_type=F32)
    draft_scores = draft_scores * scale + slope * (place + length).astype(F32)
    token = lax.broadcasted_iota(jnp.int32, (rows, draft), 0) % draft
    draft_scores = jnp.where(place <= token, draft_scores, -jnp.inf)
    top = jnp.maximum(
        jnp.max(suffix_scores, axis=1, keepdims=True), jnp.max(draft_scores, axis=1, keepdims=True)
    )
    suffix_weights = jnp.exp(suffix_scores - top)
    draft_weights = jnp.exp(draft_scores - top)
    total = jnp.sum(suffix_weights, axis=1, keepdims=True) + jnp.sum(
        draft_weights, axis=1, keepdims=True
    )
    sums = jnp.dot(suffix_weights.astype(BF16), suffix_ref[1], preferred_element_type=F32)
    sums += jnp.dot(draft_weights.astype(BF16), draft_ref[1], preferred_element_type=F32)
    sums = sums * (1.0 / total)
    level = top + jnp.log(total)
    result = jnp.zeros((draft, width), F32)
    stats = jnp.zeros((draft, LANES), F32)
    lane = lax.broadcasted_iota(jnp.int32, (draft, LANES), 1)
    for head in range(heads):
        rows_of = slice(head * draft, (head + 1) * draft)
        result = jnp.where(masks[head], sums[rows_of], result)
        stats = jnp.where(lane == head, level[rows_of], stats)
    out_ref[...] = result
    stats_ref[...] = stats


def own_part(query_rows, suffix_kv, draft_kv, slopes, length):
    draft, width = query_rows.shape
    heads = slopes.shape[0]
    vmem = pl.BlockSpec(memory_space=pltpu.VMEM)
    smem = pl.BlockSpec(memory_space=pltpu.SMEM)
    return pl.pallas_call(
        functools.partial(own_kernel, heads=heads, head_size=width // heads),
        out_shape=(
            jax.ShapeDtypeStruct((draft, width), F32),
            jax.ShapeDtypeStruct((draft, LANES), F32),
        ),
        in_specs=[smem, smem, vmem, vmem, vmem],
        out_specs=(vmem, vmem),
        compiler_params=pltpu.CompilerParams(vmem_limit_bytes=12 * MIB),
    )(length, slopes, query_rows, suffix_kv, draft_kv)


def merge_kernel(parts_ref, own_ref, level_ref, out_ref, *, heads, head_size):
    count = parts_ref.shape[0]
    draft, width = own_ref.shape
    tiles = width // LANES
    levels = [level_ref[...]]
    for part in range(count):
        packed = parts_ref[part, tiles * draft : (tiles + 1) * draft].astype(F32)
        levels.append(
            packed
            + pltpu.roll(packed, LANES - heads, 1)
            + pltpu.roll(packed, LANES - 2 * heads, 1)
        )
    top = functools.reduce(jnp.maximum, levels)
    shares = [jnp.exp(level - top) for level in levels]
    total = functools.reduce(jnp.add, shares)
    shares = [share / total for share in shares]
    for tile in range(tiles):
        lanes = slice(tile * LANES, (tile + 1) * LANES)
        joined = jnp.zeros((draft, LANES), F32)
        for part, share in enumerate(shares):
            factor = jnp.zeros((draft, LANES), F32)
            for head in range(heads):
                first, last = head_lanes(head, tile, head_size)
                if first < last:
                    factor = jnp.where(
                        lane_mask((draft, LANES), first, last), share[:, head : head + 1], factor
                    )
            if part == 0:
                value = own_ref[:, lanes]
            else:
                value = parts_ref[part - 1, tile * draft : (tile + 1) * draft].astype(F32)
            joined += factor * value
        joined = joined.astype(BF16)
        for target in range(out_ref.shape[0]):
            out_ref[target, :, lanes] = joined


def merge_parts(parts, own, level, heads, targets):
    draft, width = own.shape
    vmem = pl.BlockSpec(memory_space=pltpu.VMEM)
    return pl.pallas_call(
        functools.partial(merge_kernel, heads=heads, head_size=width // heads),
        out_shape=jax.ShapeDtypeStruct((targets, draft, width), BF16),
        in_specs=[vmem, vmem, vmem],
        out_specs=vmem,
        compiler_params=pltpu.CompilerParams(vmem_limit_bytes=10 * MIB),
    )(parts, own, level)


def packed_sums(value, lanes):
    lane = lax.broadcasted_iota(jnp.int32, (value.shape[0], lanes), 1)
    packed = jnp.zeros((value.shape[0], lanes), F32)
    for place, term in enumerate(split_three(value)):
        packed = jnp.where(lane == place, term, packed)
    return packed.astype(BF16)


def project_kernel(rows_ref, weight_ref, parts_ref, out_ref):
    blocks, columns, _ = weight_ref.shape
    targets, held, lanes = out_ref.shape
    req, draft, width = rows_ref.shape
    mp = targets // req
    pair = held // draft
    rows = rows_ref[...].reshape(req * draft, width)
    products = []
    for block in range(blocks):
        product = lax.dot_general(
            rows, weight_ref[block], (((1,), (1,)), ((), ())), preferred_element_type=F32
        )
        looked_up = parts_ref[block, parts_ref.shape[1] - columns :].astype(F32)
        products.append(product + jnp.transpose(looked_up))
    sums = packed_sums(
        jnp.sum(functools.reduce(jnp.add, products), axis=1, keepdims=True), lanes - columns
    )
    for block, product in enumerate(products):
        product = jnp.concatenate([product.astype(BF16), sums], axis=1)
        piece, half = divmod(block, pair)
        for target in range(req):
            out_ref[target * mp + piece, half * draft : (half + 1) * draft] = product[
                target * draft : (target + 1) * draft
            ]


def project_rows(rows, weight, parts, mp):
    req, draft, _ = rows.shape
    blocks, columns, _ = weight.shape
    lanes = -(-(columns + 3) // LANES) * LANES
    vmem = pl.BlockSpec(memory_space=pltpu.VMEM)
    return pl.pallas_call(
        project_kernel,
        out_shape=jax.ShapeDtypeStruct((req * mp, blocks // mp * draft, lanes), BF16),
        in_specs=[vmem, vmem, vmem],
        out_specs=vmem,
        compiler_params=pltpu.CompilerParams(vmem_limit_bytes=10 * MIB),
    )(rows, weight, parts)


def residual_kernel(parts_ref, gain_ref, out_ref, centred_ref, *, mp, columns):
    sources, held, _ = parts_ref.shape
    draft, width = out_ref.shape
    blocks = []
    for half in range(held // draft):
        lines = slice(half * draft, (half + 1) * draft)
        for source in range(sources // mp):
            block = parts_ref[source * mp, lines].astype(F32)
            for piece in range(1, mp):
                block += parts_ref[source * mp + piece, lines].astype(F32)
            blocks.append(block)
    residual = jnp.concatenate([block[:, :columns] for block in blocks], axis=1)
    out_ref[...] = residual
    sums = functools.reduce(jnp.add, blocks[: sources // mp])
    mean = sum(sums[:, columns + term : columns + term + 1] for term in range(3)) / (mp * width)
    centred = residual - mean
    squares = packed_sums(jnp.sum(centred * centred, axis=1, keepdims=True), LANES)
    scaled = (centred * gain_ref[...]).astype(BF16)
    for target in range(centred_ref.shape[0]):
        centred_ref[target, :, :width] = scaled
        centred_ref[target, :, width:] = squares


def residual_rows(parts, gain, mp, draft, columns, targets):
    vmem = pl.BlockSpec(memory_space=pltpu.VMEM)
    width = gain.shape[0]
    return pl.pallas_call(
        functools.partial(residual_kernel, mp=mp, columns=columns),
        out_shape=(
            jax.ShapeDtypeStruct((draft, width), F32),
            jax.ShapeDtypeStruct((targets, draft, width + LANES), BF16),
        ),
        in_specs=[vmem, vmem],
        out_specs=(vmem, vmem),
        compiler_params=pltpu.CompilerParams(vmem_limit_bytes=10 * MIB),
    )(parts, gain[None, :])


def lift_kernel(rows_ref, weight_ref, out_ref, *, hidden):
    blocks, _, width = weight_ref.shape
    mp, height, _ = out_ref.shape
    pair = blocks // mp
    rows = rows_ref[:, :width]
    for block in range(blocks):
        piece, place = divmod(block, pair)
        out_ref[piece, place * hidden : (place + 1) * hidden] = lax.dot_general(
            weight_ref[block, weight_ref.shape[1] - hidden :],
            rows,
            (((1,), (1,)), ((), ())),
            preferred_element_type=F32,
        ).astype(BF16)
    squares = jnp.transpose(rows_ref[:, width:].astype(F32)).astype(BF16)
    for piece in range(mp):
        out_ref[piece, pair * hidden :] = squares[: height - pair * hidden]


def lift_rows(rows, weight, hidden, mp):
    blocks = weight.shape[0]
    vmem = pl.BlockSpec(memory_space=pltpu.VMEM)
    return pl.pallas_call(
        functools.partial(lift_kernel, hidden=hidden),
        out_shape=jax.ShapeDtypeStruct((mp, blocks // mp * hidden + 16, rows.shape[0]), BF16),
        in_specs=[vmem, vmem],
        out_specs=vmem,
        compiler_params=pltpu.CompilerParams(vmem_limit_bytes=20 * MIB),
    )(rows, weight)


def gelu_kernel(parts_ref, out_ref, *, model_width):
    hidden = out_ref.shape[1]
    total = parts_ref[0].astype(F32)
    for piece in range(1, parts_ref.shape[0]):
        total += parts_ref[piece].astype(F32)
    squares = sum(total[hidden + term : hidden + term + 1] for term in range(3))
    lifted = total[:hidden] * lax.rsqrt(squares / model_width + 1e-05)
    activated = (0.5 * lifted * (1.0 + lax.erf(lifted * math.sqrt(0.5)))).astype(BF16)
    for target in range(out_ref.shape[0]):
        out_ref[target] = activated


def activate(parts, hidden, model_width):
    vmem = pl.BlockSpec(memory_space=pltpu.VMEM)
    return pl.pallas_call(
        functools.partial(gelu_kernel, model_width=model_width),
        out_shape=jax.ShapeDtypeStruct((parts.shape[0], hidden, parts.shape[2]), BF16),
        in_specs=[vmem],
        out_specs=vmem,
        compiler_params=pltpu.CompilerParams(vmem_limit_bytes=10 * MIB),
    )(parts)


def lower_kernel(hidden_ref, weight_ref, out_ref):
    blocks, features, _ = weight_ref.shape
    pair = blocks // hidden_ref.shape[0]
    total = None
    for block in range(blocks):
        piece, place = divmod(block, pair)
        product = lax.dot_general(
            hidden_ref[piece, place * features : (place + 1) * features],
            weight_ref[block],
            (((0,), (0,)), ((), ())),
            preferred_element_type=F32,
        )
        total = product if total is None else total + product
    out_ref[...] = total.astype(BF16).reshape(out_ref.shape)


def lower_rows(hidden, weight, targets):
    vmem = pl.BlockSpec(memory_space=pltpu.VMEM)
    return pl.pallas_call(
        lower_kernel,
        out_shape=jax.ShapeDtypeStruct((targets, hidden.shape[2] // targets, weight.shape[2]), BF16),
        in_specs=[vmem, vmem],
        out_specs=vmem,
        compiler_params=pltpu.CompilerParams(vmem_limit_bytes=20 * MIB),
    )(hidden, weight)


def finish_kernel(parts_ref, residual_ref, out_ref):
    total = parts_ref[0].astype(F32)
    for piece in range(1, parts_ref.shape[0]):
        total += parts_ref[piece].astype(F32)
    out_ref[...] = residual_ref[...] + total


def finish(parts, residual):
    vmem = pl.BlockSpec(memory_space=pltpu.VMEM)
    return pl.pallas_call(
        finish_kernel,
        out_shape=jax.ShapeDtypeStruct(residual.shape, F32),
        in_specs=[vmem, vmem],
        out_specs=vmem,
        compiler_params=pltpu.CompilerParams(vmem_limit_bytes=10 * MIB),
    )(parts, residual)


def after(value, earlier):
    return lax.optimization_barrier((value, earlier))[0]


def exchange(value, axis):
    return lax.all_to_all(value, axis, split_axis=0, concat_axis=0, tiled=True)


def per_device(
    token_ids,
    embed_table,
    queries,
    draft_kv,
    prefix_kv,
    suffix_kv,
    suffix_len,
    slopes,
    out_weight,
    ln_gain,
    up_weight,
    down_weight,
):
    heads = slopes.shape[0]
    _, draft, width = queries.shape
    prompt_local = prefix_kv.shape[1]
    ctx_count = lax.axis_size("ctx")
    req_count = lax.axis_size("req")
    mp_count = lax.axis_size("mp")
    ctx_index = lax.axis_index("ctx")
    model_index = lax.axis_index("mp")
    quarter = ln_gain.shape[0]

    copies = jnp.broadcast_to(queries, (ctx_count, draft, width))
    gathered = exchange(copies, "ctx")
    columns, hidden = out_weight.shape[1], up_weight.shape[1]
    upper = -(-columns // 32) * 16
    first, second = out_weight.T[:upper], out_weight.T[upper:]
    second = jnp.pad(second, ((0, 2 * upper - columns), (0, 0)))
    both = jnp.concatenate([jnp.concatenate([first, second], axis=1), up_weight.T], axis=0)
    both = lax.all_gather(both, "ctx")
    down_all = lax.all_gather(after(down_weight, copies), "ctx")

    vocab_local = embed_table.shape[0]
    shifted = token_ids.reshape(1, -1) - model_index * vocab_local
    looked_up = look_up(shifted, embed_table.T)
    gathered, looked_up = lax.optimization_barrier((gathered, looked_up))

    offset = (prompt_local * (ctx_count - ctx_index)).astype(jnp.int32).reshape(1)
    parts = prompt_part(
        gathered.reshape(ctx_count * draft, width),
        prefix_kv,
        slopes,
        offset,
        looked_up,
        ctx_count,
    )
    own, own_level = own_part(
        after(queries[0], parts), suffix_kv[:, 0], draft_kv[:, 0], slopes, suffix_len
    )
    parts = exchange(parts, "ctx")
    attended = exchange(merge_parts(parts, own, own_level, heads, req_count), "req")

    out_all = jnp.concatenate(
        [both[:, :upper, :width], both[:, : columns - upper, width:]], axis=1
    )
    pieces = exchange(project_rows(attended, out_all, parts, mp_count), ("req", "mp"))
    residual, centred = residual_rows(
        pieces, ln_gain, mp_count, draft, columns, req_count
    )
    centred = exchange(centred, "req").reshape(req_count * draft, -1)

    lifted = exchange(lift_rows(centred, both, hidden, mp_count), "mp")
    activated, down_all = lax.optimization_barrier(
        (
            activate(lifted, ctx_count // mp_count * hidden, quarter * mp_count),
            down_all,
        )
    )
    activated = exchange(activated, "mp")
    lowered = exchange(lower_rows(activated, down_all, req_count), "req")
    layer_out = finish(lowered, residual)
    return residual[None], layer_out[None]


def solution(mesh):
    rows = ("ctx", "req")
    in_specs = (
        P(),
        P("mp", rows),
        P(rows, None, "mp"),
        P(None, rows, None, "mp"),
        P(None, "ctx", "mp"),
        P(None, rows, None, "mp"),
        P(rows),
        P("mp"),
        P("mp", rows),
        P("mp"),
        P("mp", rows),
        P(rows, "mp"),
    )
    out_specs = (P(rows, None, "mp"), P(rows, None, "mp"))
    return jax.shard_map(
        per_device, mesh=mesh, in_specs=in_specs, out_specs=out_specs, check_vma=False
    )
```

```python
import functools
import math

import jax
import jax.numpy as jnp
from jax import lax
from jax.experimental import pallas as pl
from jax.experimental.pallas import tpu as pltpu
from jax.sharding import PartitionSpec as P

LANES = 128
F32 = jnp.float32
BF16 = jnp.bfloat16
MIB = 1024 * 1024


def head_lanes(head, tile, head_size):
    first = max(head * head_size - tile * LANES, 0)
    last = min((head + 1) * head_size - tile * LANES, LANES)
    return first, last


def head_tiles(head, head_size):
    return range(head * head_size // LANES, ((head + 1) * head_size - 1) // LANES + 1)


def lane_mask(shape, first, last):
    lane = lax.broadcasted_iota(jnp.int32, shape, len(shape) - 1)
    return (lane >= first) & (lane < last)


def split_three(value):
    high = value.astype(BF16).astype(F32)
    rest = value - high
    middle = rest.astype(BF16).astype(F32)
    low = rest - middle
    return high, middle, low


def prompt_kernel(
    offset_ref, slopes_ref, query_ref, looked_ref, prefix_ref, out_ref, *, heads, head_size
):
    rows, width = query_ref.shape
    keys = prefix_ref.shape[1]
    tiles = width // LANES
    scale = 1.0 / math.sqrt(head_size)
    position = (
        lax.broadcasted_iota(jnp.int32, (1, keys), 1) - offset_ref[0]
    ).astype(F32)
    parts = [jnp.zeros((rows, LANES), F32) for _ in range(tiles)]
    stats = jnp.zeros((rows, LANES), F32)
    stat_lane = lax.broadcasted_iota(jnp.int32, (rows, LANES), 1)
    for head in range(heads):
        span = head_tiles(head, head_size)
        window = slice(span[0] * LANES, (span[-1] + 1) * LANES)
        query_window = jnp.concatenate(
            [
                jnp.where(
                    lane_mask((rows, LANES), *head_lanes(head, tile, head_size)),
                    query_ref[:, tile * LANES : (tile + 1) * LANES],
                    jnp.zeros((rows, LANES), BF16),
                )
                for tile in span
            ],
            axis=1,
        )
        scores = lax.dot_general(
            query_window,
            prefix_ref[0, :, window],
            (((1,), (1,)), ((), ())),
            preferred_element_type=F32,
        )
        scores = scores * scale + slopes_ref[head] * position
        top = jnp.max(scores, axis=1, keepdims=True)
        weights = jnp.exp(scores - top)
        total = jnp.sum(weights, axis=1, keepdims=True)
        sums = jnp.dot(
            weights.astype(BF16), prefix_ref[1, :, window], preferred_element_type=F32
        )
        sums = sums * (1.0 / total)
        for place, tile in enumerate(span):
            parts[tile] = jnp.where(
                lane_mask((rows, LANES), *head_lanes(head, tile, head_size)),
                sums[:, place * LANES : (place + 1) * LANES],
                parts[tile],
            )
        stats = jnp.where(stat_lane % heads == head, top + jnp.log(total), stats)
    high, middle, low = split_three(stats)
    group = stat_lane // heads
    packed = jnp.where(
        group == 0, high, jnp.where(group == 1, middle, jnp.where(group == 2, low, 0.0))
    )
    targets = out_ref.shape[0]
    draft = rows // targets
    for tile, value in enumerate([*parts, packed]):
        value = value.astype(BF16)
        for target in range(targets):
            out_ref[target, tile * draft : (tile + 1) * draft] = value[
                target * draft : (target + 1) * draft
            ]
    for target in range(targets):
        out_ref[target, (tiles + 1) * draft :] = looked_ref[
            :, target * LANES : (target + 1) * LANES
        ]


def prompt_part(query_rows, prefix_kv, slopes, offset, looked_up, targets):
    rows, width = query_rows.shape
    heads = slopes.shape[0]
    tiles = width // LANES
    return pl.pallas_call(
        functools.partial(prompt_kernel, heads=heads, head_size=width // heads),
        out_shape=jax.ShapeDtypeStruct(
            (targets, (tiles + 1) * (rows // targets) + looked_up.shape[0], LANES), BF16
        ),
        in_specs=[
            pl.BlockSpec(memory_space=pltpu.SMEM),
            pl.BlockSpec(memory_space=pltpu.SMEM),
            pl.BlockSpec(memory_space=pltpu.VMEM),
            pl.BlockSpec(memory_space=pltpu.VMEM),
            pl.BlockSpec(memory_space=pltpu.VMEM),
        ],
        out_specs=pl.BlockSpec(memory_space=pltpu.VMEM),
        compiler_params=pltpu.CompilerParams(vmem_limit_bytes=20 * MIB),
    )(offset, slopes, query_rows, looked_up, prefix_kv)


def lookup_kernel(ids_ref, table_ref, out_ref):
    count = ids_ref.shape[1]
    features, vocab = table_ref.shape
    step = math.gcd(vocab, 2 * LANES)
    ids = ids_ref[...]
    place = lax.broadcasted_iota(jnp.int32, (step, count), 0)
    total = jnp.zeros((features, count), F32)
    for first in range(0, vocab, step):
        chosen = jnp.where(place == ids - first, 1.0, 0.0).astype(BF16)
        total += jnp.dot(table_ref[:, first : first + step], chosen, preferred_element_type=F32)
    out_ref[...] = total.astype(BF16)


def look_up(ids, table):
    vmem = pl.BlockSpec(memory_space=pltpu.VMEM)
    return pl.pallas_call(
        lookup_kernel,
        out_shape=jax.ShapeDtypeStruct((table.shape[0], ids.shape[1]), BF16),
        in_specs=[vmem, vmem],
        out_specs=vmem,
        compiler_params=pltpu.CompilerParams(vmem_limit_bytes=12 * MIB),
    )(ids, table)


def own_kernel(
    length_ref, slopes_ref, query_ref, suffix_ref, draft_ref, out_ref, stats_ref, *, heads, head_size
):
    draft, width = query_ref.shape
    slots = suffix_ref.shape[1]
    rows = heads * draft
    query = query_ref[...]
    masks = [
        lane_mask((draft, width), head * head_size, (head + 1) * head_size)
        for head in range(heads)
    ]
    spread = jnp.concatenate(
        [jnp.where(mask, query, jnp.zeros_like(query)) for mask in masks], axis=0
    )
    row = lax.broadcasted_iota(jnp.int32, (rows, 1), 0)
    slope = jnp.zeros((rows, 1), F32)
    for head in range(heads):
        slope = jnp.where(row // draft == head, slopes_ref[head], slope)
    scale = 1.0 / math.sqrt(head_size)
    length = length_ref[0]
    contract = (((1,), (1,)), ((), ()))
    slot = lax.broadcasted_iota(jnp.int32, (rows, slots), 1)
    suffix_scores = lax.dot_general(spread, suffix_ref[0], contract, preferred_element_type=F32)
    suffix_scores = suffix_scores * scale + slope * slot.astype(F32)
    suffix_scores = jnp.where(slot < length, suffix_scores, -jnp.inf)
    place = lax.broadcasted_iota(jnp.int32, (rows, draft), 1)
    draft_scores = lax.dot_general(spread, draft_ref[0], contract, preferred_element_type=F32)
    draft_scores = draft_scores * scale + slope * (place + length).astype(F32)
    token = lax.broadcasted_iota(jnp.int32, (rows, draft), 0) % draft
    draft_scores = jnp.where(place <= token, draft_scores, -jnp.inf)
    top = jnp.maximum(
        jnp.max(suffix_scores, axis=1, keepdims=True), jnp.max(draft_scores, axis=1, keepdims=True)
    )
    suffix_weights = jnp.exp(suffix_scores - top)
    draft_weights = jnp.exp(draft_scores - top)
    total = jnp.sum(suffix_weights, axis=1, keepdims=True) + jnp.sum(
        draft_weights, axis=1, keepdims=True
    )
    sums = jnp.dot(suffix_weights.astype(BF16), suffix_ref[1], preferred_element_type=F32)
    sums += jnp.dot(draft_weights.astype(BF16), draft_ref[1], preferred_element_type=F32)
    sums = sums * (1.0 / total)
    level = top + jnp.log(total)
    result = jnp.zeros((draft, width), F32)
    stats = jnp.zeros((draft, LANES), F32)
    lane = lax.broadcasted_iota(jnp.int32, (draft, LANES), 1)
    for head in range(heads):
        rows_of = slice(head * draft, (head + 1) * draft)
        result = jnp.where(masks[head], sums[rows_of], result)
        stats = jnp.where(lane == head, level[rows_of], stats)
    out_ref[...] = result
    stats_ref[...] = stats


def own_part(query_rows, suffix_kv, draft_kv, slopes, length):
    draft, width = query_rows.shape
    heads = slopes.shape[0]
    vmem = pl.BlockSpec(memory_space=pltpu.VMEM)
    smem = pl.BlockSpec(memory_space=pltpu.SMEM)
    return pl.pallas_call(
        functools.partial(own_kernel, heads=heads, head_size=width // heads),
        out_shape=(
            jax.ShapeDtypeStruct((draft, width), F32),
            jax.ShapeDtypeStruct((draft, LANES), F32),
        ),
        in_specs=[smem, smem, vmem, vmem, vmem],
        out_specs=(vmem, vmem),
        compiler_params=pltpu.CompilerParams(vmem_limit_bytes=12 * MIB),
    )(length, slopes, query_rows, suffix_kv, draft_kv)


def merge_kernel(parts_ref, own_ref, level_ref, out_ref, *, heads, head_size):
    count = parts_ref.shape[0]
    draft, width = own_ref.shape
    tiles = width // LANES
    levels = [level_ref[...]]
    for part in range(count):
        packed = parts_ref[part, tiles * draft : (tiles + 1) * draft].astype(F32)
        levels.append(
            packed
            + pltpu.roll(packed, LANES - heads, 1)
            + pltpu.roll(packed, LANES - 2 * heads, 1)
        )
    top = functools.reduce(jnp.maximum, levels)
    shares = [jnp.exp(level - top) for level in levels]
    total = functools.reduce(jnp.add, shares)
    shares = [share / total for share in shares]
    for tile in range(tiles):
        lanes = slice(tile * LANES, (tile + 1) * LANES)
        joined = jnp.zeros((draft, LANES), F32)
        for part, share in enumerate(shares):
            factor = jnp.zeros((draft, LANES), F32)
            for head in range(heads):
                first, last = head_lanes(head, tile, head_size)
                if first < last:
                    factor = jnp.where(
                        lane_mask((draft, LANES), first, last), share[:, head : head + 1], factor
                    )
            if part == 0:
                value = own_ref[:, lanes]
            else:
                value = parts_ref[part - 1, tile * draft : (tile + 1) * draft].astype(F32)
            joined += factor * value
        joined = joined.astype(BF16)
        for target in range(out_ref.shape[0]):
            out_ref[target, :, lanes] = joined


def merge_parts(parts, own, level, heads, targets):
    draft, width = own.shape
    vmem = pl.BlockSpec(memory_space=pltpu.VMEM)
    return pl.pallas_call(
        functools.partial(merge_kernel, heads=heads, head_size=width // heads),
        out_shape=jax.ShapeDtypeStruct((targets, draft, width), BF16),
        in_specs=[vmem, vmem, vmem],
        out_specs=vmem,
        compiler_params=pltpu.CompilerParams(vmem_limit_bytes=10 * MIB),
    )(parts, own, level)


def packed_sums(value, lanes):
    lane = lax.broadcasted_iota(jnp.int32, (value.shape[0], lanes), 1)
    packed = jnp.zeros((value.shape[0], lanes), F32)
    for place, term in enumerate(split_three(value)):
        packed = jnp.where(lane == place, term, packed)
    return packed.astype(BF16)


def project_kernel(ctx_ref, rows_ref, parts_ref, *refs, mp):
    *weight_refs, out_ref = refs
    columns = weight_refs[0].shape[0]
    blocks = len(weight_refs)
    _, pair, draft, lanes = out_ref.shape
    req, _, width = rows_ref.shape
    rows = rows_ref[...].reshape(req * draft, width)
    products = []
    for place, weight_ref in enumerate(weight_refs):
        beside, back = divmod(place, blocks // pair)
        block = lax.rem(ctx_ref[0] + blocks - pair * back, blocks) ^ beside
        product = lax.dot_general(
            rows, weight_ref[...], (((1,), (1,)), ((), ())), preferred_element_type=F32
        )
        looked_up = parts_ref[block, parts_ref.shape[1] - columns :].astype(F32)
        products.append((block, product + jnp.transpose(looked_up)))
    total = functools.reduce(jnp.add, [product for _, product in products])
    sums = packed_sums(jnp.sum(total, axis=1, keepdims=True), lanes - columns)
    for block, product in products:
        product = jnp.concatenate([product.astype(BF16), sums], axis=1)
        piece, half = lax.shift_right_logical(block, 1), block & 1
        for target in range(req):
            out_ref[target * mp + piece, half] = product[target * draft : (target + 1) * draft]


def project_rows(rows, weights, parts, ctx_index, mp):
    req, draft, _ = rows.shape
    columns = weights[0].shape[0]
    lanes = -(-(columns + 3) // LANES) * LANES
    vmem = pl.BlockSpec(memory_space=pltpu.VMEM)
    return pl.pallas_call(
        functools.partial(project_kernel, mp=mp),
        out_shape=jax.ShapeDtypeStruct((req * mp, len(weights) // mp, draft, lanes), BF16),
        in_specs=[pl.BlockSpec(memory_space=pltpu.SMEM)] + [vmem] * (2 + len(weights)),
        out_specs=vmem,
        compiler_params=pltpu.CompilerParams(vmem_limit_bytes=10 * MIB),
    )(ctx_index, rows, parts, *weights)


def residual_kernel(parts_ref, gain_ref, out_ref, centred_ref, *, mp, columns):
    sources, pair, _, _ = parts_ref.shape
    _, width = out_ref.shape
    blocks = []
    for half in range(pair):
        for source in range(sources // mp):
            block = parts_ref[source * mp, half].astype(F32)
            for piece in range(1, mp):
                block += parts_ref[source * mp + piece, half].astype(F32)
            blocks.append(block)
    residual = jnp.concatenate([block[:, :columns] for block in blocks], axis=1)
    out_ref[...] = residual
    sums = functools.reduce(jnp.add, blocks[: sources // mp])
    mean = sum(sums[:, columns + term : columns + term + 1] for term in range(3)) / (mp * width)
    centred = residual - mean
    squares = packed_sums(jnp.sum(centred * centred, axis=1, keepdims=True), LANES)
    scaled = (centred * gain_ref[...]).astype(BF16)
    for target in range(centred_ref.shape[0]):
        centred_ref[target, :, :width] = scaled
        centred_ref[target, :, width:] = squares


def residual_rows(parts, gain, mp, draft, columns, targets):
    vmem = pl.BlockSpec(memory_space=pltpu.VMEM)
    width = gain.shape[0]
    return pl.pallas_call(
        functools.partial(residual_kernel, mp=mp, columns=columns),
        out_shape=(
            jax.ShapeDtypeStruct((draft, width), F32),
            jax.ShapeDtypeStruct((targets, draft, width + LANES), BF16),
        ),
        in_specs=[vmem, vmem],
        out_specs=(vmem, vmem),
        compiler_params=pltpu.CompilerParams(vmem_limit_bytes=10 * MIB),
    )(parts, gain[None, :])


def lift_kernel(rows_ref, weight_ref, out_ref, *, hidden):
    blocks, _, width = weight_ref.shape
    mp, height, _ = out_ref.shape
    pair = blocks // mp
    rows = rows_ref[:, :width]
    for block in range(blocks):
        piece, place = divmod(block, pair)
        out_ref[piece, place * hidden : (place + 1) * hidden] = lax.dot_general(
            weight_ref[block, weight_ref.shape[1] - hidden :],
            rows,
            (((1,), (1,)), ((), ())),
            preferred_element_type=F32,
        ).astype(BF16)
    squares = jnp.transpose(rows_ref[:, width:].astype(F32)).astype(BF16)
    for piece in range(mp):
        out_ref[piece, pair * hidden :] = squares[: height - pair * hidden]


def lift_rows(rows, weight, hidden, mp):
    blocks = weight.shape[0]
    vmem = pl.BlockSpec(memory_space=pltpu.VMEM)
    return pl.pallas_call(
        functools.partial(lift_kernel, hidden=hidden),
        out_shape=jax.ShapeDtypeStruct((mp, blocks // mp * hidden + 16, rows.shape[0]), BF16),
        in_specs=[vmem, vmem],
        out_specs=vmem,
        compiler_params=pltpu.CompilerParams(vmem_limit_bytes=20 * MIB),
    )(rows, weight)


def gelu_kernel(parts_ref, out_ref, *, model_width):
    hidden = out_ref.shape[1]
    total = parts_ref[0].astype(F32)
    for piece in range(1, parts_ref.shape[0]):
        total += parts_ref[piece].astype(F32)
    squares = sum(total[hidden + term : hidden + term + 1] for term in range(3))
    lifted = total[:hidden] * lax.rsqrt(squares / model_width + 1e-05)
    activated = (0.5 * lifted * (1.0 + lax.erf(lifted * math.sqrt(0.5)))).astype(BF16)
    for target in range(out_ref.shape[0]):
        out_ref[target] = activated


def activate(parts, hidden, model_width):
    vmem = pl.BlockSpec(memory_space=pltpu.VMEM)
    return pl.pallas_call(
        functools.partial(gelu_kernel, model_width=model_width),
        out_shape=jax.ShapeDtypeStruct((parts.shape[0], hidden, parts.shape[2]), BF16),
        in_specs=[vmem],
        out_specs=vmem,
        compiler_params=pltpu.CompilerParams(vmem_limit_bytes=10 * MIB),
    )(parts)


def lower_kernel(hidden_ref, weight_ref, out_ref):
    blocks, features, _ = weight_ref.shape
    pair = blocks // hidden_ref.shape[0]
    total = None
    for block in range(blocks):
        piece, place = divmod(block, pair)
        product = lax.dot_general(
            hidden_ref[piece, place * features : (place + 1) * features],
            weight_ref[block],
            (((0,), (0,)), ((), ())),
            preferred_element_type=F32,
        )
        total = product if total is None else total + product
    out_ref[...] = total.astype(BF16).reshape(out_ref.shape)


def lower_rows(hidden, weight, targets):
    vmem = pl.BlockSpec(memory_space=pltpu.VMEM)
    return pl.pallas_call(
        lower_kernel,
        out_shape=jax.ShapeDtypeStruct((targets, hidden.shape[2] // targets, weight.shape[2]), BF16),
        in_specs=[vmem, vmem],
        out_specs=vmem,
        compiler_params=pltpu.CompilerParams(vmem_limit_bytes=20 * MIB),
    )(hidden, weight)


def finish_kernel(parts_ref, residual_ref, out_ref):
    total = parts_ref[0].astype(F32)
    for piece in range(1, parts_ref.shape[0]):
        total += parts_ref[piece].astype(F32)
    out_ref[...] = residual_ref[...] + total


def finish(parts, residual):
    vmem = pl.BlockSpec(memory_space=pltpu.VMEM)
    return pl.pallas_call(
        finish_kernel,
        out_shape=jax.ShapeDtypeStruct(residual.shape, F32),
        in_specs=[vmem, vmem],
        out_specs=vmem,
        compiler_params=pltpu.CompilerParams(vmem_limit_bytes=10 * MIB),
    )(parts, residual)


def after(value, earlier):
    return lax.optimization_barrier((value, earlier))[0]


def exchange(value, axis):
    return lax.all_to_all(value, axis, split_axis=0, concat_axis=0, tiled=True)


def per_device(
    token_ids,
    embed_table,
    queries,
    draft_kv,
    prefix_kv,
    suffix_kv,
    suffix_len,
    slopes,
    out_weight,
    ln_gain,
    up_weight,
    down_weight,
):
    heads = slopes.shape[0]
    _, draft, width = queries.shape
    prompt_local = prefix_kv.shape[1]
    ctx_count = lax.axis_size("ctx")
    req_count = lax.axis_size("req")
    mp_count = lax.axis_size("mp")
    ctx_index = lax.axis_index("ctx")
    model_index = lax.axis_index("mp")
    quarter = ln_gain.shape[0]

    copies = jnp.broadcast_to(queries, (ctx_count, draft, width))
    gathered = exchange(copies, "ctx")
    up_all = lax.all_gather(after(up_weight, copies).T, "ctx")
    down_all = lax.all_gather(after(down_weight, copies), "ctx")

    vocab_local = embed_table.shape[0]
    shifted = token_ids.reshape(1, -1) - model_index * vocab_local
    looked_up = look_up(shifted, embed_table.T)
    gathered, looked_up = lax.optimization_barrier((gathered, looked_up))

    out_blocks = [after(out_weight.T, looked_up)]
    out_blocks += [
        lax.ppermute(out_blocks[0], "ctx", [(i, (i + step) % ctx_count) for i in range(ctx_count)])
        for step in range(2, ctx_count, 2)
    ]

    offset = (prompt_local * (ctx_count - ctx_index)).astype(jnp.int32).reshape(1)
    parts = prompt_part(
        gathered.reshape(ctx_count * draft, width),
        prefix_kv,
        slopes,
        offset,
        looked_up,
        ctx_count,
    )
    own, own_level = own_part(
        after(queries[0], parts), suffix_kv[:, 0], draft_kv[:, 0], slopes, suffix_len
    )
    parts = exchange(parts, "ctx")
    out_blocks += [
        lax.ppermute(after(block, own), "ctx", [(i, i ^ 1) for i in range(ctx_count)])
        for block in out_blocks
    ]
    attended = exchange(merge_parts(parts, own, own_level, heads, req_count), "req")

    pieces = exchange(
        project_rows(
            attended, out_blocks, parts, ctx_index.astype(jnp.int32).reshape(1), mp_count
        ),
        ("req", "mp"),
    )
    residual, centred = residual_rows(
        pieces, ln_gain, mp_count, draft, out_weight.shape[1], req_count
    )
    centred = exchange(centred, "req").reshape(req_count * draft, -1)

    hidden = up_weight.shape[1]
    lifted = exchange(lift_rows(centred, up_all, hidden, mp_count), "mp")
    activated = activate(lifted, ctx_count // mp_count * hidden, quarter * mp_count)
    activated = exchange(activated, "mp")
    lowered = exchange(lower_rows(activated, down_all, req_count), "req")
    layer_out = finish(lowered, residual)
    return residual[None], layer_out[None]


def solution(mesh):
    rows = ("ctx", "req")
    in_specs = (
        P(),
        P("mp", rows),
        P(rows, None, "mp"),
        P(None, rows, None, "mp"),
        P(None, "ctx", "mp"),
        P(None, rows, None, "mp"),
        P(rows),
        P("mp"),
        P("mp", rows),
        P("mp"),
        P("mp", rows),
        P(rows, "mp"),
    )
    out_specs = (P(rows, None, "mp"), P(rows, None, "mp"))
    return jax.shard_map(
        per_device, mesh=mesh, in_specs=in_specs, out_specs=out_specs, check_vma=False
    )
```

```python
import functools
import math

import jax
import jax.numpy as jnp
from jax import lax
from jax.experimental import pallas as pl
from jax.experimental.pallas import tpu as pltpu
from jax.sharding import PartitionSpec as P

LANES = 128
F32 = jnp.float32
BF16 = jnp.bfloat16
MIB = 1024 * 1024


def head_lanes(head, tile, head_size):
    first = max(head * head_size - tile * LANES, 0)
    last = min((head + 1) * head_size - tile * LANES, LANES)
    return first, last


def head_tiles(head, head_size):
    return range(head * head_size // LANES, ((head + 1) * head_size - 1) // LANES + 1)


def lane_mask(shape, first, last):
    lane = lax.broadcasted_iota(jnp.int32, shape, len(shape) - 1)
    return (lane >= first) & (lane < last)


def split_three(value):
    high = value.astype(BF16).astype(F32)
    rest = value - high
    middle = rest.astype(BF16).astype(F32)
    low = rest - middle
    return high, middle, low


def prompt_kernel(
    offset_ref, slopes_ref, query_ref, looked_ref, prefix_ref, out_ref, *, heads, head_size
):
    rows, width = query_ref.shape
    keys = prefix_ref.shape[1]
    tiles = width // LANES
    scale = 1.0 / math.sqrt(head_size)
    position = (
        lax.broadcasted_iota(jnp.int32, (1, keys), 1) - offset_ref[0]
    ).astype(F32)
    parts = [jnp.zeros((rows, LANES), F32) for _ in range(tiles)]
    stats = jnp.zeros((rows, LANES), F32)
    stat_lane = lax.broadcasted_iota(jnp.int32, (rows, LANES), 1)
    for head in range(heads):
        span = head_tiles(head, head_size)
        window = slice(span[0] * LANES, (span[-1] + 1) * LANES)
        query_window = jnp.concatenate(
            [
                jnp.where(
                    lane_mask((rows, LANES), *head_lanes(head, tile, head_size)),
                    query_ref[:, tile * LANES : (tile + 1) * LANES],
                    jnp.zeros((rows, LANES), BF16),
                )
                for tile in span
            ],
            axis=1,
        )
        scores = lax.dot_general(
            query_window,
            prefix_ref[0, :, window],
            (((1,), (1,)), ((), ())),
            preferred_element_type=F32,
        )
        scores = scores * scale + slopes_ref[:, head : head + 1] * position
        top = jnp.max(scores, axis=1, keepdims=True)
        weights = jnp.exp(scores - top)
        total = jnp.sum(weights, axis=1, keepdims=True)
        sums = jnp.dot(
            weights.astype(BF16), prefix_ref[1, :, window], preferred_element_type=F32
        )
        sums = sums * (1.0 / total)
        for place, tile in enumerate(span):
            parts[tile] = jnp.where(
                lane_mask((rows, LANES), *head_lanes(head, tile, head_size)),
                sums[:, place * LANES : (place + 1) * LANES],
                parts[tile],
            )
        stats = jnp.where(stat_lane % heads == head, top + jnp.log(total), stats)
    high, middle, low = split_three(stats)
    group = stat_lane // heads
    packed = jnp.where(
        group == 0, high, jnp.where(group == 1, middle, jnp.where(group == 2, low, 0.0))
    )
    targets = out_ref.shape[0]
    draft = rows // targets
    for tile, value in enumerate([*parts, packed]):
        value = value.astype(BF16)
        for target in range(targets):
            out_ref[target, tile * draft : (tile + 1) * draft] = value[
                target * draft : (target + 1) * draft
            ]
    for target in range(targets):
        out_ref[target, (tiles + 1) * draft :] = looked_ref[
            :, target * LANES : (target + 1) * LANES
        ]


def prompt_part(query_rows, prefix_kv, slopes, offset, looked_up, targets):
    rows, width = query_rows.shape
    heads = slopes.shape[0]
    tiles = width // LANES
    return pl.pallas_call(
        functools.partial(prompt_kernel, heads=heads, head_size=width // heads),
        out_shape=jax.ShapeDtypeStruct(
            (targets, (tiles + 1) * (rows // targets) + looked_up.shape[0], LANES), BF16
        ),
        in_specs=[
            pl.BlockSpec(memory_space=pltpu.SMEM),
            pl.BlockSpec(memory_space=pltpu.VMEM),
            pl.BlockSpec(memory_space=pltpu.VMEM),
            pl.BlockSpec(memory_space=pltpu.VMEM),
            pl.BlockSpec(memory_space=pltpu.VMEM),
        ],
        out_specs=pl.BlockSpec(memory_space=pltpu.VMEM),
        compiler_params=pltpu.CompilerParams(vmem_limit_bytes=20 * MIB),
    )(offset, slopes[None, :], query_rows, looked_up, prefix_kv)


def lookup_kernel(ids_ref, table_ref, out_ref):
    count = ids_ref.shape[1]
    features, vocab = table_ref.shape
    step = math.gcd(vocab, 2 * LANES)
    ids = ids_ref[...]
    place = lax.broadcasted_iota(jnp.int32, (step, count), 0)
    total = jnp.zeros((features, count), F32)
    for first in range(0, vocab, step):
        chosen = jnp.where(place == ids - first, 1.0, 0.0).astype(BF16)
        total += jnp.dot(table_ref[:, first : first + step], chosen, preferred_element_type=F32)
    out_ref[...] = total.astype(BF16)


def look_up(ids, table):
    vmem = pl.BlockSpec(memory_space=pltpu.VMEM)
    return pl.pallas_call(
        lookup_kernel,
        out_shape=jax.ShapeDtypeStruct((table.shape[0], ids.shape[1]), BF16),
        in_specs=[vmem, vmem],
        out_specs=vmem,
        compiler_params=pltpu.CompilerParams(vmem_limit_bytes=12 * MIB),
    )(ids, table)


def own_kernel(
    length_ref, slopes_ref, query_ref, suffix_ref, draft_ref, out_ref, stats_ref, *, heads, head_size
):
    draft, width = query_ref.shape
    slots = suffix_ref.shape[1]
    rows = heads * draft
    query = query_ref[...]
    masks = [
        lane_mask((draft, width), head * head_size, (head + 1) * head_size)
        for head in range(heads)
    ]
    spread = jnp.concatenate(
        [jnp.where(mask, query, jnp.zeros_like(query)) for mask in masks], axis=0
    )
    row = lax.broadcasted_iota(jnp.int32, (rows, 1), 0)
    slope = jnp.zeros((rows, 1), F32)
    for head in range(heads):
        slope = jnp.where(row // draft == head, slopes_ref[:, head : head + 1], slope)
    scale = 1.0 / math.sqrt(head_size)
    length = length_ref[0]
    contract = (((1,), (1,)), ((), ()))
    slot = lax.broadcasted_iota(jnp.int32, (rows, slots), 1)
    suffix_scores = lax.dot_general(spread, suffix_ref[0], contract, preferred_element_type=F32)
    suffix_scores = suffix_scores * scale + slope * slot.astype(F32)
    suffix_scores = jnp.where(slot < length, suffix_scores, -jnp.inf)
    place = lax.broadcasted_iota(jnp.int32, (rows, draft), 1)
    draft_scores = lax.dot_general(spread, draft_ref[0], contract, preferred_element_type=F32)
    draft_scores = draft_scores * scale + slope * (place + length).astype(F32)
    token = lax.broadcasted_iota(jnp.int32, (rows, draft), 0) % draft
    draft_scores = jnp.where(place <= token, draft_scores, -jnp.inf)
    top = jnp.maximum(
        jnp.max(suffix_scores, axis=1, keepdims=True), jnp.max(draft_scores, axis=1, keepdims=True)
    )
    suffix_weights = jnp.exp(suffix_scores - top)
    draft_weights = jnp.exp(draft_scores - top)
    total = jnp.sum(suffix_weights, axis=1, keepdims=True) + jnp.sum(
        draft_weights, axis=1, keepdims=True
    )
    sums = jnp.dot(suffix_weights.astype(BF16), suffix_ref[1], preferred_element_type=F32)
    sums += jnp.dot(draft_weights.astype(BF16), draft_ref[1], preferred_element_type=F32)
    sums = sums * (1.0 / total)
    level = top + jnp.log(total)
    result = jnp.zeros((draft, width), F32)
    stats = jnp.zeros((draft, LANES), F32)
    lane = lax.broadcasted_iota(jnp.int32, (draft, LANES), 1)
    for head in range(heads):
        rows_of = slice(head * draft, (head + 1) * draft)
        result = jnp.where(masks[head], sums[rows_of], result)
        stats = jnp.where(lane == head, level[rows_of], stats)
    out_ref[...] = result
    stats_ref[...] = stats


def own_part(query_rows, suffix_kv, draft_kv, slopes, length):
    draft, width = query_rows.shape
    heads = slopes.shape[0]
    vmem = pl.BlockSpec(memory_space=pltpu.VMEM)
    smem = pl.BlockSpec(memory_space=pltpu.SMEM)
    return pl.pallas_call(
        functools.partial(own_kernel, heads=heads, head_size=width // heads),
        out_shape=(
            jax.ShapeDtypeStruct((draft, width), F32),
            jax.ShapeDtypeStruct((draft, LANES), F32),
        ),
        in_specs=[smem, vmem, vmem, vmem, vmem],
        out_specs=(vmem, vmem),
        compiler_params=pltpu.CompilerParams(vmem_limit_bytes=12 * MIB),
    )(length, slopes[None, :], query_rows, suffix_kv, draft_kv)


def merge_kernel(parts_ref, own_ref, level_ref, out_ref, *, heads, head_size):
    count = parts_ref.shape[0]
    draft, width = own_ref.shape
    tiles = width // LANES
    levels = [level_ref[...]]
    for part in range(count):
        packed = parts_ref[part, tiles * draft : (tiles + 1) * draft].astype(F32)
        levels.append(
            packed
            + pltpu.roll(packed, LANES - heads, 1)
            + pltpu.roll(packed, LANES - 2 * heads, 1)
        )
    top = functools.reduce(jnp.maximum, levels)
    shares = [jnp.exp(level - top) for level in levels]
    total = functools.reduce(jnp.add, shares)
    shares = [share / total for share in shares]
    for tile in range(tiles):
        lanes = slice(tile * LANES, (tile + 1) * LANES)
        joined = jnp.zeros((draft, LANES), F32)
        for part, share in enumerate(shares):
            factor = jnp.zeros((draft, LANES), F32)
            for head in range(heads):
                first, last = head_lanes(head, tile, head_size)
                if first < last:
                    factor = jnp.where(
                        lane_mask((draft, LANES), first, last), share[:, head : head + 1], factor
                    )
            if part == 0:
                value = own_ref[:, lanes]
            else:
                value = parts_ref[part - 1, tile * draft : (tile + 1) * draft].astype(F32)
            joined += factor * value
        joined = joined.astype(BF16)
        for target in range(out_ref.shape[0]):
            out_ref[target, :, lanes] = joined


def merge_parts(parts, own, level, heads, targets):
    draft, width = own.shape
    vmem = pl.BlockSpec(memory_space=pltpu.VMEM)
    return pl.pallas_call(
        functools.partial(merge_kernel, heads=heads, head_size=width // heads),
        out_shape=jax.ShapeDtypeStruct((targets, draft, width), BF16),
        in_specs=[vmem, vmem, vmem],
        out_specs=vmem,
        compiler_params=pltpu.CompilerParams(vmem_limit_bytes=10 * MIB),
    )(parts, own, level)


def packed_sums(value, lanes):
    lane = lax.broadcasted_iota(jnp.int32, (value.shape[0], lanes), 1)
    packed = jnp.zeros((value.shape[0], lanes), F32)
    for place, term in enumerate(split_three(value)):
        packed = jnp.where(lane == place, term, packed)
    return packed.astype(BF16)


def project_kernel(ctx_ref, rows_ref, parts_ref, *refs, mp):
    *weight_refs, out_ref = refs
    columns = weight_refs[0].shape[0]
    blocks = len(weight_refs)
    _, pair, draft, lanes = out_ref.shape
    req, _, width = rows_ref.shape
    rows = rows_ref[...].reshape(req * draft, width)
    products = []
    for place, weight_ref in enumerate(weight_refs):
        beside, back = divmod(place, blocks // pair)
        block = lax.rem(ctx_ref[0] + blocks - pair * back, blocks) ^ beside
        product = lax.dot_general(
            rows, weight_ref[...], (((1,), (1,)), ((), ())), preferred_element_type=F32
        )
        looked_up = parts_ref[block, parts_ref.shape[1] - columns :].astype(F32)
        products.append((block, product + jnp.transpose(looked_up)))
    total = functools.reduce(jnp.add, [product for _, product in products])
    sums = packed_sums(jnp.sum(total, axis=1, keepdims=True), lanes - columns)
    for block, product in products:
        product = jnp.concatenate([product.astype(BF16), sums], axis=1)
        piece, half = lax.shift_right_logical(block, 1), block & 1
        for target in range(req):
            out_ref[target * mp + piece, half] = product[target * draft : (target + 1) * draft]


def project_rows(rows, weights, parts, ctx_index, mp):
    req, draft, _ = rows.shape
    columns = weights[0].shape[0]
    lanes = -(-(columns + 3) // LANES) * LANES
    vmem = pl.BlockSpec(memory_space=pltpu.VMEM)
    return pl.pallas_call(
        functools.partial(project_kernel, mp=mp),
        out_shape=jax.ShapeDtypeStruct((req * mp, len(weights) // mp, draft, lanes), BF16),
        in_specs=[pl.BlockSpec(memory_space=pltpu.SMEM)] + [vmem] * (2 + len(weights)),
        out_specs=vmem,
        compiler_params=pltpu.CompilerParams(vmem_limit_bytes=10 * MIB),
    )(ctx_index, rows, parts, *weights)


def residual_kernel(parts_ref, gain_ref, out_ref, centred_ref, *, mp, columns):
    sources, pair, _, _ = parts_ref.shape
    _, width = out_ref.shape
    blocks = []
    for half in range(pair):
        for source in range(sources // mp):
            block = parts_ref[source * mp, half].astype(F32)
            for piece in range(1, mp):
                block += parts_ref[source * mp + piece, half].astype(F32)
            blocks.append(block)
    residual = jnp.concatenate([block[:, :columns] for block in blocks], axis=1)
    out_ref[...] = residual
    sums = functools.reduce(jnp.add, blocks[: sources // mp])
    mean = sum(sums[:, columns + term : columns + term + 1] for term in range(3)) / (mp * width)
    centred = residual - mean
    squares = packed_sums(jnp.sum(centred * centred, axis=1, keepdims=True), LANES)
    scaled = (centred * gain_ref[...]).astype(BF16)
    for target in range(centred_ref.shape[0]):
        centred_ref[target, :, :width] = scaled
        centred_ref[target, :, width:] = squares


def residual_rows(parts, gain, mp, draft, columns, targets):
    vmem = pl.BlockSpec(memory_space=pltpu.VMEM)
    width = gain.shape[0]
    return pl.pallas_call(
        functools.partial(residual_kernel, mp=mp, columns=columns),
        out_shape=(
            jax.ShapeDtypeStruct((draft, width), F32),
            jax.ShapeDtypeStruct((targets, draft, width + LANES), BF16),
        ),
        in_specs=[vmem, vmem],
        out_specs=(vmem, vmem),
        compiler_params=pltpu.CompilerParams(vmem_limit_bytes=10 * MIB),
    )(parts, gain[None, :])


def lift_kernel(rows_ref, weight_ref, out_ref, *, hidden):
    blocks, _, width = weight_ref.shape
    mp, height, _ = out_ref.shape
    pair = blocks // mp
    rows = rows_ref[:, :width]
    for block in range(blocks):
        piece, place = divmod(block, pair)
        out_ref[piece, place * hidden : (place + 1) * hidden] = lax.dot_general(
            weight_ref[block, weight_ref.shape[1] - hidden :],
            rows,
            (((1,), (1,)), ((), ())),
            preferred_element_type=F32,
        ).astype(BF16)
    squares = jnp.transpose(rows_ref[:, width:].astype(F32)).astype(BF16)
    for piece in range(mp):
        out_ref[piece, pair * hidden :] = squares[: height - pair * hidden]


def lift_rows(rows, weight, hidden, mp):
    blocks = weight.shape[0]
    vmem = pl.BlockSpec(memory_space=pltpu.VMEM)
    return pl.pallas_call(
        functools.partial(lift_kernel, hidden=hidden),
        out_shape=jax.ShapeDtypeStruct((mp, blocks // mp * hidden + 16, rows.shape[0]), BF16),
        in_specs=[vmem, vmem],
        out_specs=vmem,
        compiler_params=pltpu.CompilerParams(vmem_limit_bytes=20 * MIB),
    )(rows, weight)


def gelu_kernel(parts_ref, out_ref, *, model_width):
    hidden = out_ref.shape[1]
    total = parts_ref[0].astype(F32)
    for piece in range(1, parts_ref.shape[0]):
        total += parts_ref[piece].astype(F32)
    squares = sum(total[hidden + term : hidden + term + 1] for term in range(3))
    lifted = total[:hidden] * lax.rsqrt(squares / model_width + 1e-05)
    activated = (0.5 * lifted * (1.0 + lax.erf(lifted * math.sqrt(0.5)))).astype(BF16)
    for target in range(out_ref.shape[0]):
        out_ref[target] = activated


def activate(parts, hidden, model_width):
    vmem = pl.BlockSpec(memory_space=pltpu.VMEM)
    return pl.pallas_call(
        functools.partial(gelu_kernel, model_width=model_width),
        out_shape=jax.ShapeDtypeStruct((parts.shape[0], hidden, parts.shape[2]), BF16),
        in_specs=[vmem],
        out_specs=vmem,
        compiler_params=pltpu.CompilerParams(vmem_limit_bytes=10 * MIB),
    )(parts)


def lower_kernel(hidden_ref, weight_ref, out_ref):
    blocks, features, _ = weight_ref.shape
    pair = blocks // hidden_ref.shape[0]
    total = None
    for block in range(blocks):
        piece, place = divmod(block, pair)
        product = lax.dot_general(
            hidden_ref[piece, place * features : (place + 1) * features],
            weight_ref[block],
            (((0,), (0,)), ((), ())),
            preferred_element_type=F32,
        )
        total = product if total is None else total + product
    out_ref[...] = total.astype(BF16).reshape(out_ref.shape)


def lower_rows(hidden, weight, targets):
    vmem = pl.BlockSpec(memory_space=pltpu.VMEM)
    return pl.pallas_call(
        lower_kernel,
        out_shape=jax.ShapeDtypeStruct((targets, hidden.shape[2] // targets, weight.shape[2]), BF16),
        in_specs=[vmem, vmem],
        out_specs=vmem,
        compiler_params=pltpu.CompilerParams(vmem_limit_bytes=20 * MIB),
    )(hidden, weight)


def finish_kernel(parts_ref, residual_ref, out_ref):
    total = parts_ref[0].astype(F32)
    for piece in range(1, parts_ref.shape[0]):
        total += parts_ref[piece].astype(F32)
    out_ref[...] = residual_ref[...] + total


def finish(parts, residual):
    vmem = pl.BlockSpec(memory_space=pltpu.VMEM)
    return pl.pallas_call(
        finish_kernel,
        out_shape=jax.ShapeDtypeStruct(residual.shape, F32),
        in_specs=[vmem, vmem],
        out_specs=vmem,
        compiler_params=pltpu.CompilerParams(vmem_limit_bytes=10 * MIB),
    )(parts, residual)


def after(value, earlier):
    return lax.optimization_barrier((value, earlier))[0]


def exchange(value, axis):
    return lax.all_to_all(value, axis, split_axis=0, concat_axis=0, tiled=True)


def per_device(
    token_ids,
    embed_table,
    queries,
    draft_kv,
    prefix_kv,
    suffix_kv,
    suffix_len,
    slopes,
    out_weight,
    ln_gain,
    up_weight,
    down_weight,
):
    heads = slopes.shape[0]
    _, draft, width = queries.shape
    prompt_local = prefix_kv.shape[1]
    ctx_count = lax.axis_size("ctx")
    req_count = lax.axis_size("req")
    mp_count = lax.axis_size("mp")
    ctx_index = lax.axis_index("ctx")
    model_index = lax.axis_index("mp")
    quarter = ln_gain.shape[0]

    copies = jnp.broadcast_to(queries, (ctx_count, draft, width))
    gathered = exchange(copies, "ctx")
    vocab_local = embed_table.shape[0]
    shifted = token_ids.reshape(1, -1) - model_index * vocab_local
    looked_up = look_up(shifted, embed_table.T)
    gathered, looked_up = lax.optimization_barrier((gathered, looked_up))
    up_all = lax.all_gather(after(up_weight, gathered).T, "ctx")
    down_all = lax.all_gather(after(down_weight, gathered), "ctx")

    out_blocks = [after(out_weight.T, looked_up)]
    out_blocks += [
        lax.ppermute(out_blocks[0], "ctx", [(i, (i + step) % ctx_count) for i in range(ctx_count)])
        for step in range(2, ctx_count, 2)
    ]

    offset = (prompt_local * (ctx_count - ctx_index)).astype(jnp.int32).reshape(1)
    parts = prompt_part(
        gathered.reshape(ctx_count * draft, width),
        prefix_kv,
        slopes,
        offset,
        looked_up,
        ctx_count,
    )
    parts, *out_blocks = lax.optimization_barrier((parts, *out_blocks))
    own, own_level = own_part(
        after(queries[0], parts), suffix_kv[:, 0], draft_kv[:, 0], slopes, suffix_len
    )
    parts = exchange(parts, "ctx")
    out_blocks += [
        lax.ppermute(block, "ctx", [(i, i ^ 1) for i in range(ctx_count)])
        for block in out_blocks
    ]
    attended = exchange(merge_parts(parts, own, own_level, heads, req_count), "req")

    pieces = exchange(
        project_rows(
            attended, out_blocks, parts, ctx_index.astype(jnp.int32).reshape(1), mp_count
        ),
        ("req", "mp"),
    )
    residual, centred = residual_rows(
        pieces, ln_gain, mp_count, draft, out_weight.shape[1], req_count
    )
    centred = exchange(centred, "req").reshape(req_count * draft, -1)

    hidden = up_weight.shape[1]
    lifted = exchange(lift_rows(centred, up_all, hidden, mp_count), "mp")
    activated = activate(lifted, ctx_count // mp_count * hidden, quarter * mp_count)
    activated = exchange(activated, "mp")
    lowered = exchange(lower_rows(activated, down_all, req_count), "req")
    layer_out = finish(lowered, residual)
    return residual[None], layer_out[None]


def solution(mesh):
    rows = ("ctx", "req")
    in_specs = (
        P(),
        P("mp", rows),
        P(rows, None, "mp"),
        P(None, rows, None, "mp"),
        P(None, "ctx", "mp"),
        P(None, rows, None, "mp"),
        P(rows),
        P("mp"),
        P("mp", rows),
        P("mp"),
        P("mp", rows),
        P(rows, "mp"),
    )
    out_specs = (P(rows, None, "mp"), P(rows, None, "mp"))
    return jax.shard_map(
        per_device, mesh=mesh, in_specs=in_specs, out_specs=out_specs, check_vma=False
    )
```

```python
import functools
import math

import jax
import jax.numpy as jnp
from jax import lax
from jax.experimental import pallas as pl
from jax.experimental.pallas import tpu as pltpu
from jax.sharding import PartitionSpec as P

LANES = 128
F32 = jnp.float32
BF16 = jnp.bfloat16
MIB = 1024 * 1024


def head_lanes(head, tile, head_size):
    first = max(head * head_size - tile * LANES, 0)
    last = min((head + 1) * head_size - tile * LANES, LANES)
    return first, last


def head_tiles(head, head_size):
    return range(head * head_size // LANES, ((head + 1) * head_size - 1) // LANES + 1)


def lane_mask(shape, first, last):
    lane = lax.broadcasted_iota(jnp.int32, shape, len(shape) - 1)
    return (lane >= first) & (lane < last)


def split_three(value):
    high = value.astype(BF16).astype(F32)
    rest = value - high
    middle = rest.astype(BF16).astype(F32)
    low = rest - middle
    return high, middle, low


def prompt_kernel(
    offset_ref, slopes_ref, query_ref, looked_ref, prefix_ref, out_ref, *, heads, head_size
):
    rows, width = query_ref.shape
    keys = prefix_ref.shape[1]
    tiles = width // LANES
    scale = 1.0 / math.sqrt(head_size)
    position = (
        lax.broadcasted_iota(jnp.int32, (1, keys), 1) - offset_ref[0]
    ).astype(F32)
    parts = [jnp.zeros((rows, LANES), F32) for _ in range(tiles)]
    stats = jnp.zeros((rows, LANES), F32)
    stat_lane = lax.broadcasted_iota(jnp.int32, (rows, LANES), 1)
    for head in range(heads):
        span = head_tiles(head, head_size)
        window = slice(span[0] * LANES, (span[-1] + 1) * LANES)
        query_window = jnp.concatenate(
            [
                jnp.where(
                    lane_mask((rows, LANES), *head_lanes(head, tile, head_size)),
                    query_ref[:, tile * LANES : (tile + 1) * LANES],
                    jnp.zeros((rows, LANES), BF16),
                )
                for tile in span
            ],
            axis=1,
        )
        scores = lax.dot_general(
            query_window,
            prefix_ref[0, :, window],
            (((1,), (1,)), ((), ())),
            preferred_element_type=F32,
        )
        scores = scores * scale + slopes_ref[:, head : head + 1] * position
        top = jnp.max(scores, axis=1, keepdims=True)
        weights = jnp.exp(scores - top)
        total = jnp.sum(weights, axis=1, keepdims=True)
        sums = jnp.dot(
            weights.astype(BF16), prefix_ref[1, :, window], preferred_element_type=F32
        )
        sums = sums * (1.0 / total)
        for place, tile in enumerate(span):
            parts[tile] = jnp.where(
                lane_mask((rows, LANES), *head_lanes(head, tile, head_size)),
                sums[:, place * LANES : (place + 1) * LANES],
                parts[tile],
            )
        stats = jnp.where(stat_lane % heads == head, top + jnp.log(total), stats)
    high, middle, low = split_three(stats)
    group = stat_lane // heads
    packed = jnp.where(
        group == 0, high, jnp.where(group == 1, middle, jnp.where(group == 2, low, 0.0))
    )
    targets = out_ref.shape[0]
    draft = rows // targets
    for tile, value in enumerate([*parts, packed]):
        value = value.astype(BF16)
        for target in range(targets):
            out_ref[target, tile * draft : (tile + 1) * draft] = value[
                target * draft : (target + 1) * draft
            ]
    for target in range(targets):
        out_ref[target, (tiles + 1) * draft :] = looked_ref[
            :, target * LANES : (target + 1) * LANES
        ]


def prompt_part(query_rows, prefix_kv, slopes, offset, looked_up, targets):
    rows, width = query_rows.shape
    heads = slopes.shape[0]
    tiles = width // LANES
    return pl.pallas_call(
        functools.partial(prompt_kernel, heads=heads, head_size=width // heads),
        out_shape=jax.ShapeDtypeStruct(
            (targets, (tiles + 1) * (rows // targets) + looked_up.shape[0], LANES), BF16
        ),
        in_specs=[
            pl.BlockSpec(memory_space=pltpu.SMEM),
            pl.BlockSpec(memory_space=pltpu.VMEM),
            pl.BlockSpec(memory_space=pltpu.VMEM),
            pl.BlockSpec(memory_space=pltpu.VMEM),
            pl.BlockSpec(memory_space=pltpu.VMEM),
        ],
        out_specs=pl.BlockSpec(memory_space=pltpu.VMEM),
        compiler_params=pltpu.CompilerParams(vmem_limit_bytes=20 * MIB),
    )(offset, slopes[None, :], query_rows, looked_up, prefix_kv)


def lookup_kernel(ids_ref, table_ref, out_ref):
    count = ids_ref.shape[1]
    features, vocab = table_ref.shape
    step = math.gcd(vocab, 2 * LANES)
    ids = ids_ref[...]
    place = lax.broadcasted_iota(jnp.int32, (step, count), 0)
    total = jnp.zeros((features, count), F32)
    for first in range(0, vocab, step):
        chosen = jnp.where(place == ids - first, 1.0, 0.0).astype(BF16)
        total += jnp.dot(table_ref[:, first : first + step], chosen, preferred_element_type=F32)
    out_ref[...] = total.astype(BF16)


def look_up(ids, table):
    vmem = pl.BlockSpec(memory_space=pltpu.VMEM)
    return pl.pallas_call(
        lookup_kernel,
        out_shape=jax.ShapeDtypeStruct((table.shape[0], ids.shape[1]), BF16),
        in_specs=[vmem, vmem],
        out_specs=vmem,
        compiler_params=pltpu.CompilerParams(vmem_limit_bytes=12 * MIB),
    )(ids, table)


def own_kernel(
    length_ref, slopes_ref, query_ref, suffix_ref, draft_ref, out_ref, stats_ref, *, heads, head_size
):
    draft, width = query_ref.shape
    slots = suffix_ref.shape[1]
    rows = heads * draft
    query = query_ref[...]
    masks = [
        lane_mask((draft, width), head * head_size, (head + 1) * head_size)
        for head in range(heads)
    ]
    spread = jnp.concatenate(
        [jnp.where(mask, query, jnp.zeros_like(query)) for mask in masks], axis=0
    )
    row = lax.broadcasted_iota(jnp.int32, (rows, 1), 0)
    slope = jnp.zeros((rows, 1), F32)
    for head in range(heads):
        slope = jnp.where(row // draft == head, slopes_ref[:, head : head + 1], slope)
    scale = 1.0 / math.sqrt(head_size)
    length = length_ref[0]
    contract = (((1,), (1,)), ((), ()))
    slot = lax.broadcasted_iota(jnp.int32, (rows, slots), 1)
    suffix_scores = lax.dot_general(spread, suffix_ref[0], contract, preferred_element_type=F32)
    suffix_scores = suffix_scores * scale + slope * slot.astype(F32)
    suffix_scores = jnp.where(slot < length, suffix_scores, -jnp.inf)
    place = lax.broadcasted_iota(jnp.int32, (rows, draft), 1)
    draft_scores = lax.dot_general(spread, draft_ref[0], contract, preferred_element_type=F32)
    draft_scores = draft_scores * scale + slope * (place + length).astype(F32)
    token = lax.broadcasted_iota(jnp.int32, (rows, draft), 0) % draft
    draft_scores = jnp.where(place <= token, draft_scores, -jnp.inf)
    top = jnp.maximum(
        jnp.max(suffix_scores, axis=1, keepdims=True), jnp.max(draft_scores, axis=1, keepdims=True)
    )
    suffix_weights = jnp.exp(suffix_scores - top)
    draft_weights = jnp.exp(draft_scores - top)
    total = jnp.sum(suffix_weights, axis=1, keepdims=True) + jnp.sum(
        draft_weights, axis=1, keepdims=True
    )
    sums = jnp.dot(suffix_weights.astype(BF16), suffix_ref[1], preferred_element_type=F32)
    sums += jnp.dot(draft_weights.astype(BF16), draft_ref[1], preferred_element_type=F32)
    sums = sums * (1.0 / total)
    level = top + jnp.log(total)
    result = jnp.zeros((draft, width), F32)
    stats = jnp.zeros((draft, LANES), F32)
    lane = lax.broadcasted_iota(jnp.int32, (draft, LANES), 1)
    for head in range(heads):
        rows_of = slice(head * draft, (head + 1) * draft)
        result = jnp.where(masks[head], sums[rows_of], result)
        stats = jnp.where(lane == head, level[rows_of], stats)
    out_ref[...] = result
    stats_ref[...] = stats


def own_part(query_rows, suffix_kv, draft_kv, slopes, length):
    draft, width = query_rows.shape
    heads = slopes.shape[0]
    vmem = pl.BlockSpec(memory_space=pltpu.VMEM)
    smem = pl.BlockSpec(memory_space=pltpu.SMEM)
    return pl.pallas_call(
        functools.partial(own_kernel, heads=heads, head_size=width // heads),
        out_shape=(
            jax.ShapeDtypeStruct((draft, width), F32),
            jax.ShapeDtypeStruct((draft, LANES), F32),
        ),
        in_specs=[smem, vmem, vmem, vmem, vmem],
        out_specs=(vmem, vmem),
        compiler_params=pltpu.CompilerParams(vmem_limit_bytes=12 * MIB),
    )(length, slopes[None, :], query_rows, suffix_kv, draft_kv)


def merge_kernel(parts_ref, own_ref, level_ref, out_ref, *, heads, head_size):
    count = parts_ref.shape[0]
    draft, width = own_ref.shape
    tiles = width // LANES
    levels = [level_ref[...]]
    for part in range(count):
        packed = parts_ref[part, tiles * draft : (tiles + 1) * draft].astype(F32)
        levels.append(
            packed
            + pltpu.roll(packed, LANES - heads, 1)
            + pltpu.roll(packed, LANES - 2 * heads, 1)
        )
    top = functools.reduce(jnp.maximum, levels)
    shares = [jnp.exp(level - top) for level in levels]
    total = functools.reduce(jnp.add, shares)
    shares = [share / total for share in shares]
    for tile in range(tiles):
        lanes = slice(tile * LANES, (tile + 1) * LANES)
        joined = jnp.zeros((draft, LANES), F32)
        for part, share in enumerate(shares):
            factor = jnp.zeros((draft, LANES), F32)
            for head in range(heads):
                first, last = head_lanes(head, tile, head_size)
                if first < last:
                    factor = jnp.where(
                        lane_mask((draft, LANES), first, last), share[:, head : head + 1], factor
                    )
            if part == 0:
                value = own_ref[:, lanes]
            else:
                value = parts_ref[part - 1, tile * draft : (tile + 1) * draft].astype(F32)
            joined += factor * value
        joined = joined.astype(BF16)
        for target in range(out_ref.shape[0]):
            out_ref[target, :, lanes] = joined


def merge_parts(parts, own, level, heads, targets):
    draft, width = own.shape
    vmem = pl.BlockSpec(memory_space=pltpu.VMEM)
    return pl.pallas_call(
        functools.partial(merge_kernel, heads=heads, head_size=width // heads),
        out_shape=jax.ShapeDtypeStruct((targets, draft, width), BF16),
        in_specs=[vmem, vmem, vmem],
        out_specs=vmem,
        compiler_params=pltpu.CompilerParams(vmem_limit_bytes=10 * MIB),
    )(parts, own, level)


def packed_sums(value, lanes):
    lane = lax.broadcasted_iota(jnp.int32, (value.shape[0], lanes), 1)
    packed = jnp.zeros((value.shape[0], lanes), F32)
    for place, term in enumerate(split_three(value)):
        packed = jnp.where(lane == place, term, packed)
    return packed.astype(BF16)


def project_kernel(ctx_ref, rows_ref, parts_ref, *refs, mp):
    *weight_refs, out_ref = refs
    columns = weight_refs[0].shape[0]
    blocks = len(weight_refs)
    _, pair, draft, lanes = out_ref.shape
    req, _, width = rows_ref.shape
    rows = rows_ref[...].reshape(req * draft, width)
    products = []
    for place, weight_ref in enumerate(weight_refs):
        beside, back = divmod(place, blocks // pair)
        block = lax.rem(ctx_ref[0] + blocks - pair * back, blocks) ^ beside
        product = lax.dot_general(
            rows, weight_ref[...], (((1,), (1,)), ((), ())), preferred_element_type=F32
        )
        looked_up = parts_ref[block, parts_ref.shape[1] - columns :].astype(F32)
        products.append((block, product + jnp.transpose(looked_up)))
    total = functools.reduce(jnp.add, [product for _, product in products])
    sums = packed_sums(jnp.sum(total, axis=1, keepdims=True), lanes - columns)
    for block, product in products:
        product = jnp.concatenate([product.astype(BF16), sums], axis=1)
        piece, half = lax.shift_right_logical(block, 1), block & 1
        for target in range(req):
            out_ref[target * mp + piece, half] = product[target * draft : (target + 1) * draft]


def project_rows(rows, weights, parts, ctx_index, mp):
    req, draft, _ = rows.shape
    columns = weights[0].shape[0]
    lanes = -(-(columns + 3) // LANES) * LANES
    vmem = pl.BlockSpec(memory_space=pltpu.VMEM)
    return pl.pallas_call(
        functools.partial(project_kernel, mp=mp),
        out_shape=jax.ShapeDtypeStruct((req * mp, len(weights) // mp, draft, lanes), BF16),
        in_specs=[pl.BlockSpec(memory_space=pltpu.SMEM)] + [vmem] * (2 + len(weights)),
        out_specs=vmem,
        compiler_params=pltpu.CompilerParams(vmem_limit_bytes=10 * MIB),
    )(ctx_index, rows, parts, *weights)


def residual_kernel(parts_ref, gain_ref, out_ref, centred_ref, *, mp, columns):
    sources, pair, _, _ = parts_ref.shape
    _, width = out_ref.shape
    blocks = []
    for half in range(pair):
        for source in range(sources // mp):
            block = parts_ref[source * mp, half].astype(F32)
            for piece in range(1, mp):
                block += parts_ref[source * mp + piece, half].astype(F32)
            blocks.append(block)
    residual = jnp.concatenate([block[:, :columns] for block in blocks], axis=1)
    out_ref[...] = residual
    sums = functools.reduce(jnp.add, blocks[: sources // mp])
    mean = sum(sums[:, columns + term : columns + term + 1] for term in range(3)) / (mp * width)
    centred = residual - mean
    squares = packed_sums(jnp.sum(centred * centred, axis=1, keepdims=True), LANES)
    scaled = (centred * gain_ref[...]).astype(BF16)
    for target in range(centred_ref.shape[0]):
        centred_ref[target, :, :width] = scaled
        centred_ref[target, :, width:] = squares


def residual_rows(parts, gain, mp, draft, columns, targets):
    vmem = pl.BlockSpec(memory_space=pltpu.VMEM)
    width = gain.shape[0]
    return pl.pallas_call(
        functools.partial(residual_kernel, mp=mp, columns=columns),
        out_shape=(
            jax.ShapeDtypeStruct((draft, width), F32),
            jax.ShapeDtypeStruct((targets, draft, width + LANES), BF16),
        ),
        in_specs=[vmem, vmem],
        out_specs=(vmem, vmem),
        compiler_params=pltpu.CompilerParams(vmem_limit_bytes=10 * MIB),
    )(parts, gain[None, :])


def lift_kernel(rows_ref, *refs):
    *weight_refs, out_ref = refs
    width = weight_refs[0].shape[1]
    mp, height, _ = out_ref.shape
    held = sum(ref.shape[0] for ref in weight_refs) // mp
    rows = rows_ref[:, :width]
    first = 0
    for ref in weight_refs:
        piece, place = divmod(first, held)
        out_ref[piece, place : place + ref.shape[0]] = lax.dot_general(
            ref[...], rows, (((1,), (1,)), ((), ())), preferred_element_type=F32
        ).astype(BF16)
        first += ref.shape[0]
    squares = jnp.transpose(rows_ref[:, width:].astype(F32)).astype(BF16)
    for piece in range(mp):
        out_ref[piece, held:] = squares[: height - held]


def lift_rows(rows, weights, mp):
    held = sum(weight.shape[0] for weight in weights) // mp
    vmem = pl.BlockSpec(memory_space=pltpu.VMEM)
    return pl.pallas_call(
        lift_kernel,
        out_shape=jax.ShapeDtypeStruct((mp, held + 16, rows.shape[0]), BF16),
        in_specs=[vmem] * (1 + len(weights)),
        out_specs=vmem,
        compiler_params=pltpu.CompilerParams(vmem_limit_bytes=20 * MIB),
    )(rows, *weights)


def gelu_kernel(parts_ref, out_ref, *, model_width):
    hidden = out_ref.shape[1]
    total = parts_ref[0].astype(F32)
    for piece in range(1, parts_ref.shape[0]):
        total += parts_ref[piece].astype(F32)
    squares = sum(total[hidden + term : hidden + term + 1] for term in range(3))
    lifted = total[:hidden] * lax.rsqrt(squares / model_width + 1e-05)
    activated = (0.5 * lifted * (1.0 + lax.erf(lifted * math.sqrt(0.5)))).astype(BF16)
    for target in range(out_ref.shape[0]):
        out_ref[target] = activated


def activate(parts, hidden, model_width):
    vmem = pl.BlockSpec(memory_space=pltpu.VMEM)
    return pl.pallas_call(
        functools.partial(gelu_kernel, model_width=model_width),
        out_shape=jax.ShapeDtypeStruct((parts.shape[0], hidden, parts.shape[2]), BF16),
        in_specs=[vmem],
        out_specs=vmem,
        compiler_params=pltpu.CompilerParams(vmem_limit_bytes=10 * MIB),
    )(parts)


def lower_kernel(hidden_ref, *refs):
    *weight_refs, out_ref = refs
    held = hidden_ref.shape[1]
    total = None
    first = 0
    for ref in weight_refs:
        piece, place = divmod(first, held)
        product = lax.dot_general(
            hidden_ref[piece, place : place + ref.shape[0]],
            ref[...],
            (((0,), (0,)), ((), ())),
            preferred_element_type=F32,
        )
        total = product if total is None else total + product
        first += ref.shape[0]
    out_ref[...] = total.astype(BF16).reshape(out_ref.shape)


def lower_rows(hidden, weights, targets):
    vmem = pl.BlockSpec(memory_space=pltpu.VMEM)
    return pl.pallas_call(
        lower_kernel,
        out_shape=jax.ShapeDtypeStruct(
            (targets, hidden.shape[2] // targets, weights[0].shape[1]), BF16
        ),
        in_specs=[vmem] * (1 + len(weights)),
        out_specs=vmem,
        compiler_params=pltpu.CompilerParams(vmem_limit_bytes=20 * MIB),
    )(hidden, *weights)


def finish_kernel(parts_ref, residual_ref, out_ref):
    total = parts_ref[0].astype(F32)
    for piece in range(1, parts_ref.shape[0]):
        total += parts_ref[piece].astype(F32)
    out_ref[...] = residual_ref[...] + total


def finish(parts, residual):
    vmem = pl.BlockSpec(memory_space=pltpu.VMEM)
    return pl.pallas_call(
        finish_kernel,
        out_shape=jax.ShapeDtypeStruct(residual.shape, F32),
        in_specs=[vmem, vmem],
        out_specs=vmem,
        compiler_params=pltpu.CompilerParams(vmem_limit_bytes=10 * MIB),
    )(parts, residual)


def after(value, earlier):
    return lax.optimization_barrier((value, earlier))[0]


def shifted_by(block, step):
    count = lax.axis_size("ctx")
    return lax.ppermute(block, "ctx", [(i, (i + step) % count) for i in range(count)])


def beside(blocks):
    count = lax.axis_size("ctx")
    return [lax.ppermute(block, "ctx", [(i, i ^ 1) for i in range(count)]) for block in blocks]


def nearest(block):
    return [block, shifted_by(block, 2), shifted_by(block, -2)]


def farthest(blocks):
    _, back, on = blocks
    half = back.shape[0] // 2
    return [shifted_by(back[:half], 2), shifted_by(on[half:], -2)]


def exchange(value, axis):
    return lax.all_to_all(value, axis, split_axis=0, concat_axis=0, tiled=True)


def per_device(
    token_ids,
    embed_table,
    queries,
    draft_kv,
    prefix_kv,
    suffix_kv,
    suffix_len,
    slopes,
    out_weight,
    ln_gain,
    up_weight,
    down_weight,
):
    heads = slopes.shape[0]
    _, draft, width = queries.shape
    prompt_local = prefix_kv.shape[1]
    ctx_count = lax.axis_size("ctx")
    req_count = lax.axis_size("req")
    mp_count = lax.axis_size("mp")
    ctx_index = lax.axis_index("ctx")
    model_index = lax.axis_index("mp")
    quarter = ln_gain.shape[0]

    copies = jnp.broadcast_to(queries, (ctx_count, draft, width))
    gathered = exchange(copies, "ctx")
    vocab_local = embed_table.shape[0]
    shifted = token_ids.reshape(1, -1) - model_index * vocab_local
    looked_up = look_up(shifted, embed_table.T)
    gathered, looked_up = lax.optimization_barrier((gathered, looked_up))
    out_blocks = [after(out_weight.T, looked_up)]
    out_blocks += [shifted_by(out_blocks[0], step) for step in range(2, ctx_count, 2)]
    up_blocks = nearest(after(up_weight.T, looked_up))

    offset = (prompt_local * (ctx_count - ctx_index)).astype(jnp.int32).reshape(1)
    parts = prompt_part(
        gathered.reshape(ctx_count * draft, width),
        prefix_kv,
        slopes,
        offset,
        looked_up,
        ctx_count,
    )
    parts, *out_blocks = lax.optimization_barrier((parts, *out_blocks))
    own, own_level = own_part(
        after(queries[0], parts), suffix_kv[:, 0], draft_kv[:, 0], slopes, suffix_len
    )
    parts = exchange(parts, "ctx")
    out_blocks += beside(out_blocks)
    merged = merge_parts(parts, own, own_level, heads, req_count)
    merged, *up_blocks = lax.optimization_barrier((merged, *up_blocks))
    attended = exchange(merged, "req")
    up_blocks += farthest(up_blocks)
    down_blocks = nearest(after(down_weight, merged))

    pieces = project_rows(
        attended, out_blocks, parts, ctx_index.astype(jnp.int32).reshape(1), mp_count
    )
    pieces, *up_blocks = lax.optimization_barrier((pieces, *up_blocks))
    pieces = exchange(pieces, ("req", "mp"))
    up_blocks += beside(up_blocks)
    residual, centred = residual_rows(
        pieces, ln_gain, mp_count, draft, out_weight.shape[1], req_count
    )
    centred, *down_blocks = lax.optimization_barrier((centred, *down_blocks))
    centred = exchange(centred, "req").reshape(req_count * draft, -1)
    down_blocks += farthest(down_blocks)

    lifted = lift_rows(centred, up_blocks, mp_count)
    lifted, *down_blocks = lax.optimization_barrier((lifted, *down_blocks))
    lifted = exchange(lifted, "mp")
    down_blocks += beside(down_blocks)
    hidden = up_weight.shape[1] * ctx_count // mp_count
    activated = exchange(activate(lifted, hidden, quarter * mp_count), "mp")
    lowered = exchange(lower_rows(activated, down_blocks, req_count), "req")
    layer_out = finish(lowered, residual)
    return residual[None], layer_out[None]


def solution(mesh):
    rows = ("ctx", "req")
    in_specs = (
        P(),
        P("mp", rows),
        P(rows, None, "mp"),
        P(None, rows, None, "mp"),
        P(None, "ctx", "mp"),
        P(None, rows, None, "mp"),
        P(rows),
        P("mp"),
        P("mp", rows),
        P("mp"),
        P("mp", rows),
        P(rows, "mp"),
    )
    out_specs = (P(rows, None, "mp"), P(rows, None, "mp"))
    return jax.shard_map(
        per_device, mesh=mesh, in_specs=in_specs, out_specs=out_specs, check_vma=False
    )
```

```python
import functools
import math

import jax
import jax.numpy as jnp
from jax import lax
from jax.experimental import pallas as pl
from jax.experimental.pallas import tpu as pltpu
from jax.sharding import PartitionSpec as P

LANES = 128
F32 = jnp.float32
BF16 = jnp.bfloat16
MIB = 1024 * 1024


def head_lanes(head, tile, head_size):
    first = max(head * head_size - tile * LANES, 0)
    last = min((head + 1) * head_size - tile * LANES, LANES)
    return first, last


def head_tiles(head, head_size):
    return range(head * head_size // LANES, ((head + 1) * head_size - 1) // LANES + 1)


def lane_mask(shape, first, last):
    lane = lax.broadcasted_iota(jnp.int32, shape, len(shape) - 1)
    return (lane >= first) & (lane < last)


def split_three(value):
    high = value.astype(BF16).astype(F32)
    rest = value - high
    middle = rest.astype(BF16).astype(F32)
    low = rest - middle
    return high, middle, low


def prompt_kernel(
    offset_ref, slopes_ref, query_ref, looked_ref, prefix_ref, out_ref, *, heads, head_size
):
    rows, width = query_ref.shape
    keys = prefix_ref.shape[1]
    tiles = width // LANES
    scale = 1.0 / math.sqrt(head_size)
    position = (
        lax.broadcasted_iota(jnp.int32, (1, keys), 1) - offset_ref[0]
    ).astype(F32)
    parts = [jnp.zeros((rows, LANES), F32) for _ in range(tiles)]
    stats = jnp.zeros((rows, LANES), F32)
    stat_lane = lax.broadcasted_iota(jnp.int32, (rows, LANES), 1)
    for head in range(heads):
        span = head_tiles(head, head_size)
        window = slice(span[0] * LANES, (span[-1] + 1) * LANES)
        query_window = jnp.concatenate(
            [
                jnp.where(
                    lane_mask((rows, LANES), *head_lanes(head, tile, head_size)),
                    query_ref[:, tile * LANES : (tile + 1) * LANES],
                    jnp.zeros((rows, LANES), BF16),
                )
                for tile in span
            ],
            axis=1,
        )
        scores = lax.dot_general(
            query_window,
            prefix_ref[0, :, window],
            (((1,), (1,)), ((), ())),
            preferred_element_type=F32,
        )
        scores = scores * scale + slopes_ref[:, head : head + 1] * position
        top = jnp.max(scores, axis=1, keepdims=True)
        weights = jnp.exp(scores - top)
        total = jnp.sum(weights, axis=1, keepdims=True)
        sums = jnp.dot(
            weights.astype(BF16), prefix_ref[1, :, window], preferred_element_type=F32
        )
        sums = sums * (1.0 / total)
        for place, tile in enumerate(span):
            parts[tile] = jnp.where(
                lane_mask((rows, LANES), *head_lanes(head, tile, head_size)),
                sums[:, place * LANES : (place + 1) * LANES],
                parts[tile],
            )
        stats = jnp.where(stat_lane % heads == head, top + jnp.log(total), stats)
    high, middle, low = split_three(stats)
    group = stat_lane // heads
    packed = jnp.where(
        group == 0, high, jnp.where(group == 1, middle, jnp.where(group == 2, low, 0.0))
    )
    targets = out_ref.shape[0]
    draft = rows // targets
    for tile, value in enumerate([*parts, packed]):
        value = value.astype(BF16)
        for target in range(targets):
            out_ref[target, tile * draft : (tile + 1) * draft] = value[
                target * draft : (target + 1) * draft
            ]
    for target in range(targets):
        out_ref[target, (tiles + 1) * draft :] = looked_ref[
            :, target * LANES : (target + 1) * LANES
        ]


def prompt_part(query_rows, prefix_kv, slopes, offset, looked_up, targets):
    rows, width = query_rows.shape
    heads = slopes.shape[0]
    tiles = width // LANES
    return pl.pallas_call(
        functools.partial(prompt_kernel, heads=heads, head_size=width // heads),
        out_shape=jax.ShapeDtypeStruct(
            (targets, (tiles + 1) * (rows // targets) + looked_up.shape[0], LANES), BF16
        ),
        in_specs=[
            pl.BlockSpec(memory_space=pltpu.SMEM),
            pl.BlockSpec(memory_space=pltpu.VMEM),
            pl.BlockSpec(memory_space=pltpu.VMEM),
            pl.BlockSpec(memory_space=pltpu.VMEM),
            pl.BlockSpec(memory_space=pltpu.VMEM),
        ],
        out_specs=pl.BlockSpec(memory_space=pltpu.VMEM),
        compiler_params=pltpu.CompilerParams(vmem_limit_bytes=20 * MIB),
    )(offset, slopes[None, :], query_rows, looked_up, prefix_kv)


def lookup_kernel(ids_ref, table_ref, out_ref):
    count = ids_ref.shape[1]
    features, vocab = table_ref.shape
    step = math.gcd(vocab, 2 * LANES)
    ids = ids_ref[...]
    place = lax.broadcasted_iota(jnp.int32, (step, count), 0)
    total = jnp.zeros((features, count), F32)
    for first in range(0, vocab, step):
        chosen = jnp.where(place == ids - first, 1.0, 0.0).astype(BF16)
        total += jnp.dot(table_ref[:, first : first + step], chosen, preferred_element_type=F32)
    out_ref[...] = total.astype(BF16)


def look_up(ids, table):
    vmem = pl.BlockSpec(memory_space=pltpu.VMEM)
    return pl.pallas_call(
        lookup_kernel,
        out_shape=jax.ShapeDtypeStruct((table.shape[0], ids.shape[1]), BF16),
        in_specs=[vmem, vmem],
        out_specs=vmem,
        compiler_params=pltpu.CompilerParams(vmem_limit_bytes=12 * MIB),
    )(ids, table)


def own_kernel(
    length_ref, slopes_ref, query_ref, suffix_ref, draft_ref, out_ref, stats_ref, *, heads, head_size
):
    draft, width = query_ref.shape
    slots = suffix_ref.shape[1]
    rows = heads * draft
    query = query_ref[...]
    masks = [
        lane_mask((draft, width), head * head_size, (head + 1) * head_size)
        for head in range(heads)
    ]
    spread = jnp.concatenate(
        [jnp.where(mask, query, jnp.zeros_like(query)) for mask in masks], axis=0
    )
    row = lax.broadcasted_iota(jnp.int32, (rows, 1), 0)
    slope = jnp.zeros((rows, 1), F32)
    for head in range(heads):
        slope = jnp.where(row // draft == head, slopes_ref[:, head : head + 1], slope)
    scale = 1.0 / math.sqrt(head_size)
    length = length_ref[0]
    contract = (((1,), (1,)), ((), ()))
    slot = lax.broadcasted_iota(jnp.int32, (rows, slots), 1)
    suffix_scores = lax.dot_general(spread, suffix_ref[0], contract, preferred_element_type=F32)
    suffix_scores = suffix_scores * scale + slope * slot.astype(F32)
    suffix_scores = jnp.where(slot < length, suffix_scores, -jnp.inf)
    place = lax.broadcasted_iota(jnp.int32, (rows, draft), 1)
    draft_scores = lax.dot_general(spread, draft_ref[0], contract, preferred_element_type=F32)
    draft_scores = draft_scores * scale + slope * (place + length).astype(F32)
    token = lax.broadcasted_iota(jnp.int32, (rows, draft), 0) % draft
    draft_scores = jnp.where(place <= token, draft_scores, -jnp.inf)
    top = jnp.maximum(
        jnp.max(suffix_scores, axis=1, keepdims=True), jnp.max(draft_scores, axis=1, keepdims=True)
    )
    suffix_weights = jnp.exp(suffix_scores - top)
    draft_weights = jnp.exp(draft_scores - top)
    total = jnp.sum(suffix_weights, axis=1, keepdims=True) + jnp.sum(
        draft_weights, axis=1, keepdims=True
    )
    sums = jnp.dot(suffix_weights.astype(BF16), suffix_ref[1], preferred_element_type=F32)
    sums += jnp.dot(draft_weights.astype(BF16), draft_ref[1], preferred_element_type=F32)
    sums = sums * (1.0 / total)
    level = top + jnp.log(total)
    result = jnp.zeros((draft, width), F32)
    stats = jnp.zeros((draft, LANES), F32)
    lane = lax.broadcasted_iota(jnp.int32, (draft, LANES), 1)
    for head in range(heads):
        rows_of = slice(head * draft, (head + 1) * draft)
        result = jnp.where(masks[head], sums[rows_of], result)
        stats = jnp.where(lane == head, level[rows_of], stats)
    out_ref[...] = result
    stats_ref[...] = stats


def own_part(query_rows, suffix_kv, draft_kv, slopes, length):
    draft, width = query_rows.shape
    heads = slopes.shape[0]
    vmem = pl.BlockSpec(memory_space=pltpu.VMEM)
    smem = pl.BlockSpec(memory_space=pltpu.SMEM)
    return pl.pallas_call(
        functools.partial(own_kernel, heads=heads, head_size=width // heads),
        out_shape=(
            jax.ShapeDtypeStruct((draft, width), F32),
            jax.ShapeDtypeStruct((draft, LANES), F32),
        ),
        in_specs=[smem, vmem, vmem, vmem, vmem],
        out_specs=(vmem, vmem),
        compiler_params=pltpu.CompilerParams(vmem_limit_bytes=12 * MIB),
    )(length, slopes[None, :], query_rows, suffix_kv, draft_kv)


def merge_kernel(parts_ref, own_ref, level_ref, out_ref, *, heads, head_size):
    count = parts_ref.shape[0]
    draft, width = own_ref.shape
    tiles = width // LANES
    levels = [level_ref[...]]
    for part in range(count):
        packed = parts_ref[part, tiles * draft : (tiles + 1) * draft].astype(F32)
        levels.append(
            packed
            + pltpu.roll(packed, LANES - heads, 1)
            + pltpu.roll(packed, LANES - 2 * heads, 1)
        )
    top = functools.reduce(jnp.maximum, levels)
    shares = [jnp.exp(level - top) for level in levels]
    total = functools.reduce(jnp.add, shares)
    shares = [share / total for share in shares]
    for tile in range(tiles):
        lanes = slice(tile * LANES, (tile + 1) * LANES)
        joined = jnp.zeros((draft, LANES), F32)
        for part, share in enumerate(shares):
            factor = jnp.zeros((draft, LANES), F32)
            for head in range(heads):
                first, last = head_lanes(head, tile, head_size)
                if first < last:
                    factor = jnp.where(
                        lane_mask((draft, LANES), first, last), share[:, head : head + 1], factor
                    )
            if part == 0:
                value = own_ref[:, lanes]
            else:
                value = parts_ref[part - 1, tile * draft : (tile + 1) * draft].astype(F32)
            joined += factor * value
        joined = joined.astype(BF16)
        for target in range(out_ref.shape[0]):
            out_ref[target, :, lanes] = joined


def merge_parts(parts, own, level, heads, targets):
    draft, width = own.shape
    vmem = pl.BlockSpec(memory_space=pltpu.VMEM)
    return pl.pallas_call(
        functools.partial(merge_kernel, heads=heads, head_size=width // heads),
        out_shape=jax.ShapeDtypeStruct((targets, draft, width), BF16),
        in_specs=[vmem, vmem, vmem],
        out_specs=vmem,
        compiler_params=pltpu.CompilerParams(vmem_limit_bytes=10 * MIB),
    )(parts, own, level)


def packed_sums(value, lanes):
    lane = lax.broadcasted_iota(jnp.int32, (value.shape[0], lanes), 1)
    packed = jnp.zeros((value.shape[0], lanes), F32)
    for place, term in enumerate(split_three(value)):
        packed = jnp.where(lane == place, term, packed)
    return packed.astype(BF16)


def project_kernel(ctx_ref, rows_ref, parts_ref, *refs, mp):
    *weight_refs, out_ref = refs
    columns = weight_refs[0].shape[0]
    blocks = len(weight_refs)
    _, pair, draft, lanes = out_ref.shape
    req, _, width = rows_ref.shape
    rows = rows_ref[...].reshape(req * draft, width)
    products = []
    for place, weight_ref in enumerate(weight_refs):
        beside, back = divmod(place, blocks // pair)
        block = lax.rem(ctx_ref[0] + blocks - pair * back, blocks) ^ beside
        product = lax.dot_general(
            rows, weight_ref[...], (((1,), (1,)), ((), ())), preferred_element_type=F32
        )
        looked_up = parts_ref[block, parts_ref.shape[1] - columns :].astype(F32)
        products.append((block, product + jnp.transpose(looked_up)))
    total = functools.reduce(jnp.add, [product for _, product in products])
    sums = packed_sums(jnp.sum(total, axis=1, keepdims=True), lanes - columns)
    for block, product in products:
        product = jnp.concatenate([product.astype(BF16), sums], axis=1)
        piece, half = lax.shift_right_logical(block, 1), block & 1
        for target in range(req):
            out_ref[target * mp + piece, half] = product[target * draft : (target + 1) * draft]


def project_rows(rows, weights, parts, ctx_index, mp):
    req, draft, _ = rows.shape
    columns = weights[0].shape[0]
    lanes = -(-(columns + 3) // LANES) * LANES
    vmem = pl.BlockSpec(memory_space=pltpu.VMEM)
    return pl.pallas_call(
        functools.partial(project_kernel, mp=mp),
        out_shape=jax.ShapeDtypeStruct((req * mp, len(weights) // mp, draft, lanes), BF16),
        in_specs=[pl.BlockSpec(memory_space=pltpu.SMEM)] + [vmem] * (2 + len(weights)),
        out_specs=vmem,
        compiler_params=pltpu.CompilerParams(vmem_limit_bytes=10 * MIB),
    )(ctx_index, rows, parts, *weights)


def residual_kernel(parts_ref, gain_ref, out_ref, centred_ref, *, mp, columns):
    sources, pair, _, _ = parts_ref.shape
    _, width = out_ref.shape
    blocks = []
    for half in range(pair):
        for source in range(sources // mp):
            block = parts_ref[source * mp, half].astype(F32)
            for piece in range(1, mp):
                block += parts_ref[source * mp + piece, half].astype(F32)
            blocks.append(block)
    residual = jnp.concatenate([block[:, :columns] for block in blocks], axis=1)
    out_ref[...] = residual
    sums = functools.reduce(jnp.add, blocks[: sources // mp])
    mean = sum(sums[:, columns + term : columns + term + 1] for term in range(3)) / (mp * width)
    centred = residual - mean
    squares = packed_sums(jnp.sum(centred * centred, axis=1, keepdims=True), LANES)
    scaled = (centred * gain_ref[...]).astype(BF16)
    for target in range(centred_ref.shape[0]):
        centred_ref[target, :, :width] = scaled
        centred_ref[target, :, width:] = squares


def residual_rows(parts, gain, mp, draft, columns, targets):
    vmem = pl.BlockSpec(memory_space=pltpu.VMEM)
    width = gain.shape[0]
    return pl.pallas_call(
        functools.partial(residual_kernel, mp=mp, columns=columns),
        out_shape=(
            jax.ShapeDtypeStruct((draft, width), F32),
            jax.ShapeDtypeStruct((targets, draft, width + LANES), BF16),
        ),
        in_specs=[vmem, vmem],
        out_specs=(vmem, vmem),
        compiler_params=pltpu.CompilerParams(vmem_limit_bytes=10 * MIB),
    )(parts, gain[None, :])


def lift_kernel(ctx_ref, rows_ref, weight_ref, out_ref):
    blocks, hidden, width = weight_ref.shape
    mp, height, _ = out_ref.shape
    pair = blocks // mp
    rows = rows_ref[:, :width]
    for place in range(blocks):
        other, step = divmod(place, blocks // 2)
        step = (0, blocks - 2, 2, 4)[step]
        block = lax.rem(ctx_ref[0] + step, blocks) ^ other
        piece, line = divmod(place, pair)
        out_ref[piece, line * hidden : (line + 1) * hidden] = lax.dot_general(
            weight_ref[block], rows, (((1,), (1,)), ((), ())), preferred_element_type=F32
        ).astype(BF16)
    squares = jnp.transpose(rows_ref[:, width:].astype(F32)).astype(BF16)
    for piece in range(mp):
        out_ref[piece, pair * hidden :] = squares[: height - pair * hidden]


def lift_rows(rows, weight, ctx_index, mp):
    blocks, hidden, _ = weight.shape
    vmem = pl.BlockSpec(memory_space=pltpu.VMEM)
    return pl.pallas_call(
        lift_kernel,
        out_shape=jax.ShapeDtypeStruct((mp, blocks // mp * hidden + 16, rows.shape[0]), BF16),
        in_specs=[pl.BlockSpec(memory_space=pltpu.SMEM), vmem, vmem],
        out_specs=vmem,
        compiler_params=pltpu.CompilerParams(vmem_limit_bytes=20 * MIB),
    )(ctx_index, rows, weight)


def gelu_kernel(parts_ref, out_ref, *, model_width):
    hidden = out_ref.shape[1]
    total = parts_ref[0].astype(F32)
    for piece in range(1, parts_ref.shape[0]):
        total += parts_ref[piece].astype(F32)
    squares = sum(total[hidden + term : hidden + term + 1] for term in range(3))
    lifted = total[:hidden] * lax.rsqrt(squares / model_width + 1e-05)
    activated = (0.5 * lifted * (1.0 + lax.erf(lifted * math.sqrt(0.5)))).astype(BF16)
    for target in range(out_ref.shape[0]):
        out_ref[target] = activated


def activate(parts, hidden, model_width):
    vmem = pl.BlockSpec(memory_space=pltpu.VMEM)
    return pl.pallas_call(
        functools.partial(gelu_kernel, model_width=model_width),
        out_shape=jax.ShapeDtypeStruct((parts.shape[0], hidden, parts.shape[2]), BF16),
        in_specs=[vmem],
        out_specs=vmem,
        compiler_params=pltpu.CompilerParams(vmem_limit_bytes=10 * MIB),
    )(parts)


def lower_kernel(hidden_ref, *refs):
    *weight_refs, out_ref = refs
    held = hidden_ref.shape[1]
    total = None
    first = 0
    for ref in weight_refs:
        piece, place = divmod(first, held)
        product = lax.dot_general(
            hidden_ref[piece, place : place + ref.shape[0]],
            ref[...],
            (((0,), (0,)), ((), ())),
            preferred_element_type=F32,
        )
        total = product if total is None else total + product
        first += ref.shape[0]
    out_ref[...] = total.astype(BF16).reshape(out_ref.shape)


def lower_rows(hidden, weights, targets):
    vmem = pl.BlockSpec(memory_space=pltpu.VMEM)
    return pl.pallas_call(
        lower_kernel,
        out_shape=jax.ShapeDtypeStruct(
            (targets, hidden.shape[2] // targets, weights[0].shape[1]), BF16
        ),
        in_specs=[vmem] * (1 + len(weights)),
        out_specs=vmem,
        compiler_params=pltpu.CompilerParams(vmem_limit_bytes=20 * MIB),
    )(hidden, *weights)


def finish_kernel(parts_ref, residual_ref, out_ref):
    total = parts_ref[0].astype(F32)
    for piece in range(1, parts_ref.shape[0]):
        total += parts_ref[piece].astype(F32)
    out_ref[...] = residual_ref[...] + total


def finish(parts, residual):
    vmem = pl.BlockSpec(memory_space=pltpu.VMEM)
    return pl.pallas_call(
        finish_kernel,
        out_shape=jax.ShapeDtypeStruct(residual.shape, F32),
        in_specs=[vmem, vmem],
        out_specs=vmem,
        compiler_params=pltpu.CompilerParams(vmem_limit_bytes=10 * MIB),
    )(parts, residual)


def after(value, earlier):
    return lax.optimization_barrier((value, earlier))[0]


def shifted_by(block, step):
    count = lax.axis_size("ctx")
    return lax.ppermute(block, "ctx", [(i, (i + step) % count) for i in range(count)])


def beside(blocks):
    count = lax.axis_size("ctx")
    return [lax.ppermute(block, "ctx", [(i, i ^ 1) for i in range(count)]) for block in blocks]


def nearest(block):
    return [block, shifted_by(block, 2), shifted_by(block, -2)]


def farthest(blocks):
    _, back, on = blocks
    half = back.shape[0] // 2
    return [shifted_by(back[:half], 2), shifted_by(on[half:], -2)]


def exchange(value, axis):
    return lax.all_to_all(value, axis, split_axis=0, concat_axis=0, tiled=True)


def per_device(
    token_ids,
    embed_table,
    queries,
    draft_kv,
    prefix_kv,
    suffix_kv,
    suffix_len,
    slopes,
    out_weight,
    ln_gain,
    up_weight,
    down_weight,
):
    heads = slopes.shape[0]
    _, draft, width = queries.shape
    prompt_local = prefix_kv.shape[1]
    ctx_count = lax.axis_size("ctx")
    req_count = lax.axis_size("req")
    mp_count = lax.axis_size("mp")
    ctx_index = lax.axis_index("ctx")
    model_index = lax.axis_index("mp")
    quarter = ln_gain.shape[0]

    copies = jnp.broadcast_to(queries, (ctx_count, draft, width))
    gathered = exchange(copies, "ctx")
    vocab_local = embed_table.shape[0]
    shifted = token_ids.reshape(1, -1) - model_index * vocab_local
    looked_up = look_up(shifted, embed_table.T)
    gathered, looked_up = lax.optimization_barrier((gathered, looked_up))
    out_blocks = [after(out_weight.T, looked_up)]
    out_blocks += [shifted_by(out_blocks[0], step) for step in range(2, ctx_count, 2)]
    offset = (prompt_local * (ctx_count - ctx_index)).astype(jnp.int32).reshape(1)
    parts = prompt_part(
        gathered.reshape(ctx_count * draft, width),
        prefix_kv,
        slopes,
        offset,
        looked_up,
        ctx_count,
    )
    parts, *out_blocks = lax.optimization_barrier((parts, *out_blocks))
    own, own_level = own_part(
        after(queries[0], parts), suffix_kv[:, 0], draft_kv[:, 0], slopes, suffix_len
    )
    parts = exchange(parts, "ctx")
    out_blocks += beside(out_blocks)
    merged = merge_parts(parts, own, own_level, heads, req_count)
    up_all = lax.all_gather(after(up_weight, merged).T, "ctx")
    attended = exchange(merged, "req")

    ctx_number = ctx_index.astype(jnp.int32).reshape(1)
    pieces = project_rows(attended, out_blocks, parts, ctx_number, mp_count)
    down_blocks = nearest(after(down_weight, pieces))
    pieces = exchange(pieces, ("req", "mp"))
    residual, centred = residual_rows(
        pieces, ln_gain, mp_count, draft, out_weight.shape[1], req_count
    )
    centred, *down_blocks = lax.optimization_barrier((centred, *down_blocks))
    centred = exchange(centred, "req").reshape(req_count * draft, -1)
    down_blocks += farthest(down_blocks)

    lifted = lift_rows(centred, up_all, ctx_number, mp_count)
    lifted, *down_blocks = lax.optimization_barrier((lifted, *down_blocks))
    lifted = exchange(lifted, "mp")
    down_blocks += beside(down_blocks)
    hidden = up_weight.shape[1] * ctx_count // mp_count
    activated = exchange(activate(lifted, hidden, quarter * mp_count), "mp")
    lowered = exchange(lower_rows(activated, down_blocks, req_count), "req")
    layer_out = finish(lowered, residual)
    return residual[None], layer_out[None]


def solution(mesh):
    rows = ("ctx", "req")
    in_specs = (
        P(),
        P("mp", rows),
        P(rows, None, "mp"),
        P(None, rows, None, "mp"),
        P(None, "ctx", "mp"),
        P(None, rows, None, "mp"),
        P(rows),
        P("mp"),
        P("mp", rows),
        P("mp"),
        P("mp", rows),
        P(rows, "mp"),
    )
    out_specs = (P(rows, None, "mp"), P(rows, None, "mp"))
    return jax.shard_map(
        per_device, mesh=mesh, in_specs=in_specs, out_specs=out_specs, check_vma=False
    )
```

```python
import functools
import math

import jax
import jax.numpy as jnp
from jax import lax
from jax.experimental import pallas as pl
from jax.experimental.pallas import tpu as pltpu
from jax.sharding import PartitionSpec as P

LANES = 128
F32 = jnp.float32
BF16 = jnp.bfloat16
MIB = 1024 * 1024


def head_lanes(head, tile, head_size):
    first = max(head * head_size - tile * LANES, 0)
    last = min((head + 1) * head_size - tile * LANES, LANES)
    return first, last


def head_tiles(head, head_size):
    return range(head * head_size // LANES, ((head + 1) * head_size - 1) // LANES + 1)


def lane_mask(shape, first, last):
    lane = lax.broadcasted_iota(jnp.int32, shape, len(shape) - 1)
    return (lane >= first) & (lane < last)


def split_three(value):
    high = value.astype(BF16).astype(F32)
    rest = value - high
    middle = rest.astype(BF16).astype(F32)
    low = rest - middle
    return high, middle, low


def prompt_kernel(
    offset_ref, slopes_ref, query_ref, looked_ref, prefix_ref, out_ref, *, heads, head_size
):
    rows, width = query_ref.shape
    keys = prefix_ref.shape[1]
    tiles = width // LANES
    scale = 1.0 / math.sqrt(head_size)
    position = (
        lax.broadcasted_iota(jnp.int32, (1, keys), 1) - offset_ref[0]
    ).astype(F32)
    parts = [jnp.zeros((rows, LANES), F32) for _ in range(tiles)]
    stats = jnp.zeros((rows, LANES), F32)
    stat_lane = lax.broadcasted_iota(jnp.int32, (rows, LANES), 1)
    for head in range(heads):
        span = head_tiles(head, head_size)
        window = slice(span[0] * LANES, (span[-1] + 1) * LANES)
        query_window = jnp.concatenate(
            [
                jnp.where(
                    lane_mask((rows, LANES), *head_lanes(head, tile, head_size)),
                    query_ref[:, tile * LANES : (tile + 1) * LANES],
                    jnp.zeros((rows, LANES), BF16),
                )
                for tile in span
            ],
            axis=1,
        )
        scores = lax.dot_general(
            query_window,
            prefix_ref[0, :, window],
            (((1,), (1,)), ((), ())),
            preferred_element_type=F32,
        )
        scores = scores * scale + slopes_ref[:, head : head + 1] * position
        top = jnp.max(scores, axis=1, keepdims=True)
        weights = jnp.exp(scores - top)
        total = jnp.sum(weights, axis=1, keepdims=True)
        sums = jnp.dot(
            weights.astype(BF16), prefix_ref[1, :, window], preferred_element_type=F32
        )
        sums = sums * (1.0 / total)
        for place, tile in enumerate(span):
            parts[tile] = jnp.where(
                lane_mask((rows, LANES), *head_lanes(head, tile, head_size)),
                sums[:, place * LANES : (place + 1) * LANES],
                parts[tile],
            )
        stats = jnp.where(stat_lane % heads == head, top + jnp.log(total), stats)
    high, middle, low = split_three(stats)
    group = stat_lane // heads
    packed = jnp.where(
        group == 0, high, jnp.where(group == 1, middle, jnp.where(group == 2, low, 0.0))
    )
    targets = out_ref.shape[0]
    draft = rows // targets
    for tile, value in enumerate([*parts, packed]):
        value = value.astype(BF16)
        for target in range(targets):
            out_ref[target, tile * draft : (tile + 1) * draft] = value[
                target * draft : (target + 1) * draft
            ]
    for target in range(targets):
        out_ref[target, (tiles + 1) * draft :] = looked_ref[
            :, target * LANES : (target + 1) * LANES
        ]


def prompt_part(query_rows, prefix_kv, slopes, offset, looked_up, targets):
    rows, width = query_rows.shape
    heads = slopes.shape[0]
    tiles = width // LANES
    return pl.pallas_call(
        functools.partial(prompt_kernel, heads=heads, head_size=width // heads),
        out_shape=jax.ShapeDtypeStruct(
            (targets, (tiles + 1) * (rows // targets) + looked_up.shape[0], LANES), BF16
        ),
        in_specs=[
            pl.BlockSpec(memory_space=pltpu.SMEM),
            pl.BlockSpec(memory_space=pltpu.VMEM),
            pl.BlockSpec(memory_space=pltpu.VMEM),
            pl.BlockSpec(memory_space=pltpu.VMEM),
            pl.BlockSpec(memory_space=pltpu.VMEM),
        ],
        out_specs=pl.BlockSpec(memory_space=pltpu.VMEM),
        compiler_params=pltpu.CompilerParams(vmem_limit_bytes=20 * MIB),
    )(offset, slopes[None, :], query_rows, looked_up, prefix_kv)


def lookup_kernel(ids_ref, table_ref, out_ref):
    count = ids_ref.shape[1]
    features, vocab = table_ref.shape
    step = math.gcd(vocab, 2 * LANES)
    ids = ids_ref[...]
    place = lax.broadcasted_iota(jnp.int32, (step, count), 0)
    total = jnp.zeros((features, count), F32)
    for first in range(0, vocab, step):
        chosen = jnp.where(place == ids - first, 1.0, 0.0).astype(BF16)
        total += jnp.dot(table_ref[:, first : first + step], chosen, preferred_element_type=F32)
    out_ref[...] = total.astype(BF16)


def look_up(ids, table):
    vmem = pl.BlockSpec(memory_space=pltpu.VMEM)
    return pl.pallas_call(
        lookup_kernel,
        out_shape=jax.ShapeDtypeStruct((table.shape[0], ids.shape[1]), BF16),
        in_specs=[vmem, vmem],
        out_specs=vmem,
        compiler_params=pltpu.CompilerParams(vmem_limit_bytes=12 * MIB),
    )(ids, table)


def own_kernel(
    length_ref, slopes_ref, query_ref, suffix_ref, draft_ref, out_ref, stats_ref, *, heads, head_size
):
    draft, width = query_ref.shape
    slots = suffix_ref.shape[1]
    rows = heads * draft
    query = query_ref[...]
    masks = [
        lane_mask((draft, width), head * head_size, (head + 1) * head_size)
        for head in range(heads)
    ]
    spread = jnp.concatenate(
        [jnp.where(mask, query, jnp.zeros_like(query)) for mask in masks], axis=0
    )
    row = lax.broadcasted_iota(jnp.int32, (rows, 1), 0)
    slope = jnp.zeros((rows, 1), F32)
    for head in range(heads):
        slope = jnp.where(row // draft == head, slopes_ref[:, head : head + 1], slope)
    scale = 1.0 / math.sqrt(head_size)
    length = length_ref[0]
    contract = (((1,), (1,)), ((), ()))
    slot = lax.broadcasted_iota(jnp.int32, (rows, slots), 1)
    suffix_scores = lax.dot_general(spread, suffix_ref[0], contract, preferred_element_type=F32)
    suffix_scores = suffix_scores * scale + slope * slot.astype(F32)
    suffix_scores = jnp.where(slot < length, suffix_scores, -jnp.inf)
    place = lax.broadcasted_iota(jnp.int32, (rows, draft), 1)
    draft_scores = lax.dot_general(spread, draft_ref[0], contract, preferred_element_type=F32)
    draft_scores = draft_scores * scale + slope * (place + length).astype(F32)
    token = lax.broadcasted_iota(jnp.int32, (rows, draft), 0) % draft
    draft_scores = jnp.where(place <= token, draft_scores, -jnp.inf)
    top = jnp.maximum(
        jnp.max(suffix_scores, axis=1, keepdims=True), jnp.max(draft_scores, axis=1, keepdims=True)
    )
    suffix_weights = jnp.exp(suffix_scores - top)
    draft_weights = jnp.exp(draft_scores - top)
    total = jnp.sum(suffix_weights, axis=1, keepdims=True) + jnp.sum(
        draft_weights, axis=1, keepdims=True
    )
    sums = jnp.dot(suffix_weights.astype(BF16), suffix_ref[1], preferred_element_type=F32)
    sums += jnp.dot(draft_weights.astype(BF16), draft_ref[1], preferred_element_type=F32)
    sums = sums * (1.0 / total)
    level = top + jnp.log(total)
    result = jnp.zeros((draft, width), F32)
    stats = jnp.zeros((draft, LANES), F32)
    lane = lax.broadcasted_iota(jnp.int32, (draft, LANES), 1)
    for head in range(heads):
        rows_of = slice(head * draft, (head + 1) * draft)
        result = jnp.where(masks[head], sums[rows_of], result)
        stats = jnp.where(lane == head, level[rows_of], stats)
    out_ref[...] = result
    stats_ref[...] = stats


def own_part(query_rows, suffix_kv, draft_kv, slopes, length):
    draft, width = query_rows.shape
    heads = slopes.shape[0]
    vmem = pl.BlockSpec(memory_space=pltpu.VMEM)
    smem = pl.BlockSpec(memory_space=pltpu.SMEM)
    return pl.pallas_call(
        functools.partial(own_kernel, heads=heads, head_size=width // heads),
        out_shape=(
            jax.ShapeDtypeStruct((draft, width), F32),
            jax.ShapeDtypeStruct((draft, LANES), F32),
        ),
        in_specs=[smem, vmem, vmem, vmem, vmem],
        out_specs=(vmem, vmem),
        compiler_params=pltpu.CompilerParams(vmem_limit_bytes=12 * MIB),
    )(length, slopes[None, :], query_rows, suffix_kv, draft_kv)


def merge_kernel(parts_ref, own_ref, level_ref, out_ref, *, heads, head_size):
    count = parts_ref.shape[0]
    draft, width = own_ref.shape
    tiles = width // LANES
    levels = [level_ref[...]]
    for part in range(count):
        packed = parts_ref[part, tiles * draft : (tiles + 1) * draft].astype(F32)
        levels.append(
            packed
            + pltpu.roll(packed, LANES - heads, 1)
            + pltpu.roll(packed, LANES - 2 * heads, 1)
        )
    top = functools.reduce(jnp.maximum, levels)
    shares = [jnp.exp(level - top) for level in levels]
    total = functools.reduce(jnp.add, shares)
    shares = [share / total for share in shares]
    for tile in range(tiles):
        lanes = slice(tile * LANES, (tile + 1) * LANES)
        joined = jnp.zeros((draft, LANES), F32)
        for part, share in enumerate(shares):
            factor = jnp.zeros((draft, LANES), F32)
            for head in range(heads):
                first, last = head_lanes(head, tile, head_size)
                if first < last:
                    factor = jnp.where(
                        lane_mask((draft, LANES), first, last), share[:, head : head + 1], factor
                    )
            if part == 0:
                value = own_ref[:, lanes]
            else:
                value = parts_ref[part - 1, tile * draft : (tile + 1) * draft].astype(F32)
            joined += factor * value
        joined = joined.astype(BF16)
        for target in range(out_ref.shape[0]):
            out_ref[target, :, lanes] = joined


def merge_parts(parts, own, level, heads, targets):
    draft, width = own.shape
    vmem = pl.BlockSpec(memory_space=pltpu.VMEM)
    return pl.pallas_call(
        functools.partial(merge_kernel, heads=heads, head_size=width // heads),
        out_shape=jax.ShapeDtypeStruct((targets, draft, width), BF16),
        in_specs=[vmem, vmem, vmem],
        out_specs=vmem,
        compiler_params=pltpu.CompilerParams(vmem_limit_bytes=10 * MIB),
    )(parts, own, level)


def packed_sums(value, lanes):
    lane = lax.broadcasted_iota(jnp.int32, (value.shape[0], lanes), 1)
    packed = jnp.zeros((value.shape[0], lanes), F32)
    for place, term in enumerate(split_three(value)):
        packed = jnp.where(lane == place, term, packed)
    return packed.astype(BF16)


def project_kernel(ctx_ref, rows_ref, parts_ref, *refs, mp):
    *weight_refs, out_ref = refs
    columns = weight_refs[0].shape[0]
    blocks = len(weight_refs)
    _, pair, draft, lanes = out_ref.shape
    req, _, width = rows_ref.shape
    rows = rows_ref[...].reshape(req * draft, width)
    products = []
    for place, weight_ref in enumerate(weight_refs):
        beside, back = divmod(place, blocks // pair)
        block = lax.rem(ctx_ref[0] + blocks - pair * back, blocks) ^ beside
        product = lax.dot_general(
            rows, weight_ref[...], (((1,), (1,)), ((), ())), preferred_element_type=F32
        )
        looked_up = parts_ref[block, parts_ref.shape[1] - columns :].astype(F32)
        products.append((block, product + jnp.transpose(looked_up)))
    total = functools.reduce(jnp.add, [product for _, product in products])
    sums = packed_sums(jnp.sum(total, axis=1, keepdims=True), lanes - columns)
    for block, product in products:
        product = jnp.concatenate([product.astype(BF16), sums], axis=1)
        piece, half = lax.shift_right_logical(block, 1), block & 1
        for target in range(req):
            out_ref[target * mp + piece, half] = product[target * draft : (target + 1) * draft]


def project_rows(rows, weights, parts, ctx_index, mp):
    req, draft, _ = rows.shape
    columns = weights[0].shape[0]
    lanes = -(-(columns + 3) // LANES) * LANES
    vmem = pl.BlockSpec(memory_space=pltpu.VMEM)
    return pl.pallas_call(
        functools.partial(project_kernel, mp=mp),
        out_shape=jax.ShapeDtypeStruct((req * mp, len(weights) // mp, draft, lanes), BF16),
        in_specs=[pl.BlockSpec(memory_space=pltpu.SMEM)] + [vmem] * (2 + len(weights)),
        out_specs=vmem,
        compiler_params=pltpu.CompilerParams(vmem_limit_bytes=10 * MIB),
    )(ctx_index, rows, parts, *weights)


def residual_kernel(parts_ref, gain_ref, out_ref, centred_ref, *, mp, columns):
    sources, pair, _, _ = parts_ref.shape
    _, width = out_ref.shape
    blocks = []
    for half in range(pair):
        for source in range(sources // mp):
            block = parts_ref[source * mp, half].astype(F32)
            for piece in range(1, mp):
                block += parts_ref[source * mp + piece, half].astype(F32)
            blocks.append(block)
    residual = jnp.concatenate([block[:, :columns] for block in blocks], axis=1)
    out_ref[...] = residual
    sums = functools.reduce(jnp.add, blocks[: sources // mp])
    mean = sum(sums[:, columns + term : columns + term + 1] for term in range(3)) / (mp * width)
    centred = residual - mean
    squares = packed_sums(jnp.sum(centred * centred, axis=1, keepdims=True), LANES)
    scaled = (centred * gain_ref[...]).astype(BF16)
    for target in range(centred_ref.shape[0]):
        centred_ref[target, :, :width] = scaled
        centred_ref[target, :, width:] = squares


def residual_rows(parts, gain, mp, draft, columns, targets):
    vmem = pl.BlockSpec(memory_space=pltpu.VMEM)
    width = gain.shape[0]
    return pl.pallas_call(
        functools.partial(residual_kernel, mp=mp, columns=columns),
        out_shape=(
            jax.ShapeDtypeStruct((draft, width), F32),
            jax.ShapeDtypeStruct((targets, draft, width + LANES), BF16),
        ),
        in_specs=[vmem, vmem],
        out_specs=(vmem, vmem),
        compiler_params=pltpu.CompilerParams(vmem_limit_bytes=10 * MIB),
    )(parts, gain[None, :])


def lift_kernel(rows_ref, weight_ref, out_ref, *, hidden):
    blocks, _, width = weight_ref.shape
    mp, height, _ = out_ref.shape
    pair = blocks // mp
    rows = rows_ref[:, :width]
    for block in range(blocks):
        piece, place = divmod(block, pair)
        out_ref[piece, place * hidden : (place + 1) * hidden] = lax.dot_general(
            weight_ref[block, weight_ref.shape[1] - hidden :],
            rows,
            (((1,), (1,)), ((), ())),
            preferred_element_type=F32,
        ).astype(BF16)
    squares = jnp.transpose(rows_ref[:, width:].astype(F32)).astype(BF16)
    for piece in range(mp):
        out_ref[piece, pair * hidden :] = squares[: height - pair * hidden]


def lift_rows(rows, weight, hidden, mp):
    blocks = weight.shape[0]
    vmem = pl.BlockSpec(memory_space=pltpu.VMEM)
    return pl.pallas_call(
        functools.partial(lift_kernel, hidden=hidden),
        out_shape=jax.ShapeDtypeStruct((mp, blocks // mp * hidden + 16, rows.shape[0]), BF16),
        in_specs=[vmem, vmem],
        out_specs=vmem,
        compiler_params=pltpu.CompilerParams(vmem_limit_bytes=20 * MIB),
    )(rows, weight)


def gelu_kernel(parts_ref, out_ref, *, model_width):
    hidden = out_ref.shape[1]
    total = parts_ref[0].astype(F32)
    for piece in range(1, parts_ref.shape[0]):
        total += parts_ref[piece].astype(F32)
    squares = sum(total[hidden + term : hidden + term + 1] for term in range(3))
    lifted = total[:hidden] * lax.rsqrt(squares / model_width + 1e-05)
    activated = (0.5 * lifted * (1.0 + lax.erf(lifted * math.sqrt(0.5)))).astype(BF16)
    for target in range(out_ref.shape[0]):
        out_ref[target] = activated


def activate(parts, hidden, model_width):
    vmem = pl.BlockSpec(memory_space=pltpu.VMEM)
    return pl.pallas_call(
        functools.partial(gelu_kernel, model_width=model_width),
        out_shape=jax.ShapeDtypeStruct((parts.shape[0], hidden, parts.shape[2]), BF16),
        in_specs=[vmem],
        out_specs=vmem,
        compiler_params=pltpu.CompilerParams(vmem_limit_bytes=10 * MIB),
    )(parts)


def lower_kernel(hidden_ref, weight_ref, out_ref):
    blocks, features, _ = weight_ref.shape
    pair = blocks // hidden_ref.shape[0]
    total = None
    for block in range(blocks):
        piece, place = divmod(block, pair)
        product = lax.dot_general(
            hidden_ref[piece, place * features : (place + 1) * features],
            weight_ref[block],
            (((0,), (0,)), ((), ())),
            preferred_element_type=F32,
        )
        total = product if total is None else total + product
    out_ref[...] = total.astype(BF16).reshape(out_ref.shape)


def lower_rows(hidden, weight, targets):
    vmem = pl.BlockSpec(memory_space=pltpu.VMEM)
    return pl.pallas_call(
        lower_kernel,
        out_shape=jax.ShapeDtypeStruct((targets, hidden.shape[2] // targets, weight.shape[2]), BF16),
        in_specs=[vmem, vmem],
        out_specs=vmem,
        compiler_params=pltpu.CompilerParams(vmem_limit_bytes=20 * MIB),
    )(hidden, weight)


def finish_kernel(parts_ref, residual_ref, out_ref):
    total = parts_ref[0].astype(F32)
    for piece in range(1, parts_ref.shape[0]):
        total += parts_ref[piece].astype(F32)
    out_ref[...] = residual_ref[...] + total


def finish(parts, residual):
    vmem = pl.BlockSpec(memory_space=pltpu.VMEM)
    return pl.pallas_call(
        finish_kernel,
        out_shape=jax.ShapeDtypeStruct(residual.shape, F32),
        in_specs=[vmem, vmem],
        out_specs=vmem,
        compiler_params=pltpu.CompilerParams(vmem_limit_bytes=10 * MIB),
    )(parts, residual)


def after(value, earlier):
    return lax.optimization_barrier((value, earlier))[0]


def exchange(value, axis):
    return lax.all_to_all(value, axis, split_axis=0, concat_axis=0, tiled=True)


def per_device(
    token_ids,
    embed_table,
    queries,
    draft_kv,
    prefix_kv,
    suffix_kv,
    suffix_len,
    slopes,
    out_weight,
    ln_gain,
    up_weight,
    down_weight,
):
    heads = slopes.shape[0]
    _, draft, width = queries.shape
    prompt_local = prefix_kv.shape[1]
    ctx_count = lax.axis_size("ctx")
    req_count = lax.axis_size("req")
    mp_count = lax.axis_size("mp")
    ctx_index = lax.axis_index("ctx")
    model_index = lax.axis_index("mp")
    quarter = ln_gain.shape[0]

    copies = jnp.broadcast_to(queries, (ctx_count, draft, width))
    gathered = exchange(copies, "ctx")
    vocab_local = embed_table.shape[0]
    shifted = token_ids.reshape(1, -1) - model_index * vocab_local
    looked_up = look_up(shifted, embed_table.T)
    gathered, looked_up = lax.optimization_barrier((gathered, looked_up))
    out_blocks = [after(out_weight.T, looked_up)]
    out_blocks += [
        lax.ppermute(out_blocks[0], "ctx", [(i, (i + step) % ctx_count) for i in range(ctx_count)])
        for step in range(2, ctx_count, 2)
    ]

    offset = (prompt_local * (ctx_count - ctx_index)).astype(jnp.int32).reshape(1)
    parts = prompt_part(
        gathered.reshape(ctx_count * draft, width),
        prefix_kv,
        slopes,
        offset,
        looked_up,
        ctx_count,
    )
    parts, *out_blocks = lax.optimization_barrier((parts, *out_blocks))
    up_all = lax.all_gather(after(up_weight, parts).T, "ctx")
    down_all = lax.all_gather(after(down_weight, parts), "ctx")
    own, own_level = own_part(
        after(queries[0], parts), suffix_kv[:, 0], draft_kv[:, 0], slopes, suffix_len
    )
    parts = exchange(parts, "ctx")
    out_blocks += [
        lax.ppermute(block, "ctx", [(i, i ^ 1) for i in range(ctx_count)])
        for block in out_blocks
    ]
    attended = exchange(merge_parts(parts, own, own_level, heads, req_count), "req")

    pieces = exchange(
        project_rows(
            attended, out_blocks, parts, ctx_index.astype(jnp.int32).reshape(1), mp_count
        ),
        ("req", "mp"),
    )
    residual, centred = residual_rows(
        pieces, ln_gain, mp_count, draft, out_weight.shape[1], req_count
    )
    centred = exchange(centred, "req").reshape(req_count * draft, -1)

    hidden = up_weight.shape[1]
    lifted = exchange(lift_rows(centred, up_all, hidden, mp_count), "mp")
    activated = activate(lifted, ctx_count // mp_count * hidden, quarter * mp_count)
    activated = exchange(activated, "mp")
    lowered = exchange(lower_rows(activated, down_all, req_count), "req")
    layer_out = finish(lowered, residual)
    return residual[None], layer_out[None]


def solution(mesh):
    rows = ("ctx", "req")
    in_specs = (
        P(),
        P("mp", rows),
        P(rows, None, "mp"),
        P(None, rows, None, "mp"),
        P(None, "ctx", "mp"),
        P(None, rows, None, "mp"),
        P(rows),
        P("mp"),
        P("mp", rows),
        P("mp"),
        P("mp", rows),
        P(rows, "mp"),
    )
    out_specs = (P(rows, None, "mp"), P(rows, None, "mp"))
    return jax.shard_map(
        per_device, mesh=mesh, in_specs=in_specs, out_specs=out_specs, check_vma=False
    )
```
